32 devices in a mesh: dp: 16 (over z, y, core), tensor: 2 (over x).
Axes of the slice: x: 2, y: 2, z: 4, core: 2. Of those that a mesh axis runs over, the one named last changes fastest.
Arguments:
- tokens: bfloat16 [8192, 2048], P(('dp', 'tensor')), may hold values from -6 to 6
- lengths: int32 [16], P('dp'), may hold values from 1 to 512, 6144 in all
- cotangent: bfloat16 [8192, 2048], P(('dp', 'tensor')), may hold values from -6 to 6
- gain_in: float32 [2048], P(('dp', 'tensor')), may hold values from 0.5 to 1.5
- gain_ffn: float32 [2048], P(('dp', 'tensor')), may hold values from 0.5 to 1.5
- gain_out: float32 [512], P(('dp', 'tensor')), may hold values from 0.5 to 1.5
- w_query: float32 [2048, 1536], P('dp', 'tensor'), may hold values from -0.125 to 0.125
- w_key: float32 [2048, 1536], P('dp', 'tensor'), may hold values from -0.125 to 0.125
- w_value: float32 [2048, 3072], P('dp', 'tensor'), may hold values from -0.125 to 0.125
- w_gate: float32 [2048, 3072], P('dp', 'tensor'), may hold values from -0.125 to 0.125
- w_beta: float32 [2048, 6], P('dp', 'tensor'), may hold values from -0.125 to 0.125
- w_decay: float32 [2048, 6], P('dp', 'tensor'), may hold values from -0.125 to 0.125
- conv_query: float32 [4, 6, 256], P(None, 'tensor', 'dp'), may hold values from -3 to 3
- conv_key: float32 [4, 6, 256], P(None, 'tensor', 'dp'), may hold values from -3 to 3
- conv_value: float32 [4, 6, 512], P(None, 'tensor', 'dp'), may hold values from -3 to 3
- decay_log: float32 [6], replicated, may hold values from 0 to 2.7726
- decay_bias: float32 [6], replicated, may hold values from -6.91 to -2.25
- w_output: float32 [3072, 2048], P('tensor', 'dp'), may hold values from -0.109375 to 0.109375
- w_ffn_gate: float32 [2048, 5632], P('dp', 'tensor'), may hold values from -0.125 to 0.125
- w_ffn_up: float32 [2048, 5632], P('dp', 'tensor'), may hold values from -0.125 to 0.125
- w_ffn_down: float32 [5632, 2048], P('tensor', 'dp'), may hold values from -0.078125 to 0.078125
Outputs:
- out_tokens: bfloat16 [8192, 2048], P(('dp', 'tensor'))
- grad_tokens: float32 [8192, 2048], P(('dp', 'tensor'))
- grad_gain_in: float32 [2048], P(('dp', 'tensor'))
- grad_gain_ffn: float32 [2048], P(('dp', 'tensor'))
- grad_gain_out: float32 [512], P(('dp', 'tensor'))
- grad_w_query: float32 [2048, 1536], P('dp', 'tensor')
- grad_w_key: float32 [2048, 1536], P('dp', 'tensor')
- grad_w_value: float32 [2048, 3072], P('dp', 'tensor')
- grad_w_gate: float32 [2048, 3072], P('dp', 'tensor')
- grad_w_beta: float32 [2048, 6], P('dp', 'tensor')
- grad_w_decay: float32 [2048, 6], P('dp', 'tensor')
- grad_conv_query: float32 [4, 6, 256], P(None, 'tensor', 'dp')
- grad_conv_key: float32 [4, 6, 256], P(None, 'tensor', 'dp')
- grad_conv_value: float32 [4, 6, 512], P(None, 'tensor', 'dp')
- grad_decay_log: float32 [6], replicated
- grad_decay_bias: float32 [6], replicated
- grad_w_output: float32 [3072, 2048], P('tensor', 'dp')
- grad_w_ffn_gate: float32 [2048, 5632], P('dp', 'tensor')
- grad_w_ffn_up: float32 [2048, 5632], P('dp', 'tensor')
- grad_w_ffn_down: float32 [5632, 2048], P('tensor', 'dp')
The draws below stay inside these ranges and needn't reach their ends.
Inputs may be any that keep to these rules, and one draw needn't show every extreme that they name: The lengths of all slots sum to three quarters of 8192; the longest fills its slot of 512.
All inputs are finite; a program needn't handle non-finite values. No bound on the sum of `lengths` on one device may be relied on, other than what follows from the above.
Results may differ from the reference program's by a relative error of at most 0.023.
Values may be sent and summed in bfloat16 or wider, within the bound.
A program may use at most 320 MiB of HBM per device.

```python
import math
import jax
import jax.numpy as jnp
import numpy as np
from jax import lax

D = 2048
HK = 6
DK = 256
DV = 512
FF = 5632
CONV = 4
SPAN = 64
SLOT = 512
TOKENS = 8192
N_DP = 16


def draw_decay_log(key, part):
    key = jax.random.fold_in(key, 11)
    rates = jax.random.uniform(key, (HK,), jnp.float32, 1.0, 16.0)
    return jnp.log(rates)


def draw_decay_bias(key, part):
    key = jax.random.fold_in(key, 23)
    exponent = jax.random.uniform(key, (HK,), jnp.float32, jnp.log(0.001), jnp.log(0.1))
    step_size = jnp.exp(exponent)
    return step_size + jnp.log(-jnp.expm1(-step_size))


def levels(rng, extent, split, least, high):
    gain = 1.0
    for dim, blocks in split:
        draws = jax.random.uniform(jax.random.fold_in(jax.random.fold_in(rng, 6), dim), (blocks,), jnp.float32, least / len(split), high / len(split))
        gain = gain * jnp.repeat(jnp.exp(draws), extent[dim] // blocks).reshape((-1,) + (1,) * (len(extent) - 1 - dim))
    return gain


def split_up(amount, total, most, skew):
    loads = [(1 << 20) // math.isqrt(rank ** skew) + 1 for rank in range(2, amount + 1)]
    spare, counts = total - most - (amount - 1), [1] * (amount - 1)
    while spare > 0:
        free = [i for i in range(amount - 1) if counts[i] < most]
        whole, left = sum([loads[i] for i in free]), spare
        for i in free:
            addition = min(most - counts[i], max(1, left * loads[i] // whole), spare)
            counts[i] = counts[i] + addition
            spare = spare - addition
    return np.array([most] + counts)


def ragged_sizes(rng, amount, total, most, slope):
    if amount == 2:
        one = jax.random.randint(rng, (), max(1, total - most), min(most, total - 1) + 1)
        return jnp.stack([one, total - one])
    tallies = jnp.asarray(split_up(amount, total, most, slope), jnp.int32)
    twos = (amount - 1) // 2
    donor, receiver = tallies[1:1 + 2 * twos:2], tallies[2:2 + 2 * twos:2]
    slack = jnp.minimum(donor - 1, most - receiver)
    moved = jax.random.randint(jax.random.fold_in(rng, 1), (twos,), 0, 1 << 20) % (slack + 1)
    tallies = tallies.at[1:1 + 2 * twos:2].set(donor - moved).at[2:2 + 2 * twos:2].set(receiver + moved)
    return tallies[jax.random.permutation(jax.random.fold_in(rng, 2), amount)]


def scatter_about(stream_key, extent, width, most, cuts=(), kind=jnp.bfloat16):
    values = jax.random.normal(stream_key, extent, jnp.float32) * width
    if len(cuts) > 0:
        values = levels(stream_key, extent, cuts, -0.22, 0.18) * values
    return jnp.clip(values, min=-most, max=most).astype(kind)


def setup_inputs(seed: int = 0) -> dict:
    key_of = jax.random.split(jax.random.key(seed), 22)
    tokens = scatter_about(key_of[0], (TOKENS, D), 1.0, 6.0, ((0, 32),))
    lengths = ragged_sizes(key_of[1], N_DP, 3 * TOKENS // 4, SLOT, 1).astype(jnp.int32)
    cotangent = scatter_about(key_of[2], (TOKENS, D), 1.0, 6.0, ((0, 32),))
    gain_in = jnp.clip(1.0 + 0.1 * jax.random.normal(key_of[3], (D,), jnp.float32), 0.5, 1.5)
    gain_ffn = jnp.clip(1.0 + 0.1 * jax.random.normal(key_of[4], (D,), jnp.float32), 0.5, 1.5)
    gain_out = jnp.clip(1.0 + 0.1 * jax.random.normal(key_of[5], (DV,), jnp.float32), 0.5, 1.5)
    w_query = scatter_about(key_of[6], (D, HK * DK), D ** -0.5, 0.125, ((0, 16), (1, 2)), jnp.float32)
    w_key = scatter_about(key_of[7], (D, HK * DK), D ** -0.5, 0.125, ((0, 16), (1, 2)), jnp.float32)
    w_value = scatter_about(key_of[8], (D, HK * DV), D ** -0.5, 0.125, ((0, 16), (1, 2)), jnp.float32)
    w_gate = scatter_about(key_of[9], (D, HK * DV), D ** -0.5, 0.125, ((0, 16), (1, 2)), jnp.float32)
    w_beta = scatter_about(key_of[10], (D, HK), D ** -0.5, 0.125, ((0, 16), (1, 2)), jnp.float32)
    w_decay = scatter_about(key_of[11], (D, HK), D ** -0.5, 0.125, ((0, 16), (1, 2)), jnp.float32)
    conv_query = scatter_about(key_of[12], (CONV, HK, DK), CONV ** -0.5, 3.0, ((1, 2), (2, 16)), jnp.float32)
    conv_key = scatter_about(key_of[13], (CONV, HK, DK), CONV ** -0.5, 3.0, ((1, 2), (2, 16)), jnp.float32)
    conv_value = scatter_about(key_of[14], (CONV, HK, DV), CONV ** -0.5, 3.0, ((1, 2), (2, 16)), jnp.float32)
    decay_log = draw_decay_log(jax.random.fold_in(key_of[21], 71), 0)
    decay_bias = draw_decay_bias(jax.random.fold_in(key_of[21], 71), 0)
    w_output = scatter_about(key_of[17], (HK * DV, D), (HK * DV) ** -0.5, 0.109375, ((0, 2), (1, 16)), jnp.float32)
    w_ffn_gate = scatter_about(key_of[18], (D, FF), D ** -0.5, 0.125, ((0, 16), (1, 2)), jnp.float32)
    w_ffn_up = scatter_about(key_of[19], (D, FF), D ** -0.5, 0.125, ((0, 16), (1, 2)), jnp.float32)
    w_ffn_down = scatter_about(key_of[20], (FF, D), FF ** -0.5, 0.078125, ((0, 2), (1, 16)), jnp.float32)
    return {"tokens": tokens, "lengths": lengths, "cotangent": cotangent, "gain_in": gain_in, "gain_ffn": gain_ffn, "gain_out": gain_out, "w_query": w_query, "w_key": w_key, "w_value": w_value, "w_gate": w_gate, "w_beta": w_beta, "w_decay": w_decay, "conv_query": conv_query, "conv_key": conv_key, "conv_value": conv_value, "decay_log": decay_log, "decay_bias": decay_bias, "w_output": w_output, "w_ffn_gate": w_ffn_gate, "w_ffn_up": w_ffn_up, "w_ffn_down": w_ffn_down}


highest = lax.Precision.HIGHEST

@jax.custom_vjp
def low(v):
    return lax.optimization_barrier(v.astype(jnp.bfloat16)).astype(jnp.float32)

@jax.custom_vjp
def low_back(v):
    return v

def low_keep(v):
    return (low(v), None)

def low_pass(kept, grad):
    return (grad,)

def back_keep(v):
    return (v, None)

def back_low(kept, grad):
    return (low(grad),)
low.defvjp(low_keep, low_pass)
low_back.defvjp(back_keep, back_low)

def project(inputs, weight):
    return jnp.einsum('bsd,dn->bsn', inputs, low(weight), precision=highest)

def rms_scale(values):
    return lax.rsqrt(lax.optimization_barrier(jnp.mean(values * values, axis=-1, keepdims=True)) + 1e-05)

def unit_norm(values):
    return values * lax.rsqrt(lax.optimization_barrier(jnp.sum(values * values, axis=-1, keepdims=True)) + 1e-06)

def causal_conv(values, weights):
    length = values.shape[-2]
    tap_count = weights.shape[0]
    summed = jnp.zeros_like(values)
    for tap_index in range(tap_count):
        offset = tap_count - 1 - tap_index
        padding = [(0, 0)] * (values.ndim - 2) + [(offset, 0), (0, 0)]
        summed = summed + weights[tap_index] * jnp.pad(values, padding)[..., :length, :]
    return summed

def delta_rule(query_vecs, key_vecs, value_vecs, beta_vals, log_decays):
    batch_size, length, head_count, key_size = query_vecs.shape
    value_size = value_vecs.shape[-1]
    blocks = length // SPAN
    sub_len = 8
    sub_count = SPAN // sub_len

    def to_blocks(tensor_in):
        moved = jnp.moveaxis(tensor_in, 1, 0)
        return moved.reshape((blocks, SPAN) + moved.shape[1:])

    def token_step(carried, step_inputs):
        query_row, key_row, value_row, beta_row, decay_row = step_inputs
        carried = jnp.exp(decay_row)[..., None, None] * carried
        predicted = jnp.einsum('bhk,bhkv->bhv', key_row, carried, precision=highest)
        update = beta_row[..., None] * (value_row - predicted)
        carried = carried + jnp.einsum('bhk,bhv->bhkv', key_row, update, precision=highest)
        return (carried, jnp.einsum('bhk,bhkv->bhv', query_row, carried, precision=highest))

    @jax.checkpoint
    def sub_step(carried, sub_inputs):
        return lax.scan(token_step, carried, sub_inputs)

    @jax.checkpoint
    def block_step(carried, block_inputs):
        shaped = jax.tree.map(lambda tensor_in: tensor_in.reshape((sub_count, sub_len) + tensor_in.shape[1:]), block_inputs)
        carried, sub_outputs = lax.scan(sub_step, carried, shaped)
        return (carried, sub_outputs.reshape((SPAN,) + sub_outputs.shape[2:]))
    initial = jnp.zeros((batch_size, head_count, key_size, value_size), jnp.float32)
    _, outputs = lax.scan(block_step, initial, (to_blocks(query_vecs), to_blocks(key_vecs), to_blocks(value_vecs), to_blocks(beta_vals), to_blocks(log_decays)))
    outputs = outputs.reshape(length, batch_size, head_count, value_size)
    return jnp.moveaxis(outputs, 0, 1)

def layer(params, inputs, live_mask):
    gain_in, gain_ffn, gain_out, w_query, w_key, w_value, w_gate, w_beta, w_decay, conv_query, conv_key, conv_value, decay_log, decay_bias, w_output, w_ffn_gate, w_ffn_up, w_ffn_down = params
    batch_size, length, _ = inputs.shape
    normed_in = low(inputs * rms_scale(inputs) * gain_in)
    query_pre = low_back(project(normed_in, w_query))
    key_pre = low_back(project(normed_in, w_key))
    value_pre = low_back(project(normed_in, w_value))
    gate_pre = low_back(project(normed_in, w_gate))
    beta_pre = low_back(project(normed_in, w_beta))
    decay_pre = low_back(project(normed_in, w_decay))
    query_vecs = unit_norm(jax.nn.silu(causal_conv(query_pre, low(conv_query).reshape(CONV, HK * DK))).reshape(batch_size, length, HK, DK)) * DK ** (-0.5)
    key_vecs = unit_norm(jax.nn.silu(causal_conv(key_pre, low(conv_key).reshape(CONV, HK * DK))).reshape(batch_size, length, HK, DK))
    value_vecs = jax.nn.silu(causal_conv(value_pre, low(conv_value).reshape(CONV, HK * DV))).reshape(batch_size, length, HK, DV)
    beta_vals = jax.nn.sigmoid(beta_pre) * live_mask[..., None]
    log_decays = -jnp.exp(decay_log) * jax.nn.softplus(decay_pre + decay_bias)
    mixed = delta_rule(query_vecs, key_vecs, value_vecs, beta_vals, log_decays)
    gated = mixed * rms_scale(mixed) * gain_out * jax.nn.silu(gate_pre.reshape(batch_size, length, HK, DV)) * live_mask[..., None, None]
    gated = low(gated.reshape(batch_size, length, HK * DV))
    hidden = inputs + low_back(project(gated, w_output))
    normed_ffn = low(hidden * rms_scale(hidden) * gain_ffn)
    gate_act = low_back(project(normed_ffn, w_ffn_gate))
    up_act = low_back(project(normed_ffn, w_ffn_up))
    inner = low(jax.nn.silu(gate_act) * up_act)
    return hidden + low_back(project(inner, w_ffn_down))

def reference(tokens, lengths, cotangent, gain_in, gain_ffn, gain_out, w_query, w_key, w_value, w_gate, w_beta, w_decay, conv_query, conv_key, conv_value, decay_log, decay_bias, w_output, w_ffn_gate, w_ffn_up, w_ffn_down):
    params = (gain_in, gain_ffn, gain_out, w_query, w_key, w_value, w_gate, w_beta, w_decay, conv_query, conv_key, conv_value, decay_log, decay_bias, w_output, w_ffn_gate, w_ffn_up, w_ffn_down)
    group_size = max(1, min(N_DP, 1024 // SLOT))
    group_count = N_DP // group_size
    token_groups = tokens.astype(jnp.float32).reshape(group_count, group_size, SLOT, D)
    cot_groups = cotangent.astype(jnp.float32).reshape(group_count, group_size, SLOT, D)
    length_groups = lengths.astype(jnp.int32).reshape(group_count, group_size)
    positions = jnp.arange(SLOT, dtype=jnp.int32)

    def one_group(summed, group_inputs):
        token_block, cot_block, length_block = group_inputs
        live_mask = (positions[None, :] < length_block[:, None]).astype(jnp.float32)
        result, pull_back = jax.vjp(lambda weights, activations: layer(weights, activations, live_mask), params, token_block)
        grad_weights, grad_acts = pull_back(cot_block)
        summed = jax.tree.map(lambda first_term, second_term: first_term + second_term, summed, grad_weights)
        return (summed, (result, grad_acts))
    initial = jax.tree.map(jnp.zeros_like, params)
    totals, (results, grad_groups) = lax.scan(one_group, initial, (token_groups, cot_groups, length_groups))
    return (results.reshape(TOKENS, D).astype(jnp.bfloat16), grad_groups.reshape(TOKENS, D), totals[0], totals[1], totals[2], totals[3], totals[4], totals[5], totals[6], totals[7], totals[8], totals[9], totals[10], totals[11], totals[12], totals[13], totals[14], totals[15], totals[16], totals[17])
```

```python
import functools
import jax
import jax.numpy as jnp
from jax import lax
from jax.sharding import PartitionSpec as P
from jax.experimental import pallas as pl
from jax.experimental.pallas import tpu as pltpu

CH = 256
TILE = 64
PADR = 8
f32 = jnp.float32
bf16 = jnp.bfloat16


def mm(a, b, ca=1, cb=0):
    return lax.dot_general(
        a.astype(bf16), b.astype(bf16), (((ca,), (cb,)), ((), ())), preferred_element_type=f32
    )


def split2(a):
    high = a.astype(bf16)
    return high, (a - high.astype(f32)).astype(bf16)


def mm3(a, b, ca=1, cb=0):
    ah, al = split2(a)
    bh, bl = split2(b)
    return mm(ah, bh, ca, cb) + (mm(ah, bl, ca, cb) + mm(al, bh, ca, cb))


def iotas(n):
    return (
        lax.broadcasted_iota(jnp.int32, (n, n), 0),
        lax.broadcasted_iota(jnp.int32, (n, n), 1),
    )


def unit_lower_inverses(mats):
    n = mats[0].shape[0]
    rows, cols = iotas(n)
    eye = jnp.where(rows == cols, 1.0, 0.0).astype(f32)
    base = 8
    near = (rows // base) == (cols // base)
    powers = [jnp.where(near, a, 0.0) for a in mats]
    outs = [eye - p for p in powers]
    for _ in range(2):
        powers = [mm3(p, p) for p in powers]
        outs = [x + mm3(x, p) for x, p in zip(outs, powers)]
    size = base
    while size < n:
        wide = ((rows // (2 * size)) == (cols // (2 * size))) & ((rows // size) != (cols // size))
        halves = [mm3(jnp.where(wide, a, 0.0), x) for a, x in zip(mats, outs)]
        outs = [x - mm3(x, h) for x, h in zip(outs, halves)]
        size *= 2
    return outs


def sigm(v):
    return 1.0 / (1.0 + jnp.exp(-v))


def softplus(v):
    return jnp.maximum(v, 0.0) + jnp.log1p(jnp.exp(-jnp.abs(v)))


def pick(block, lane):
    lanes = lax.broadcasted_iota(jnp.int32, block.shape, 1)
    return jnp.sum(jnp.where(lanes == lane, block, 0.0), axis=1, keepdims=True)


def taps(ref):
    return [ref[i : i + 1, :] for i in range(4)]


def lanes_at(block, width):
    return pl.ds(pl.multiple_of(block * width, width), width)


def conv_rows(pad_ref, start, size, filt):
    total = None
    block = pad_ref[pl.ds(start, size + PADR), :]
    for i in range(4):
        term = filt[i] * block[PADR - 3 + i : PADR - 3 + i + size]
        total = term if total is None else total + term
    return total


def chunk_decay(logs, n):
    rows, cols = iotas(n)
    lower = jnp.where(rows >= cols, 1.0, 0.0).astype(f32)
    wide = jnp.broadcast_to(logs, (n, 128))
    h0 = wide.astype(bf16)
    r1 = wide - h0.astype(f32)
    h1 = r1.astype(bf16)
    h2 = (r1 - h1.astype(f32)).astype(bf16)
    col = (mm(lower, h0) + (mm(lower, h1) + mm(lower, h2)))[:, :1]
    row = (mm(h0, lower, 0, 1) + (mm(h1, lower, 0, 1) + mm(h2, lower, 0, 1)))[:1, :]
    return col, row


def suffix_sum(vals, n):
    rows, cols = iotas(n)
    upper = jnp.where(cols >= rows, 1.0, 0.0).astype(f32)
    wide = jnp.broadcast_to(vals, (n, 128))
    h0 = wide.astype(bf16)
    r1 = wide - h0.astype(f32)
    h1 = r1.astype(bf16)
    h2 = (r1 - h1.astype(f32)).astype(bf16)
    return (mm(upper, h0) + (mm(upper, h1) + mm(upper, h2)))[:, :1]


def load_padded(pad_ref, src_ref):
    pad_ref[0:PADR, :] = jnp.zeros((PADR, pad_ref.shape[1]), f32)
    pad_ref[PADR : PADR + src_ref.shape[0], :] = src_ref[...].astype(f32)


def fill_vectors(length, qpad, kpad, vpad, fq, fk, fv, qs, ks, vs):
    def body(t, _):
        start = pl.multiple_of(t * TILE, TILE)
        for pad, filt, dst, scale in ((qpad, fq, qs, 256 ** (-0.5)), (kpad, fk, ks, 1.0)):
            y = conv_rows(pad, start, TILE, filt)
            a = y * sigm(y)
            n = a * lax.rsqrt(jnp.sum(a * a, axis=1, keepdims=True) + 1e-06)
            dst[pl.ds(start, TILE), :] = (n * scale).astype(dst.dtype)
        y = conv_rows(vpad, start, TILE, fv)
        vs[pl.ds(start, TILE), :] = y * sigm(y)
        return 0

    lax.fori_loop(0, length // TILE, body, 0)


def beta_decay(h, heads, length, live_len, bd, log_ref, bias_ref):
    bp = pick(bd, h)
    dp = pick(bd, heads + h)
    live = (lax.broadcasted_iota(jnp.int32, (length, 1), 0) < live_len).astype(f32)
    rate = jnp.exp(pick(log_ref[0:1, :], h))
    sb = sigm(bp)
    zp = dp + pick(bias_ref[0:1, :], h)
    return sb, live, rate, zp


def fwd_kernel(
    heads, len_ref, q_ref, k_ref, v_ref, g_ref, bd_ref, fq_ref, fk_ref, fv_ref, log_ref, bias_ref,
    gain_ref, gated_ref, inv_ref, u_ref, mixed_ref, state_ref, qpad, kpad, vpad, qs, ks, vs,
):
    h = pl.program_id(0)
    length = q_ref.shape[0]
    chunks = length // CH
    load_padded(qpad, q_ref)
    load_padded(kpad, k_ref)
    load_padded(vpad, v_ref)
    fill_vectors(
        length, qpad, kpad, vpad, taps(fq_ref), taps(fk_ref), taps(fv_ref), qs, ks, vs
    )
    sb, live, rate, zp = beta_decay(h, heads, length, len_ref[0], bd_ref[...], log_ref, bias_ref)
    beta = sb * live
    logs = -rate * softplus(zp)
    rows, cols = iotas(CH)
    kept = []
    mats = []
    for n in range(chunks):
        part = slice(n * CH, (n + 1) * CH)
        col, row = chunk_decay(logs[part], CH)
        gaps = col - row
        decay = jnp.where(rows >= cols, jnp.exp(jnp.where(rows >= cols, gaps, 0.0)), 0.0)
        kf = ks[part, :]
        gram = mm3(kf, kf, 1, 1)
        mats.append(jnp.where(rows > cols, beta[part] * decay * gram, 0.0))
        kept.append((part, col, decay))
    inverses = unit_lower_inverses(mats)
    state = None
    for n in range(chunks):
        part, col, decay = kept[n]
        kf = ks[part, :]
        qf = qs[part, :]
        inv_ref[0, part, :] = inverses[n].astype(inv_ref.dtype)
        grow = jnp.exp(col)
        rhs = vs[part, :]
        if state is not None:
            rhs = rhs - grow * mm(kf, state)
        u = mm3(inverses[n], beta[part] * rhs)
        u_ref[part, :] = u.astype(u_ref.dtype)
        scores = mm(qf, kf, 1, 1) * decay
        out = mm(scores, u)
        if state is not None:
            out = out + grow * mm(qf, state)
        mixed_ref[part, :] = out
        if n + 1 < chunks:
            last = col[CH - 1 :, :]
            add = mm(kf * jnp.exp(last - col), u, 0, 0)
            state = add if state is None else jnp.exp(last) * state + add
            state_ref[0, n] = state
    gain = gain_ref[0:1, :]
    live_len = len_ref[0]

    def finish(t, _):
        start = pl.multiple_of(t * TILE, TILE)
        sl = pl.ds(start, TILE)
        m = mixed_ref[sl, :]
        gp = g_ref[sl, :].astype(f32)
        pos = start + lax.broadcasted_iota(jnp.int32, (TILE, 1), 0)
        alive = (pos < live_len).astype(f32)
        r = lax.rsqrt(jnp.mean(m * m, axis=1, keepdims=True) + 1e-05)
        gated_ref[sl, :] = (m * r * gain * (gp * sigm(gp)) * alive).astype(bf16)
        return 0

    lax.fori_loop(0, length // TILE, finish, 0)


def bwd_kernel(
    heads, len_ref, q_ref, k_ref, v_ref, g_ref, bd_ref, fq_ref, fk_ref, fv_ref, log_ref, bias_ref,
    gain_ref, inv_ref, u_ref, mixed_ref, state_ref, dg_ref,
    dpre_out, dfq_out, dfk_out, dfv_out, dgain_out, dsmall_out,
    qpad, kpad, vpad, qs, ks, vs, dos, dqs, dks, dvs, dbds,
):
    h = pl.program_id(0)
    length = q_ref.shape[0]
    chunks = length // CH
    load_padded(qpad, q_ref)
    load_padded(kpad, k_ref)
    load_padded(vpad, v_ref)
    fq, fk, fv = taps(fq_ref), taps(fk_ref), taps(fv_ref)
    fill_vectors(length, qpad, kpad, vpad, fq, fk, fv, qs, ks, vs)
    live_len = len_ref[0]
    gain = gain_ref[0:1, :]

    @pl.when(h == 0)
    def _():
        dgain_out[...] = jnp.zeros(dgain_out.shape, f32)
        dbds[...] = jnp.zeros(dbds.shape, f32)
        dsmall_out[...] = jnp.zeros(dsmall_out.shape, f32)

    def gate_back(t, acc):
        start = pl.multiple_of(t * TILE, TILE)
        sl = pl.ds(start, TILE)
        m = mixed_ref[sl, :]
        gp = g_ref[sl, :].astype(f32)
        pos = start + lax.broadcasted_iota(jnp.int32, (TILE, 1), 0)
        alive = (pos < live_len).astype(f32)
        r = lax.rsqrt(jnp.mean(m * m, axis=1, keepdims=True) + 1e-05)
        n = m * r
        t_ = dg_ref[sl, :].astype(f32) * alive
        s = sigm(gp)
        act = gp * s
        tn = t_ * n
        dpre_out[sl, lanes_at(2 * heads + h, 512)] = (
            tn * gain * (s + act * (1.0 - s))
        ).astype(bf16)
        dn = t_ * gain * act
        dos[sl, :] = r * (dn - n * jnp.mean(dn * n, axis=1, keepdims=True))
        return acc + jnp.sum((tn * act).reshape(TILE // 8, 8, tn.shape[1]), axis=0)

    dgain = lax.fori_loop(0, length // TILE, gate_back, jnp.zeros((8, gain.shape[1]), f32))
    dgain_out[...] += dgain

    sb, live, rate, zp = beta_decay(h, heads, length, live_len, bd_ref[...], log_ref, bias_ref)
    beta = sb * live
    sp = softplus(zp)
    logs = -rate * sp
    rows, cols = iotas(CH)
    incl = rows >= cols
    ones = jnp.ones((CH, 128), f32)
    dstate = None
    dbetas = [None] * chunks
    dlogs = [None] * chunks
    for n in reversed(range(chunks)):
        part = slice(n * CH, (n + 1) * CH)
        col, row = chunk_decay(logs[part], CH)
        gaps = col - row
        decay = jnp.where(incl, jnp.exp(jnp.where(incl, gaps, 0.0)), 0.0)
        grow = jnp.exp(col)
        last = col[CH - 1 :, :]
        kf = ks[part, :]
        qf = qs[part, :]
        u = u_ref[part, :].astype(f32)
        inv = inv_ref[0, part, :]
        do = dos[part, :]
        b = beta[part]
        gram = mm(kf, kf, 1, 1)
        strict_decay = jnp.where(rows > cols, decay, 0.0)
        scores = mm(qf, kf, 1, 1) * decay
        m_all = mm(do, u, 1, 1)
        du = mm(scores, do, 0, 0)
        tail = jnp.exp(last - col)
        if dstate is not None:
            kend = kf * tail
            du = du + mm(kend, dstate)
        dr = mm(inv, du, 0, 0)
        dvs[part, :] = b * dr
        da = mm(dr, u, 1, 1)
        da_dec = -da * strict_decay
        da_gram = da_dec * gram
        dbeta = jnp.sum(da_gram, axis=1, keepdims=True)
        msc = m_all * scores
        both = msc + b * da_gram
        rs = jnp.sum(both, axis=1, keepdims=True)
        both_h, both_l = split2(both)
        cs = (mm(both_h, ones, 0, 0) + mm(both_l, ones, 0, 0))[:, :1]
        dc = rs - cs
        dqk = m_all * decay
        dgram = b * da_dec
        dq = mm(dqk, kf)
        dk = mm(dqk, qf, 0, 0) + mm(dgram, kf) + mm(dgram, kf, 0, 0)
        rest = vs[part, :]
        dlast = None
        if n > 0:
            state = state_ref[0, n - 1]
            kst = mm(kf, state)
            qst = mm(qf, state)
            rest = rest - grow * kst
            dkst = -(b * grow) * dr
            dqst = grow * do
            dk = dk + mm(dkst, state, 1, 1)
            dq = dq + mm(dqst, state, 1, 1)
            dc = dc + jnp.sum(dkst * kst + dqst * qst, axis=1, keepdims=True)
            dprev = mm(kf, dkst, 0, 0) + mm(qf, dqst, 0, 0)
        dbetas[n] = dbeta + jnp.sum(dr * rest, axis=1, keepdims=True)
        if dstate is not None:
            dkend = mm(u, dstate, 1, 1)
            dk = dk + dkend * tail
            w = jnp.sum(dkend * kend, axis=1, keepdims=True)
            dc = dc - w
            dlast = jnp.sum(w, axis=0, keepdims=True)
            if n > 0:
                scale = jnp.exp(last)
                dprev = dprev + scale * dstate
                dlast = dlast + scale * jnp.sum(
                    jnp.sum(dstate * state, axis=1, keepdims=True), axis=0, keepdims=True
                )
        dlog = suffix_sum(dc, CH)
        if dlast is not None:
            dlog = dlog + dlast
        dlogs[n] = dlog
        dqs[part, :] = dq
        dks[part, :] = dk
        if n > 0:
            dstate = dprev
    dbeta = jnp.concatenate(dbetas, axis=0)
    dlog = jnp.concatenate(dlogs, axis=0)
    dbp = dbeta * live * sb * (1.0 - sb)
    dzp = -rate * dlog * sigm(zp)
    lanes = lax.broadcasted_iota(jnp.int32, (length, 128), 1)
    dbds[...] += jnp.where(lanes == h, dbp, 0.0) + jnp.where(lanes == heads + h, dzp, 0.0)

    @pl.when(h == heads - 1)
    def _():
        dpre_out[:, 12 * heads * 128 : (12 * heads + 1) * 128] = dbds[...].astype(bf16)

    small_lane = lax.broadcasted_iota(jnp.int32, (8, 128), 1)
    small_row = lax.broadcasted_iota(jnp.int32, (8, 128), 0)
    at_head = small_lane == h
    dsmall_out[...] += jnp.where(
        at_head & (small_row == 0), jnp.sum(dlog * logs, axis=0, keepdims=True), 0.0
    ) + jnp.where(at_head & (small_row == 1), jnp.sum(dzp, axis=0, keepdims=True), 0.0)

    def pre_back(t, _):
        start = pl.multiple_of(t * TILE, TILE)
        sl = pl.ds(start, TILE)
        for pad, filt, dref, scale in ((qpad, fq, dqs, 256 ** (-0.5)), (kpad, fk, dks, 1.0)):
            y = conv_rows(pad, start, TILE, filt)
            s = sigm(y)
            a = y * s
            r = lax.rsqrt(jnp.sum(a * a, axis=1, keepdims=True) + 1e-06)
            nn = a * r
            dn = dref[sl, :] * scale
            da_ = r * (dn - nn * jnp.sum(dn * nn, axis=1, keepdims=True))
            dref[sl, :] = da_ * (s + a * (1.0 - s))
        y = conv_rows(vpad, start, TILE, fv)
        s = sigm(y)
        dvs[sl, :] = dvs[sl, :] * (s + y * s * (1.0 - s))
        return 0

    lax.fori_loop(0, length // TILE, pre_back, 0)
    for dref in (dqs, dks, dvs):
        dref[length : length + PADR, :] = jnp.zeros((PADR, dref.shape[1]), f32)

    for pad, filt, dref, first, fout in (
        (qpad, fq, dqs, h, dfq_out),
        (kpad, fk, dks, heads + h, dfk_out),
        (vpad, fv, dvs, heads + h, dfv_out),
    ):
        width = dref.shape[1]

        def conv_back(t, accs, pad=pad, filt=filt, dref=dref, first=first, width=width):
            start = pl.multiple_of(t * TILE, TILE)
            dx = None
            new = []
            dys = dref[pl.ds(start, TILE + PADR), :]
            xs = pad[pl.ds(start, TILE + PADR), :]
            dy = dys[:TILE]
            for i in range(4):
                term = filt[i] * dys[3 - i : 3 - i + TILE]
                dx = term if dx is None else dx + term
                prod = dy * xs[PADR - 3 + i : PADR - 3 + i + TILE]
                new.append(accs[i] + jnp.sum(prod.reshape(TILE // 8, 8, width), axis=0))
            dpre_out[pl.ds(start, TILE), lanes_at(first, width)] = dx.astype(bf16)
            return tuple(new)

        accs = lax.fori_loop(
            0, length // TILE, conv_back, tuple(jnp.zeros((8, width), f32) for _ in range(4))
        )
        for i in range(4):
            fout[i : i + 1, :] = jnp.sum(accs[i], axis=0, keepdims=True)


def col_spec(length, width, first=0):
    return pl.BlockSpec((length, width), lambda h: (0, first + h))


def whole_spec(shape):
    return pl.BlockSpec(shape, lambda h: (0,) * len(shape))


def front_specs(length, heads):
    return [
        pl.BlockSpec(memory_space=pltpu.SMEM),
        col_spec(length, 256),
        col_spec(length, 256, heads),
        col_spec(length, 512, heads),
        col_spec(length, 512, 2 * heads),
        pl.BlockSpec((length, 128), lambda h: (0, 12 * heads)),
        col_spec(4, 256),
        col_spec(4, 256),
        col_spec(4, 512),
        whole_spec((1, 128)),
        whole_spec((1, 128)),
        whole_spec((1, 512)),
    ]


def mixer_forward(heads, lens, pre, fq, fk, fv, logs, bias, gain):
    length = pre.shape[0]
    chunks = length // CH
    kept = max(1, chunks - 1)
    return pl.pallas_call(
        functools.partial(fwd_kernel, heads),
        grid=(heads,),
        in_specs=front_specs(length, heads),
        out_specs=[
            col_spec(length, 512),
            pl.BlockSpec((1, length, CH), lambda h: (h, 0, 0)),
            col_spec(length, 512),
            col_spec(length, 512),
            pl.BlockSpec((1, kept, 256, 512), lambda h: (h, 0, 0, 0)),
        ],
        out_shape=[
            jax.ShapeDtypeStruct((length, heads * 512), bf16),
            jax.ShapeDtypeStruct((heads, length, CH), bf16),
            jax.ShapeDtypeStruct((length, heads * 512), bf16),
            jax.ShapeDtypeStruct((length, heads * 512), f32),
            jax.ShapeDtypeStruct((heads, kept, 256, 512), f32),
        ],
        scratch_shapes=[
            pltpu.VMEM((length + PADR, 256), f32),
            pltpu.VMEM((length + PADR, 256), f32),
            pltpu.VMEM((length + PADR, 512), f32),
            pltpu.VMEM((length, 256), f32),
            pltpu.VMEM((length, 256), f32),
            pltpu.VMEM((length, 512), f32),
        ],
        compiler_params=pltpu.CompilerParams(vmem_limit_bytes=50 * 1024 * 1024),
        name="mixer_forward",
    )(lens, pre, pre, pre, pre, pre, fq, fk, fv, logs, bias, gain)


def mixer_backward(heads, lens, pre, fq, fk, fv, logs, bias, gain, saved, dgated):
    length = pre.shape[0]
    chunks = length // CH
    kept = max(1, chunks - 1)
    inv, u, mixed, states = saved
    return pl.pallas_call(
        functools.partial(bwd_kernel, heads),
        grid=(heads,),
        in_specs=front_specs(length, heads)
        + [
            pl.BlockSpec((1, length, CH), lambda h: (h, 0, 0)),
            col_spec(length, 512),
            col_spec(length, 512),
            pl.BlockSpec((1, kept, 256, 512), lambda h: (h, 0, 0, 0)),
            col_spec(length, 512),
        ],
        out_specs=[
            whole_spec((length, pre.shape[1])),
            col_spec(4, 256), col_spec(4, 256), col_spec(4, 512),
            whole_spec((8, 512)), whole_spec((8, 128)),
        ],
        out_shape=[
            jax.ShapeDtypeStruct(pre.shape, bf16),
            jax.ShapeDtypeStruct((4, heads * 256), f32),
            jax.ShapeDtypeStruct((4, heads * 256), f32),
            jax.ShapeDtypeStruct((4, heads * 512), f32),
            jax.ShapeDtypeStruct((8, 512), f32),
            jax.ShapeDtypeStruct((8, 128), f32),
        ],
        scratch_shapes=[
            pltpu.VMEM((length + PADR, 256), f32),
            pltpu.VMEM((length + PADR, 256), f32),
            pltpu.VMEM((length + PADR, 512), f32),
            pltpu.VMEM((length, 256), f32),
            pltpu.VMEM((length, 256), f32),
            pltpu.VMEM((length, 512), f32),
            pltpu.VMEM((length, 512), f32),
            pltpu.VMEM((length + PADR, 256), f32),
            pltpu.VMEM((length + PADR, 256), f32),
            pltpu.VMEM((length + PADR, 512), f32),
            pltpu.VMEM((length, 128), f32),
        ],
        compiler_params=pltpu.CompilerParams(vmem_limit_bytes=50 * 1024 * 1024),
        name="mixer_backward",
    )(lens, pre, pre, pre, pre, pre, fq, fk, fv, logs, bias, gain, inv, u, mixed, states, dgated)


EXTRA = 128


def rms_scale(values):
    return lax.rsqrt(jnp.mean(values * values, axis=-1, keepdims=True) + 1e-05)


def norm_back(values, gain, grad_normed):
    scale = rms_scale(values)
    unit_vals = values * scale
    grad_unit = grad_normed * gain
    grad_values = scale * (
        grad_unit - unit_vals * jnp.mean(grad_unit * unit_vals, axis=-1, keepdims=True)
    )
    return (grad_values, jnp.sum(grad_normed * unit_vals, axis=0))


def pair_swap(values):
    return lax.ppermute(values, "tensor", [(0, 1), (1, 0)])


def pair_gather(values):
    other = pair_swap(values)
    first = lax.axis_index("tensor") == 0
    return jnp.concatenate(
        [jnp.where(first, values, other), jnp.where(first, other, values)], axis=0
    )


def pair_scatter(parts):
    rows = parts.shape[0] // 2
    mine = lax.axis_index("tensor") * rows
    kept = lax.dynamic_slice_in_dim(parts, mine, rows)
    sent = lax.dynamic_slice_in_dim(parts, rows - mine, rows).astype(bf16)
    return kept + pair_swap(sent).astype(f32)


def dot(a, b, ca=1, cb=0):
    return lax.dot_general(a, b, (((ca,), (cb,)), ((), ())), preferred_element_type=f32)


def gather_rows(values):
    return lax.all_gather(values, "dp", axis=0, tiled=True)


def scatter_rows(values):
    return lax.psum_scatter(values, "dp", scatter_dimension=0, tiled=True)


def pack_filters(fq, fk, fv, rows):
    flat = jnp.concatenate([fq, fk, fv], axis=2).reshape(-1)
    return flat.reshape(-1, rows).T


def local(
    tokens,
    lengths,
    cotangent,
    gain_in,
    gain_ffn,
    gain_out,
    w_query,
    w_key,
    w_value,
    w_gate,
    w_beta,
    w_decay,
    conv_query,
    conv_key,
    conv_value,
    decay_log,
    decay_bias,
    w_output,
    w_ffn_gate,
    w_ffn_up,
    w_ffn_down,
):
    heads = w_beta.shape[1]
    rows = w_query.shape[0]
    devices = lax.axis_size("dp")
    low = lambda v: v.astype(bf16)
    filters = pack_filters(conv_query, conv_key, conv_value, rows)
    filter_cols = filters.shape[1]
    small = jnp.concatenate([w_beta, w_decay, filters], axis=1)
    small = jnp.pad(small, ((0, 0), (0, EXTRA - small.shape[1])))
    proj_shard = jnp.concatenate(
        [low(w_query), low(w_key), low(w_value), low(w_gate), low(small)], axis=1
    )
    proj = gather_rows(proj_shard)
    out_t = gather_rows(low(w_output).T)
    gains = jnp.concatenate([gain_in, gain_ffn, gain_out])
    gains = lax.all_gather(gains, ("dp", "tensor"), axis=0, tiled=False)
    n_in, n_out = gain_in.shape[0], gain_out.shape[0]
    full_in = gains[:, :n_in].reshape(-1)
    full_ffn = gains[:, n_in : 2 * n_in].reshape(-1)
    full_out = gains[:, 2 * n_in :].reshape(1, -1)
    gate_weight = gather_rows(low(w_ffn_gate))
    up_weight = gather_rows(low(w_ffn_up))
    down_t = gather_rows(low(w_ffn_down).T)

    tap_count = conv_query.shape[0]
    piece_q, piece_v = conv_query.shape[2], conv_value.shape[2]
    flat = proj[:, 12 * heads * 128 + 2 * heads : 12 * heads * 128 + 2 * heads + filter_cols]
    flat = flat.reshape(devices, rows, filter_cols).transpose(0, 2, 1)
    flat = flat.reshape(devices, tap_count, heads, 2 * piece_q + piece_v).astype(f32)
    flat = flat.transpose(1, 2, 0, 3)
    filt_q = flat[..., :piece_q].reshape(tap_count, -1)
    filt_k = flat[..., piece_q : 2 * piece_q].reshape(tap_count, -1)
    filt_v = flat[..., 2 * piece_q :].reshape(tap_count, -1)

    head_start = lax.axis_index("tensor") * heads
    lane_pad = lambda v: jnp.pad(
        lax.dynamic_slice_in_dim(v, head_start, heads), (0, 128 - heads)
    ).reshape(1, 128)
    local_log, local_bias = lane_pad(decay_log), lane_pad(decay_bias)

    inputs = tokens.astype(f32)
    normed_in = low(inputs * rms_scale(inputs) * full_in)
    seq_in = pair_gather(normed_in)
    seq_cot = pair_gather(cotangent)
    pre = dot(seq_in, proj)
    mixer_args = (heads, lengths, pre, filt_q, filt_k, filt_v, local_log, local_bias, full_out)
    gated, *saved = mixer_forward(*mixer_args)
    hidden = inputs + pair_scatter(dot(gated, out_t, 1, 1))
    normed_ffn = low(hidden * rms_scale(hidden) * full_ffn)
    seq_ffn = pair_gather(normed_ffn)

    gate_act = dot(seq_ffn, gate_weight)
    up_act = dot(seq_ffn, up_weight)
    sigmoid_gate = jax.nn.sigmoid(gate_act)
    silu_gate = gate_act * sigmoid_gate
    inner = low(silu_gate * up_act)
    result = low(hidden + pair_scatter(dot(inner, down_t, 1, 1)))

    grad_inner = dot(seq_cot, down_t)
    grad_down = low(dot(seq_cot, inner, 0, 0))
    grad_gate_act = low(
        grad_inner * up_act * sigmoid_gate * (1.0 + gate_act * (1.0 - sigmoid_gate))
    )
    grad_up_act = low(grad_inner * silu_gate)
    grad_gate_w = low(dot(seq_ffn, grad_gate_act, 0, 0))
    grad_up_w = low(dot(seq_ffn, grad_up_act, 0, 0))
    grad_seq_ffn = dot(grad_gate_act, gate_weight, 1, 1) + dot(grad_up_act, up_weight, 1, 1)
    grad_normed_ffn = pair_scatter(grad_seq_ffn)
    grad_hidden_norm, grad_gain_ffn = norm_back(hidden, full_ffn, grad_normed_ffn)
    grad_hidden = cotangent.astype(f32) + grad_hidden_norm
    seq_grad_branch = pair_gather(low(grad_hidden))

    down_piece = scatter_rows(grad_down)
    gate_piece = scatter_rows(grad_gate_w)
    up_piece = scatter_rows(grad_up_w)

    grad_gated = dot(seq_grad_branch, out_t)
    grad_out_t = low(dot(seq_grad_branch, gated, 0, 0))
    grad_pre, grad_fq, grad_fk, grad_fv, grad_gain_out, grad_small = mixer_backward(
        *mixer_args, saved, low(grad_gated)
    )
    grad_seq_in = dot(grad_pre, proj, 1, 1)
    grad_proj = low(dot(seq_in, grad_pre, 0, 0))
    by_device = lambda g, piece: g.reshape(tap_count, heads, devices, piece)
    grad_flat = jnp.concatenate(
        [by_device(grad_fq, piece_q), by_device(grad_fk, piece_q), by_device(grad_fv, piece_v)],
        axis=3,
    ).transpose(2, 0, 1, 3)
    grad_flat = grad_flat.reshape(devices, filter_cols, rows).transpose(0, 2, 1)
    grad_flat = low(grad_flat.reshape(devices * rows, filter_cols))
    grad_proj = lax.dynamic_update_slice(grad_proj, grad_flat, (0, 12 * heads * 128 + 2 * heads))
    grad_normed_in = pair_scatter(grad_seq_in)
    out_piece = scatter_rows(grad_out_t).astype(f32)
    proj_piece = scatter_rows(grad_proj).astype(f32)

    grad_inputs_norm, grad_gain_in = norm_back(inputs, full_in, grad_normed_in)
    grad_tokens = grad_hidden + grad_inputs_norm

    spread = lambda v: lax.dynamic_update_slice(jnp.zeros_like(decay_log), v, (head_start,))
    sums = jnp.concatenate(
        [
            grad_gain_in,
            grad_gain_ffn,
            jnp.sum(grad_gain_out, axis=0),
            spread(grad_small[0, :heads]),
            spread(grad_small[1, :heads]),
        ]
    )
    sums = lax.psum(sums, ("dp", "tensor"))
    shard_index = lax.axis_index("dp") * lax.axis_size("tensor") + lax.axis_index("tensor")
    width = full_in.shape[0]
    out_width = full_out.shape[1]
    take = lambda first, piece: lax.dynamic_slice_in_dim(sums, first + shard_index * piece, piece)
    n_heads = decay_log.shape[0]
    tail = 2 * width + out_width

    q_end, k_end = heads * 256, 2 * heads * 256
    v_end, g_end = k_end + heads * 512, k_end + 2 * heads * 512
    grad_filters = proj_piece[:, g_end + 2 * heads : g_end + 2 * heads + filter_cols]
    grad_filters = grad_filters.T.reshape(tap_count, heads, 2 * piece_q + piece_v)
    return (
        result,
        grad_tokens,
        take(0, n_in),
        take(width, n_in),
        take(2 * width, n_out),
        proj_piece[:, :q_end],
        proj_piece[:, q_end:k_end],
        proj_piece[:, k_end:v_end],
        proj_piece[:, v_end:g_end],
        proj_piece[:, g_end : g_end + heads],
        proj_piece[:, g_end + heads : g_end + 2 * heads],
        grad_filters[..., :piece_q],
        grad_filters[..., piece_q : 2 * piece_q],
        grad_filters[..., 2 * piece_q :],
        sums[tail : tail + n_heads],
        sums[tail + n_heads : tail + 2 * n_heads],
        out_piece.T,
        gate_piece.astype(f32),
        up_piece.astype(f32),
        down_piece.astype(f32).T,
    )


def solution(mesh):
    rows = P(("dp", "tensor"), None)
    spread = P(("dp", "tensor"))
    weight = P("dp", "tensor")
    filters = P(None, "tensor", "dp")
    turned = P("tensor", "dp")
    return jax.shard_map(
        local,
        mesh=mesh,
        in_specs=(rows, P("dp"), rows, spread, spread, spread)
        + (weight,) * 6
        + (filters,) * 3
        + (P(), P(), turned, weight, weight, turned),
        out_specs=(rows, rows, spread, spread, spread)
        + (weight,) * 6
        + (filters,) * 3
        + (P(), P(), turned, weight, weight, turned),
        check_vma=False,
    )
```

```python
import functools
import jax
import jax.numpy as jnp
from jax import lax
from jax.sharding import PartitionSpec as P
from jax.experimental import pallas as pl
from jax.experimental.pallas import tpu as pltpu

CH = 256
TILE = 64
PADR = 8
f32 = jnp.float32
bf16 = jnp.bfloat16


def mm(a, b, ca=1, cb=0):
    return lax.dot_general(
        a.astype(bf16), b.astype(bf16), (((ca,), (cb,)), ((), ())), preferred_element_type=f32
    )


def split2(a):
    high = a.astype(bf16)
    return high, (a - high.astype(f32)).astype(bf16)


def mm3(a, b, ca=1, cb=0):
    ah, al = split2(a)
    bh, bl = split2(b)
    return mm(ah, bh, ca, cb) + (mm(ah, bl, ca, cb) + mm(al, bh, ca, cb))


def iotas(n):
    return (
        lax.broadcasted_iota(jnp.int32, (n, n), 0),
        lax.broadcasted_iota(jnp.int32, (n, n), 1),
    )


def unit_lower_inverses(mats):
    n = mats[0].shape[0]
    rows, cols = iotas(n)
    eye = jnp.where(rows == cols, 1.0, 0.0).astype(f32)
    base = 8
    near = (rows // base) == (cols // base)
    powers = [jnp.where(near, a, 0.0) for a in mats]
    outs = [eye - p for p in powers]
    for _ in range(2):
        powers = [mm3(p, p) for p in powers]
        outs = [x + mm3(x, p) for x, p in zip(outs, powers)]
    size = base
    while size < n:
        wide = ((rows // (2 * size)) == (cols // (2 * size))) & ((rows // size) != (cols // size))
        halves = [mm3(jnp.where(wide, a, 0.0), x) for a, x in zip(mats, outs)]
        outs = [x - mm3(x, h) for x, h in zip(outs, halves)]
        size *= 2
    return outs


def sigm(v):
    return 1.0 / (1.0 + jnp.exp(-v))


def softplus(v):
    return jnp.maximum(v, 0.0) + jnp.log1p(jnp.exp(-jnp.abs(v)))


def pick(block, lane):
    lanes = lax.broadcasted_iota(jnp.int32, block.shape, 1)
    return jnp.sum(jnp.where(lanes == lane, block, 0.0), axis=1, keepdims=True)


def taps(ref):
    return [ref[i : i + 1, :] for i in range(4)]


def lanes_at(block, width):
    return pl.ds(pl.multiple_of(block * width, width), width)


def conv_rows(pad_ref, start, size, filt):
    total = None
    block = pad_ref[pl.ds(start, size + PADR), :]
    for i in range(4):
        term = filt[i] * block[PADR - 3 + i : PADR - 3 + i + size]
        total = term if total is None else total + term
    return total


def chunk_decay(logs, n):
    rows, cols = iotas(n)
    lower = jnp.where(rows >= cols, 1.0, 0.0).astype(f32)
    wide = jnp.broadcast_to(logs, (n, 128))
    h0 = wide.astype(bf16)
    r1 = wide - h0.astype(f32)
    h1 = r1.astype(bf16)
    h2 = (r1 - h1.astype(f32)).astype(bf16)
    col = (mm(lower, h0) + (mm(lower, h1) + mm(lower, h2)))[:, :1]
    row = (mm(h0, lower, 0, 1) + (mm(h1, lower, 0, 1) + mm(h2, lower, 0, 1)))[:1, :]
    return col, row


def suffix_sum(vals, n):
    rows, cols = iotas(n)
    upper = jnp.where(cols >= rows, 1.0, 0.0).astype(f32)
    wide = jnp.broadcast_to(vals, (n, 128))
    h0 = wide.astype(bf16)
    r1 = wide - h0.astype(f32)
    h1 = r1.astype(bf16)
    h2 = (r1 - h1.astype(f32)).astype(bf16)
    return (mm(upper, h0) + (mm(upper, h1) + mm(upper, h2)))[:, :1]


def load_padded(pad_ref, src_ref):
    pad_ref[0:PADR, :] = jnp.zeros((PADR, pad_ref.shape[1]), f32)
    pad_ref[PADR : PADR + src_ref.shape[0], :] = src_ref[...].astype(f32)


def fill_vectors(length, qpad, kpad, vpad, fq, fk, fv, qs, ks, vs):
    def body(t, _):
        start = pl.multiple_of(t * TILE, TILE)
        for pad, filt, dst, scale in ((qpad, fq, qs, 256 ** (-0.5)), (kpad, fk, ks, 1.0)):
            y = conv_rows(pad, start, TILE, filt)
            a = y * sigm(y)
            n = a * lax.rsqrt(jnp.sum(a * a, axis=1, keepdims=True) + 1e-06)
            dst[pl.ds(start, TILE), :] = (n * scale).astype(dst.dtype)
        y = conv_rows(vpad, start, TILE, fv)
        vs[pl.ds(start, TILE), :] = y * sigm(y)
        return 0

    lax.fori_loop(0, length // TILE, body, 0)


def beta_decay(h, heads, length, live_len, bd, log_ref, bias_ref):
    bp = pick(bd, h)
    dp = pick(bd, heads + h)
    live = (lax.broadcasted_iota(jnp.int32, (length, 1), 0) < live_len).astype(f32)
    rate = jnp.exp(pick(log_ref[0:1, :], h))
    sb = sigm(bp)
    zp = dp + pick(bias_ref[0:1, :], h)
    return sb, live, rate, zp


def fwd_kernel(
    heads, len_ref, q_ref, k_ref, v_ref, g_ref, bd_ref, fq_ref, fk_ref, fv_ref, log_ref, bias_ref,
    gain_ref, gated_ref, inv_ref, u_ref, mixed_ref, state_ref, qpad, kpad, vpad, qs, ks, vs,
):
    h = pl.program_id(0)
    length = q_ref.shape[0]
    chunks = length // CH
    load_padded(qpad, q_ref)
    load_padded(kpad, k_ref)
    load_padded(vpad, v_ref)
    fill_vectors(
        length, qpad, kpad, vpad, taps(fq_ref), taps(fk_ref), taps(fv_ref), qs, ks, vs
    )
    sb, live, rate, zp = beta_decay(h, heads, length, len_ref[0], bd_ref[...], log_ref, bias_ref)
    beta = sb * live
    logs = -rate * softplus(zp)
    rows, cols = iotas(CH)
    kept = []
    mats = []
    for n in range(chunks):
        part = slice(n * CH, (n + 1) * CH)
        col, row = chunk_decay(logs[part], CH)
        gaps = col - row
        decay = jnp.where(rows >= cols, jnp.exp(jnp.where(rows >= cols, gaps, 0.0)), 0.0)
        kf = ks[part, :]
        gram = mm3(kf, kf, 1, 1)
        mats.append(jnp.where(rows > cols, beta[part] * decay * gram, 0.0))
        kept.append((part, col, decay))
    inverses = unit_lower_inverses(mats)
    state = None
    for n in range(chunks):
        part, col, decay = kept[n]
        kf = ks[part, :]
        qf = qs[part, :]
        inv_ref[0, part, :] = inverses[n].astype(inv_ref.dtype)
        grow = jnp.exp(col)
        rhs = vs[part, :]
        if state is not None:
            rhs = rhs - grow * mm(kf, state)
        u = mm3(inverses[n], beta[part] * rhs)
        u_ref[part, :] = u.astype(u_ref.dtype)
        scores = mm(qf, kf, 1, 1) * decay
        out = mm(scores, u)
        if state is not None:
            out = out + grow * mm(qf, state)
        mixed_ref[part, :] = out
        if n + 1 < chunks:
            last = col[CH - 1 :, :]
            add = mm(kf * jnp.exp(last - col), u, 0, 0)
            state = add if state is None else jnp.exp(last) * state + add
            state_ref[0, n] = state
    gain = gain_ref[0:1, :]
    live_len = len_ref[0]

    def finish(t, _):
        start = pl.multiple_of(t * TILE, TILE)
        sl = pl.ds(start, TILE)
        m = mixed_ref[sl, :]
        gp = g_ref[sl, :].astype(f32)
        pos = start + lax.broadcasted_iota(jnp.int32, (TILE, 1), 0)
        alive = (pos < live_len).astype(f32)
        r = lax.rsqrt(jnp.mean(m * m, axis=1, keepdims=True) + 1e-05)
        gated_ref[sl, :] = (m * r * gain * (gp * sigm(gp)) * alive).astype(bf16)
        return 0

    lax.fori_loop(0, length // TILE, finish, 0)


def bwd_kernel(
    heads, len_ref, q_ref, k_ref, v_ref, g_ref, bd_ref, fq_ref, fk_ref, fv_ref, log_ref, bias_ref,
    gain_ref, inv_ref, u_ref, mixed_ref, state_ref, dg_ref,
    dpre_out, dfq_out, dfk_out, dfv_out, dgain_out, dsmall_out,
    qpad, kpad, vpad, qs, ks, vs, dos, dqs, dks, dvs, dbds,
):
    h = pl.program_id(0)
    length = q_ref.shape[0]
    chunks = length // CH
    load_padded(qpad, q_ref)
    load_padded(kpad, k_ref)
    load_padded(vpad, v_ref)
    fq, fk, fv = taps(fq_ref), taps(fk_ref), taps(fv_ref)
    fill_vectors(length, qpad, kpad, vpad, fq, fk, fv, qs, ks, vs)
    live_len = len_ref[0]
    gain = gain_ref[0:1, :]

    @pl.when(h == 0)
    def _():
        dgain_out[...] = jnp.zeros(dgain_out.shape, f32)
        dbds[...] = jnp.zeros(dbds.shape, f32)
        dsmall_out[...] = jnp.zeros(dsmall_out.shape, f32)

    def gate_back(t, acc):
        start = pl.multiple_of(t * TILE, TILE)
        sl = pl.ds(start, TILE)
        m = mixed_ref[sl, :]
        gp = g_ref[sl, :].astype(f32)
        pos = start + lax.broadcasted_iota(jnp.int32, (TILE, 1), 0)
        alive = (pos < live_len).astype(f32)
        r = lax.rsqrt(jnp.mean(m * m, axis=1, keepdims=True) + 1e-05)
        n = m * r
        t_ = dg_ref[sl, :].astype(f32) * alive
        s = sigm(gp)
        act = gp * s
        tn = t_ * n
        dpre_out[sl, lanes_at(2 * heads + h, 512)] = (
            tn * gain * (s + act * (1.0 - s))
        ).astype(bf16)
        dn = t_ * gain * act
        dos[sl, :] = r * (dn - n * jnp.mean(dn * n, axis=1, keepdims=True))
        return acc + jnp.sum((tn * act).reshape(TILE // 8, 8, tn.shape[1]), axis=0)

    dgain = lax.fori_loop(0, length // TILE, gate_back, jnp.zeros((8, gain.shape[1]), f32))
    dgain_out[...] += dgain

    sb, live, rate, zp = beta_decay(h, heads, length, live_len, bd_ref[...], log_ref, bias_ref)
    beta = sb * live
    sp = softplus(zp)
    logs = -rate * sp
    rows, cols = iotas(CH)
    incl = rows >= cols
    ones = jnp.ones((CH, 128), f32)
    dstate = None
    dbetas = [None] * chunks
    dlogs = [None] * chunks
    for n in reversed(range(chunks)):
        part = slice(n * CH, (n + 1) * CH)
        col, row = chunk_decay(logs[part], CH)
        gaps = col - row
        decay = jnp.where(incl, jnp.exp(jnp.where(incl, gaps, 0.0)), 0.0)
        grow = jnp.exp(col)
        last = col[CH - 1 :, :]
        kf = ks[part, :]
        qf = qs[part, :]
        u = u_ref[part, :].astype(f32)
        inv = inv_ref[0, part, :]
        do = dos[part, :]
        b = beta[part]
        gram = mm(kf, kf, 1, 1)
        strict_decay = jnp.where(rows > cols, decay, 0.0)
        scores = mm(qf, kf, 1, 1) * decay
        m_all = mm(do, u, 1, 1)
        du = mm(scores, do, 0, 0)
        tail = jnp.exp(last - col)
        if dstate is not None:
            kend = kf * tail
            du = du + mm(kend, dstate)
        dr = mm(inv, du, 0, 0)
        dvs[part, :] = b * dr
        da = mm(dr, u, 1, 1)
        da_dec = -da * strict_decay
        da_gram = da_dec * gram
        dbeta = jnp.sum(da_gram, axis=1, keepdims=True)
        msc = m_all * scores
        both = msc + b * da_gram
        rs = jnp.sum(both, axis=1, keepdims=True)
        both_h, both_l = split2(both)
        cs = (mm(both_h, ones, 0, 0) + mm(both_l, ones, 0, 0))[:, :1]
        dc = rs - cs
        dqk = m_all * decay
        dgram = b * da_dec
        dq = mm(dqk, kf)
        dk = mm(dqk, qf, 0, 0) + mm(dgram, kf) + mm(dgram, kf, 0, 0)
        rest = vs[part, :]
        dlast = None
        if n > 0:
            state = state_ref[0, n - 1]
            kst = mm(kf, state)
            qst = mm(qf, state)
            rest = rest - grow * kst
            dkst = -(b * grow) * dr
            dqst = grow * do
            dk = dk + mm(dkst, state, 1, 1)
            dq = dq + mm(dqst, state, 1, 1)
            dc = dc + jnp.sum(dkst * kst + dqst * qst, axis=1, keepdims=True)
            dprev = mm(kf, dkst, 0, 0) + mm(qf, dqst, 0, 0)
        dbetas[n] = dbeta + jnp.sum(dr * rest, axis=1, keepdims=True)
        if dstate is not None:
            dkend = mm(u, dstate, 1, 1)
            dk = dk + dkend * tail
            w = jnp.sum(dkend * kend, axis=1, keepdims=True)
            dc = dc - w
            dlast = jnp.sum(w, axis=0, keepdims=True)
            if n > 0:
                scale = jnp.exp(last)
                dprev = dprev + scale * dstate
                dlast = dlast + scale * jnp.sum(
                    jnp.sum(dstate * state, axis=1, keepdims=True), axis=0, keepdims=True
                )
        dlog = suffix_sum(dc, CH)
        if dlast is not None:
            dlog = dlog + dlast
        dlogs[n] = dlog
        dqs[part, :] = dq
        dks[part, :] = dk
        if n > 0:
            dstate = dprev
    dbeta = jnp.concatenate(dbetas, axis=0)
    dlog = jnp.concatenate(dlogs, axis=0)
    dbp = dbeta * live * sb * (1.0 - sb)
    dzp = -rate * dlog * sigm(zp)
    lanes = lax.broadcasted_iota(jnp.int32, (length, 128), 1)
    dbds[...] += jnp.where(lanes == h, dbp, 0.0) + jnp.where(lanes == heads + h, dzp, 0.0)

    @pl.when(h == heads - 1)
    def _():
        dpre_out[:, 12 * heads * 128 : (12 * heads + 1) * 128] = dbds[...].astype(bf16)

    small_lane = lax.broadcasted_iota(jnp.int32, (8, 128), 1)
    small_row = lax.broadcasted_iota(jnp.int32, (8, 128), 0)
    at_head = small_lane == h
    dsmall_out[...] += jnp.where(
        at_head & (small_row == 0), jnp.sum(dlog * logs, axis=0, keepdims=True), 0.0
    ) + jnp.where(at_head & (small_row == 1), jnp.sum(dzp, axis=0, keepdims=True), 0.0)

    def pre_back(t, _):
        start = pl.multiple_of(t * TILE, TILE)
        sl = pl.ds(start, TILE)
        for pad, filt, dref, scale in ((qpad, fq, dqs, 256 ** (-0.5)), (kpad, fk, dks, 1.0)):
            y = conv_rows(pad, start, TILE, filt)
            s = sigm(y)
            a = y * s
            r = lax.rsqrt(jnp.sum(a * a, axis=1, keepdims=True) + 1e-06)
            nn = a * r
            dn = dref[sl, :] * scale
            da_ = r * (dn - nn * jnp.sum(dn * nn, axis=1, keepdims=True))
            dref[sl, :] = da_ * (s + a * (1.0 - s))
        y = conv_rows(vpad, start, TILE, fv)
        s = sigm(y)
        dvs[sl, :] = dvs[sl, :] * (s + y * s * (1.0 - s))
        return 0

    lax.fori_loop(0, length // TILE, pre_back, 0)
    for dref in (dqs, dks, dvs):
        dref[length : length + PADR, :] = jnp.zeros((PADR, dref.shape[1]), f32)

    for pad, filt, dref, first, fout in (
        (qpad, fq, dqs, h, dfq_out),
        (kpad, fk, dks, heads + h, dfk_out),
        (vpad, fv, dvs, heads + h, dfv_out),
    ):
        width = dref.shape[1]

        def conv_back(t, accs, pad=pad, filt=filt, dref=dref, first=first, width=width):
            start = pl.multiple_of(t * TILE, TILE)
            dx = None
            new = []
            dys = dref[pl.ds(start, TILE + PADR), :]
            xs = pad[pl.ds(start, TILE + PADR), :]
            dy = dys[:TILE]
            for i in range(4):
                term = filt[i] * dys[3 - i : 3 - i + TILE]
                dx = term if dx is None else dx + term
                prod = dy * xs[PADR - 3 + i : PADR - 3 + i + TILE]
                new.append(accs[i] + jnp.sum(prod.reshape(TILE // 8, 8, width), axis=0))
            dpre_out[pl.ds(start, TILE), lanes_at(first, width)] = dx.astype(bf16)
            return tuple(new)

        accs = lax.fori_loop(
            0, length // TILE, conv_back, tuple(jnp.zeros((8, width), f32) for _ in range(4))
        )
        for i in range(4):
            fout[i : i + 1, :] = jnp.sum(accs[i], axis=0, keepdims=True)


def col_spec(length, width, first=0):
    return pl.BlockSpec((length, width), lambda h: (0, first + h))


def whole_spec(shape):
    return pl.BlockSpec(shape, lambda h: (0,) * len(shape))


def front_specs(length, heads):
    return [
        pl.BlockSpec(memory_space=pltpu.SMEM),
        col_spec(length, 256),
        col_spec(length, 256, heads),
        col_spec(length, 512, heads),
        col_spec(length, 512, 2 * heads),
        pl.BlockSpec((length, 128), lambda h: (0, 12 * heads)),
        col_spec(4, 256),
        col_spec(4, 256),
        col_spec(4, 512),
        whole_spec((1, 128)),
        whole_spec((1, 128)),
        whole_spec((1, 512)),
    ]


def mixer_forward(heads, lens, pre, fq, fk, fv, logs, bias, gain):
    length = pre.shape[0]
    chunks = length // CH
    kept = max(1, chunks - 1)
    return pl.pallas_call(
        functools.partial(fwd_kernel, heads),
        grid=(heads,),
        in_specs=front_specs(length, heads),
        out_specs=[
            col_spec(length, 512),
            pl.BlockSpec((1, length, CH), lambda h: (h, 0, 0)),
            col_spec(length, 512),
            col_spec(length, 512),
            pl.BlockSpec((1, kept, 256, 512), lambda h: (h, 0, 0, 0)),
        ],
        out_shape=[
            jax.ShapeDtypeStruct((length, heads * 512), bf16),
            jax.ShapeDtypeStruct((heads, length, CH), bf16),
            jax.ShapeDtypeStruct((length, heads * 512), bf16),
            jax.ShapeDtypeStruct((length, heads * 512), f32),
            jax.ShapeDtypeStruct((heads, kept, 256, 512), f32),
        ],
        scratch_shapes=[
            pltpu.VMEM((length + PADR, 256), f32),
            pltpu.VMEM((length + PADR, 256), f32),
            pltpu.VMEM((length + PADR, 512), f32),
            pltpu.VMEM((length, 256), f32),
            pltpu.VMEM((length, 256), f32),
            pltpu.VMEM((length, 512), f32),
        ],
        compiler_params=pltpu.CompilerParams(vmem_limit_bytes=50 * 1024 * 1024),
        name="mixer_forward",
    )(lens, pre, pre, pre, pre, pre, fq, fk, fv, logs, bias, gain)


def mixer_backward(heads, lens, pre, fq, fk, fv, logs, bias, gain, saved, dgated):
    length = pre.shape[0]
    chunks = length // CH
    kept = max(1, chunks - 1)
    inv, u, mixed, states = saved
    return pl.pallas_call(
        functools.partial(bwd_kernel, heads),
        grid=(heads,),
        in_specs=front_specs(length, heads)
        + [
            pl.BlockSpec((1, length, CH), lambda h: (h, 0, 0)),
            col_spec(length, 512),
            col_spec(length, 512),
            pl.BlockSpec((1, kept, 256, 512), lambda h: (h, 0, 0, 0)),
            col_spec(length, 512),
        ],
        out_specs=[
            whole_spec((length, pre.shape[1])),
            col_spec(4, 256), col_spec(4, 256), col_spec(4, 512),
            whole_spec((8, 512)), whole_spec((8, 128)),
        ],
        out_shape=[
            jax.ShapeDtypeStruct(pre.shape, bf16),
            jax.ShapeDtypeStruct((4, heads * 256), f32),
            jax.ShapeDtypeStruct((4, heads * 256), f32),
            jax.ShapeDtypeStruct((4, heads * 512), f32),
            jax.ShapeDtypeStruct((8, 512), f32),
            jax.ShapeDtypeStruct((8, 128), f32),
        ],
        scratch_shapes=[
            pltpu.VMEM((length + PADR, 256), f32),
            pltpu.VMEM((length + PADR, 256), f32),
            pltpu.VMEM((length + PADR, 512), f32),
            pltpu.VMEM((length, 256), f32),
            pltpu.VMEM((length, 256), f32),
            pltpu.VMEM((length, 512), f32),
            pltpu.VMEM((length, 512), f32),
            pltpu.VMEM((length + PADR, 256), f32),
            pltpu.VMEM((length + PADR, 256), f32),
            pltpu.VMEM((length + PADR, 512), f32),
            pltpu.VMEM((length, 128), f32),
        ],
        compiler_params=pltpu.CompilerParams(vmem_limit_bytes=50 * 1024 * 1024),
        name="mixer_backward",
    )(lens, pre, pre, pre, pre, pre, fq, fk, fv, logs, bias, gain, inv, u, mixed, states, dgated)


MESH = pl.DeviceIdType.MESH


def column_chunks(widths, size):
    out = []
    for a, width in enumerate(widths):
        units = width // 128
        count = max(1, -(-width // size))
        lo = 0
        for i in range(count):
            hi = units * (i + 1) // count
            out.append((a, lo * 128, (hi - lo) * 128))
            lo = hi
    return out


def placement():
    spot = lax.axis_index("dp")
    return spot, lax.rem(spot, 2), lax.rem(lax.div(spot, 2), 2), lax.div(spot, 4)


def greet(partners):
    barrier = pltpu.get_barrier_semaphore()
    for partner in partners:
        pl.semaphore_signal(barrier, inc=1, device_id={"dp": partner}, device_id_type=MESH)
    pl.semaphore_wait(barrier, len(partners))


def remote(src, dst, send, recv, target):
    return pltpu.make_async_remote_copy(
        src_ref=src, dst_ref=dst, send_sem=send, recv_sem=recv,
        device_id={"dp": target}, device_id_type=MESH,
    )


def gather_kernel(layers, chunks, count, *refs):
    srcs, outs = refs[:count], refs[count : 2 * count]
    own_sem, zs, zr, ys, yr, cs, cr = refs[2 * count :]
    rows = srcs[0].shape[0]
    spot, core, side, layer = placement()
    at = lambda z, y, c: 4 * lax.rem(z + layers, layers) + 2 * y + c
    z_to = [at(layer + k, side, core) for k in range(1, layers)]
    y_to, c_to = at(layer, 1 - side, core), at(layer, side, 1 - core)
    greet(z_to + [y_to, c_to])

    def place(j, origin):
        a, lo, width = chunks[j]
        start = pl.multiple_of(origin * rows, rows)
        return outs[a].at[pl.ds(start, rows), lo : lo + width]

    def own(j):
        a, lo, width = chunks[j]
        return srcs[a].at[:, lo : lo + width]

    def z_copy(j, k, origin, src):
        return remote(src, place(j, origin), zs.at[j, k - 1], zr.at[j, k - 1], z_to[k - 1])

    def y_copy(j, m, origin, src):
        return remote(src, place(j, origin), ys.at[j, m], yr.at[j, m], y_to)

    def c_copy(j, m, half, origin, src):
        i = 2 * m + half
        return remote(src, place(j, origin), cs.at[j, i], cr.at[j, i], c_to)

    keep = []
    number = len(chunks)
    for j in range(number):
        for k in range(1, layers):
            z_copy(j, k, spot, own(j)).start()
        y_copy(j, 0, spot, own(j)).start()
        c_copy(j, 0, 0, spot, own(j)).start()
        copy = pltpu.make_async_copy(own(j), place(j, spot), own_sem.at[j])
        copy.start()
        keep.append(copy)

    def second(j):
        for k in range(1, layers):
            origin = at(layer - k, side, core)
            here = place(j, origin)
            z_copy(j, k, origin, here).wait_recv()
            y_copy(j, k, origin, here).start()
            c_copy(j, k, 0, origin, here).start()

    def third(j):
        for m in range(layers):
            origin = at(layer - m, 1 - side, core)
            here = place(j, origin)
            y_copy(j, m, origin, here).wait_recv()
            c_copy(j, m, 1, origin, here).start()

    for j in range(number + 1):
        if j < number:
            second(j)
        if j >= 1:
            third(j - 1)
    for j in range(number):
        keep[j].wait()
        for k in range(1, layers):
            z_copy(j, k, spot, own(j)).wait_send()
        for m in range(layers):
            y_copy(j, m, spot, own(j)).wait_send()
            for half in range(2):
                origin = at(layer - m, lax.rem(side + half, 2), 1 - core)
                c_copy(j, m, half, origin, place(j, origin)).wait()


def gather_all(shards, devices, ident, size=512):
    rows = shards[0].shape[0]
    layers = devices // 4
    chunks = column_chunks([s.shape[1] for s in shards], size)
    n = len(chunks)
    sem = lambda *shape: pltpu.SemaphoreType.DMA(shape)
    return pl.pallas_call(
        functools.partial(gather_kernel, layers, chunks, len(shards)),
        in_specs=[pl.BlockSpec(memory_space=pl.ANY)] * len(shards),
        out_specs=[pl.BlockSpec(memory_space=pl.ANY)] * len(shards),
        out_shape=[jax.ShapeDtypeStruct((devices * rows, s.shape[1]), s.dtype) for s in shards],
        scratch_shapes=[
            sem(n), sem(n, layers - 1), sem(n, layers - 1), sem(n, layers), sem(n, layers),
            sem(n, 2 * layers), sem(n, 2 * layers),
        ],
        compiler_params=pltpu.CompilerParams(collective_id=ident, has_side_effects=True),
        name="gather_rows",
    )(*shards)


def scatter_kernel(layers, chunks, count, *refs):
    srcs, out = refs[:count], refs[count]
    stage, buf1, buf2, buf3, own_sem, cs, cr, ys, yr, zs, zr = refs[count + 1 :]
    rows = out.shape[0]
    spot, core, side, layer = placement()
    at = lambda z, y, c: 4 * lax.rem(z + layers, layers) + 2 * y + c
    z_to = [at(layer + k, side, core) for k in range(1, layers)]
    y_to, c_to = at(layer, 1 - side, core), at(layer, side, 1 - core)
    greet(z_to + [y_to, c_to])
    number = len(chunks)
    firsts = []
    total = 0
    for a, lo, width in chunks:
        firsts.append(total)
        total += width

    def cols(j):
        return slice(firsts[j], firsts[j] + chunks[j][2])

    def c_copy(j):
        a, lo, width = chunks[j]
        return remote(
            srcs[a].at[:, 1 - core, :, lo : lo + width], buf1.at[:, :, cols(j)],
            cs.at[j], cr.at[j], c_to,
        )

    def own_copy(j):
        a, lo, width = chunks[j]
        return pltpu.make_async_copy(
            srcs[a].at[:, core, :, lo : lo + width],
            stage.at[j % 2, :, :, 0:width], own_sem.at[j],
        )

    def y_copy(j, m):
        block = 2 * lax.rem(layer + m, layers) + 1 - side
        return remote(
            buf1.at[block, :, cols(j)], buf2.at[m, :, cols(j)], ys.at[j, m], yr.at[j, m], y_to
        )

    def z_copy(j, k):
        return remote(
            buf2.at[k, :, cols(j)], buf3.at[k - 1, :, cols(j)], zs.at[j, k - 1], zr.at[j, k - 1],
            z_to[k - 1],
        )

    for j in range(number):
        c_copy(j).start()
    for j in range(min(2, number)):
        own_copy(j).start()

    def first(j):
        width = chunks[j][2]
        own_copy(j).wait()
        c_copy(j).wait_recv()

        def body(b, _):
            mine = stage[j % 2, b, :, 0:width].astype(f32)
            buf1[b, :, cols(j)] = (buf1[b, :, cols(j)].astype(f32) + mine).astype(bf16)
            return 0

        lax.fori_loop(0, 2 * layers, body, 0)
        for m in list(range(1, layers)) + [0]:
            y_copy(j, m).start()
        if j + 2 < number:
            own_copy(j + 2).start()

    def second(j):
        for m in list(range(1, layers)) + [0]:
            y_copy(j, m).wait_recv()
            block = 2 * lax.rem(layer + m, layers) + side
            mine = buf1[block, :, cols(j)].astype(f32)
            buf2[m, :, cols(j)] = (buf2[m, :, cols(j)].astype(f32) + mine).astype(bf16)
            if m:
                z_copy(j, m).start()

    def third(j):
        total = buf2[0, :, cols(j)].astype(f32)
        for k in range(1, layers):
            z_copy(j, k).wait_recv()
            total = total + buf3[k - 1, :, cols(j)].astype(f32)
        out[:, cols(j)] = total

    for j in range(number + 4):
        if j < number:
            first(j)
        if 0 <= j - 2 < number:
            second(j - 2)
        if 0 <= j - 4 < number:
            third(j - 4)
    for j in range(number):
        c_copy(j).wait_send()
        for m in range(layers):
            y_copy(j, m).wait_send()
        for k in range(1, layers):
            z_copy(j, k).wait_send()


def scatter_sum(parts, widths, devices, ident, size=512):
    widths = [w or p.shape[1] for w, p in zip(widths, parts)]
    rows = parts[0].shape[0] // devices
    layers = devices // 4
    chunks = column_chunks(widths, size)
    n = len(chunks)
    width = sum(widths)
    widest = max(c[2] for c in chunks)
    sem = lambda *shape: pltpu.SemaphoreType.DMA(shape)
    return pl.pallas_call(
        functools.partial(scatter_kernel, layers, chunks, len(parts)),
        in_specs=[pl.BlockSpec(memory_space=pl.ANY)] * len(parts),
        out_specs=pl.BlockSpec(memory_space=pltpu.VMEM),
        out_shape=jax.ShapeDtypeStruct((rows, width), f32),
        scratch_shapes=[
            pltpu.VMEM((2, 2 * layers, rows, widest), bf16),
            pltpu.VMEM((2 * layers, rows, width), bf16),
            pltpu.VMEM((layers, rows, width), bf16),
            pltpu.VMEM((layers - 1, rows, width), bf16),
            sem(n), sem(n), sem(n), sem(n, layers), sem(n, layers),
            sem(n, layers - 1), sem(n, layers - 1),
        ],
        compiler_params=pltpu.CompilerParams(
            collective_id=ident, has_side_effects=True, vmem_limit_bytes=52 * 1024 * 1024
        ),
        name="scatter_sum",
    )(*[p.reshape(devices // 2, 2, rows, p.shape[1]) for p in parts])


EXTRA = 128


def rms_scale(values):
    return lax.rsqrt(jnp.mean(values * values, axis=-1, keepdims=True) + 1e-05)


def norm_back(values, gain, grad_normed):
    scale = rms_scale(values)
    unit_vals = values * scale
    grad_unit = grad_normed * gain
    grad_values = scale * (
        grad_unit - unit_vals * jnp.mean(grad_unit * unit_vals, axis=-1, keepdims=True)
    )
    return (grad_values, jnp.sum(grad_normed * unit_vals, axis=0))


def pair_swap(values):
    return lax.ppermute(values, "tensor", [(0, 1), (1, 0)])


def pair_gather(values):
    other = pair_swap(values)
    first = lax.axis_index("tensor") == 0
    return jnp.concatenate(
        [jnp.where(first, values, other), jnp.where(first, other, values)], axis=0
    )


def pair_scatter(parts):
    rows = parts.shape[0] // 2
    mine = lax.axis_index("tensor") * rows
    kept = lax.dynamic_slice_in_dim(parts, mine, rows)
    sent = lax.dynamic_slice_in_dim(parts, rows - mine, rows).astype(bf16)
    return kept + pair_swap(sent).astype(f32)


def dot(a, b, ca=1, cb=0):
    return lax.dot_general(a, b, (((ca,), (cb,)), ((), ())), preferred_element_type=f32)


def high_low(values):
    high = lax.reduce_precision(values, 8, 7)
    return jnp.stack([high, values - high], axis=1).astype(bf16)


def gather_rows(values):
    return lax.all_gather(values, "dp", axis=0, tiled=True)


def scatter_rows(values):
    return lax.psum_scatter(values, "dp", scatter_dimension=0, tiled=True)


def pack_filters(fq, fk, fv, rows):
    flat = jnp.concatenate([fq, fk, fv], axis=2).reshape(-1)
    return flat.reshape(-1, rows).T


def local(
    tokens,
    lengths,
    cotangent,
    gain_in,
    gain_ffn,
    gain_out,
    w_query,
    w_key,
    w_value,
    w_gate,
    w_beta,
    w_decay,
    conv_query,
    conv_key,
    conv_value,
    decay_log,
    decay_bias,
    w_output,
    w_ffn_gate,
    w_ffn_up,
    w_ffn_down,
):
    heads = w_beta.shape[1]
    rows = w_query.shape[0]
    devices = lax.axis_size("dp")
    low = lambda v: v.astype(bf16)
    filters = pack_filters(conv_query, conv_key, conv_value, rows)
    filter_cols = filters.shape[1]
    gains = pair_gather(jnp.concatenate([gain_in, gain_ffn, gain_out])[None])
    n_in, n_out = gain_in.shape[0], gain_out.shape[0]
    pair_out = jnp.pad(gains[:, 2 * n_in :].reshape(-1), (0, rows - 2 * n_out))
    small = jnp.concatenate(
        [
            low(jnp.concatenate([w_beta, w_decay, filters], axis=1)),
            high_low(gains[:, :n_in].reshape(-1)),
            high_low(gains[:, n_in : 2 * n_in].reshape(-1)),
            high_low(pair_out),
        ],
        axis=1,
    )
    small = jnp.pad(small, ((0, 0), (0, EXTRA - small.shape[1])))
    proj_shard = jnp.concatenate(
        [low(w_query), low(w_key), low(w_value), low(w_gate), small], axis=1
    )
    seq_x = pair_gather(tokens)
    seq_cot = pair_gather(cotangent)
    proj, out_t = gather_all((proj_shard, low(w_output).T), devices, 0)
    extra_at = 12 * heads * 128
    gain_at = extra_at + 2 * heads + filter_cols
    sides = proj[:, gain_at : gain_at + 6].astype(f32)
    sides = sides[:, 0::2] + sides[:, 1::2]
    full_in, full_ffn = sides[:, 0], sides[:, 1]
    full_out = sides[:, 2].reshape(devices, rows)[:, : 2 * n_out].reshape(1, -1)
    gate_weight = gather_rows(low(w_ffn_gate))
    up_weight = gather_rows(low(w_ffn_up))
    down_t = gather_rows(low(w_ffn_down).T)

    tap_count = conv_query.shape[0]
    piece_q, piece_v = conv_query.shape[2], conv_value.shape[2]
    flat = proj[:, extra_at + 2 * heads : gain_at]
    flat = flat.reshape(devices, rows, filter_cols).transpose(0, 2, 1)
    flat = flat.reshape(devices, tap_count, heads, 2 * piece_q + piece_v).astype(f32)
    flat = flat.transpose(1, 2, 0, 3)
    filt_q = flat[..., :piece_q].reshape(tap_count, -1)
    filt_k = flat[..., piece_q : 2 * piece_q].reshape(tap_count, -1)
    filt_v = flat[..., 2 * piece_q :].reshape(tap_count, -1)

    head_start = lax.axis_index("tensor") * heads
    lane_pad = lambda v: jnp.pad(
        lax.dynamic_slice_in_dim(v, head_start, heads), (0, 128 - heads)
    ).reshape(1, 128)
    local_log, local_bias = lane_pad(decay_log), lane_pad(decay_bias)

    inputs = tokens.astype(f32)
    seq_inputs = seq_x.astype(f32)
    seq_unit = seq_inputs * rms_scale(seq_inputs)
    seq_in = low(seq_unit * full_in)
    pre = dot(seq_in, proj)
    mixer_args = (heads, lengths, pre, filt_q, filt_k, filt_v, local_log, local_bias, full_out)
    gated, *saved = mixer_forward(*mixer_args)
    hidden = inputs + pair_scatter(dot(gated, out_t, 1, 1))
    normed_ffn = low(hidden * rms_scale(hidden) * full_ffn)
    seq_ffn = pair_gather(normed_ffn)

    gate_act = dot(seq_ffn, gate_weight)
    up_act = dot(seq_ffn, up_weight)
    sigmoid_gate = jax.nn.sigmoid(gate_act)
    silu_gate = gate_act * sigmoid_gate
    inner = low(silu_gate * up_act)
    result = low(hidden + pair_scatter(dot(inner, down_t, 1, 1)))

    grad_inner = dot(seq_cot, down_t)
    grad_down = low(dot(seq_cot, inner, 0, 0))
    grad_gate_act = low(
        grad_inner * up_act * sigmoid_gate * (1.0 + gate_act * (1.0 - sigmoid_gate))
    )
    grad_up_act = low(grad_inner * silu_gate)
    grad_gate_w = low(dot(seq_ffn, grad_gate_act, 0, 0))
    grad_up_w = low(dot(seq_ffn, grad_up_act, 0, 0))
    grad_seq_ffn = dot(grad_gate_act, gate_weight, 1, 1) + dot(grad_up_act, up_weight, 1, 1)
    grad_normed_ffn = pair_scatter(grad_seq_ffn)
    grad_hidden_norm, grad_gain_ffn = norm_back(hidden, full_ffn, grad_normed_ffn)
    grad_hidden = cotangent.astype(f32) + grad_hidden_norm
    seq_grad_branch = pair_gather(low(grad_hidden))

    down_piece = scatter_rows(grad_down)
    gate_piece = scatter_rows(grad_gate_w)
    up_piece = scatter_rows(grad_up_w)

    grad_gated = dot(seq_grad_branch, out_t)
    grad_out_t = low(dot(seq_grad_branch, gated, 0, 0))
    grad_pre, grad_fq, grad_fk, grad_fv, grad_gain_out, grad_small = mixer_backward(
        *mixer_args, saved, low(grad_gated)
    )
    grad_seq_in = dot(grad_pre, proj, 1, 1)
    grad_proj = low(dot(seq_in, grad_pre, 0, 0))
    by_device = lambda g, piece: g.reshape(tap_count, heads, devices, piece)
    grad_flat = jnp.concatenate(
        [by_device(grad_fq, piece_q), by_device(grad_fk, piece_q), by_device(grad_fv, piece_v)],
        axis=3,
    ).transpose(2, 0, 1, 3)
    grad_flat = grad_flat.reshape(devices, filter_cols, rows).transpose(0, 2, 1)
    grad_flat = low(grad_flat.reshape(devices * rows, filter_cols))
    spread = lambda v: lax.dynamic_update_slice(jnp.zeros_like(decay_log), v, (head_start,))
    grad_decay = jnp.concatenate([spread(grad_small[0, :heads]), spread(grad_small[1, :heads])])
    by_rows = lambda v: jnp.pad(v, ((0, 0), (0, rows - v.shape[1]))).reshape(-1)
    columns = jnp.stack(
        [
            jnp.sum(grad_seq_in * seq_unit, axis=0),
            grad_gain_ffn,
            by_rows(jnp.sum(grad_gain_out, axis=0).reshape(devices, -1)),
            by_rows(jnp.broadcast_to(grad_decay, (devices,) + grad_decay.shape)),
        ],
        axis=1,
    )
    grad_tiny = jnp.concatenate(
        [grad_proj[:, extra_at : extra_at + 2 * heads], grad_flat, low(columns)], axis=1
    )
    grad_tiny = jnp.pad(grad_tiny, ((0, 0), (0, EXTRA - grad_tiny.shape[1])))
    pieces = scatter_sum((grad_proj, grad_out_t, grad_tiny), (extra_at, None, None), devices, 1)
    grad_normed_in = pair_scatter(grad_seq_in)
    out_width = w_output.shape[0]
    out_piece = pieces[:, extra_at : extra_at + out_width]
    tiny_piece = pieces[:, extra_at + out_width :]

    grad_inputs_norm, _ = norm_back(inputs, full_in, grad_normed_in)
    grad_tokens = grad_hidden + grad_inputs_norm

    sums = tiny_piece[:, 2 * heads + filter_cols : 2 * heads + filter_cols + 4].T
    sums = sums + pair_swap(sums)
    turn = lax.axis_index("tensor")
    take = lambda row, piece: lax.dynamic_slice_in_dim(sums[row], turn * piece, piece)
    n_heads = decay_log.shape[0]

    q_end, k_end = heads * 256, 2 * heads * 256
    v_end, g_end = k_end + heads * 512, k_end + 2 * heads * 512
    grad_filters = tiny_piece[:, 2 * heads : 2 * heads + filter_cols]
    grad_filters = grad_filters.T.reshape(tap_count, heads, 2 * piece_q + piece_v)
    return (
        result,
        grad_tokens,
        take(0, n_in),
        take(1, n_in),
        take(2, n_out),
        pieces[:, :q_end],
        pieces[:, q_end:k_end],
        pieces[:, k_end:v_end],
        pieces[:, v_end:g_end],
        tiny_piece[:, :heads],
        tiny_piece[:, heads : 2 * heads],
        grad_filters[..., :piece_q],
        grad_filters[..., piece_q : 2 * piece_q],
        grad_filters[..., 2 * piece_q :],
        sums[3, :n_heads],
        sums[3, n_heads : 2 * n_heads],
        out_piece.T,
        gate_piece.astype(f32),
        up_piece.astype(f32),
        down_piece.astype(f32).T,
    )


def solution(mesh):
    rows = P(("dp", "tensor"), None)
    spread = P(("dp", "tensor"))
    weight = P("dp", "tensor")
    filters = P(None, "tensor", "dp")
    turned = P("tensor", "dp")
    return jax.shard_map(
        local,
        mesh=mesh,
        in_specs=(rows, P("dp"), rows, spread, spread, spread)
        + (weight,) * 6
        + (filters,) * 3
        + (P(), P(), turned, weight, weight, turned),
        out_specs=(rows, rows, spread, spread, spread)
        + (weight,) * 6
        + (filters,) * 3
        + (P(), P(), turned, weight, weight, turned),
        check_vma=False,
    )
```

```python
import functools
import jax
import jax.numpy as jnp
from jax import lax
from jax.sharding import PartitionSpec as P
from jax.experimental import pallas as pl
from jax.experimental.pallas import tpu as pltpu

CH = 256
TILE = 64
PADR = 8
f32 = jnp.float32
bf16 = jnp.bfloat16


def mm(a, b, ca=1, cb=0):
    return lax.dot_general(
        a.astype(bf16), b.astype(bf16), (((ca,), (cb,)), ((), ())), preferred_element_type=f32
    )


def split2(a):
    high = a.astype(bf16)
    return high, (a - high.astype(f32)).astype(bf16)


def mm3(a, b, ca=1, cb=0):
    ah, al = split2(a)
    bh, bl = split2(b)
    return mm(ah, bh, ca, cb) + (mm(ah, bl, ca, cb) + mm(al, bh, ca, cb))


def iotas(n):
    return (
        lax.broadcasted_iota(jnp.int32, (n, n), 0),
        lax.broadcasted_iota(jnp.int32, (n, n), 1),
    )


def unit_lower_inverses(mats):
    n = mats[0].shape[0]
    rows, cols = iotas(n)
    eye = jnp.where(rows == cols, 1.0, 0.0).astype(f32)
    base = 8
    near = (rows // base) == (cols // base)
    powers = [jnp.where(near, a, 0.0) for a in mats]
    outs = [eye - p for p in powers]
    for _ in range(2):
        powers = [mm3(p, p) for p in powers]
        outs = [x + mm3(x, p) for x, p in zip(outs, powers)]
    size = base
    while size < n:
        wide = ((rows // (2 * size)) == (cols // (2 * size))) & ((rows // size) != (cols // size))
        halves = [mm3(jnp.where(wide, a, 0.0), x) for a, x in zip(mats, outs)]
        outs = [x - mm3(x, h) for x, h in zip(outs, halves)]
        size *= 2
    return outs


def sigm(v):
    return 1.0 / (1.0 + jnp.exp(-v))


def softplus(v):
    return jnp.maximum(v, 0.0) + jnp.log1p(jnp.exp(-jnp.abs(v)))


def pick(block, lane):
    lanes = lax.broadcasted_iota(jnp.int32, block.shape, 1)
    return jnp.sum(jnp.where(lanes == lane, block, 0.0), axis=1, keepdims=True)


def taps(ref):
    return [ref[i : i + 1, :] for i in range(4)]


def lanes_at(block, width):
    return pl.ds(pl.multiple_of(block * width, width), width)


def conv_rows(pad_ref, start, size, filt):
    total = None
    block = pad_ref[pl.ds(start, size + PADR), :]
    for i in range(4):
        term = filt[i] * block[PADR - 3 + i : PADR - 3 + i + size]
        total = term if total is None else total + term
    return total


def chunk_decay(logs, n):
    rows, cols = iotas(n)
    lower = jnp.where(rows >= cols, 1.0, 0.0).astype(f32)
    wide = jnp.broadcast_to(logs, (n, 128))
    h0 = wide.astype(bf16)
    r1 = wide - h0.astype(f32)
    h1 = r1.astype(bf16)
    h2 = (r1 - h1.astype(f32)).astype(bf16)
    col = (mm(lower, h0) + (mm(lower, h1) + mm(lower, h2)))[:, :1]
    row = (mm(h0, lower, 0, 1) + (mm(h1, lower, 0, 1) + mm(h2, lower, 0, 1)))[:1, :]
    return col, row


def suffix_sum(vals, n):
    rows, cols = iotas(n)
    upper = jnp.where(cols >= rows, 1.0, 0.0).astype(f32)
    wide = jnp.broadcast_to(vals, (n, 128))
    h0 = wide.astype(bf16)
    r1 = wide - h0.astype(f32)
    h1 = r1.astype(bf16)
    h2 = (r1 - h1.astype(f32)).astype(bf16)
    return (mm(upper, h0) + (mm(upper, h1) + mm(upper, h2)))[:, :1]


def load_padded(pad_ref, src_ref):
    pad_ref[0:PADR, :] = jnp.zeros((PADR, pad_ref.shape[1]), f32)
    pad_ref[PADR : PADR + src_ref.shape[0], :] = src_ref[...].astype(f32)


def fill_vectors(length, qpad, kpad, vpad, fq, fk, fv, qs, ks, vs):
    def body(t, _):
        start = pl.multiple_of(t * TILE, TILE)
        for pad, filt, dst, scale in ((qpad, fq, qs, 256 ** (-0.5)), (kpad, fk, ks, 1.0)):
            y = conv_rows(pad, start, TILE, filt)
            a = y * sigm(y)
            n = a * lax.rsqrt(jnp.sum(a * a, axis=1, keepdims=True) + 1e-06)
            dst[pl.ds(start, TILE), :] = (n * scale).astype(dst.dtype)
        y = conv_rows(vpad, start, TILE, fv)
        vs[pl.ds(start, TILE), :] = y * sigm(y)
        return 0

    lax.fori_loop(0, length // TILE, body, 0)


def beta_decay(h, heads, length, live_len, bd, log_ref, bias_ref):
    bp = pick(bd, h)
    dp = pick(bd, heads + h)
    live = (lax.broadcasted_iota(jnp.int32, (length, 1), 0) < live_len).astype(f32)
    rate = jnp.exp(pick(log_ref[0:1, :], h))
    sb = sigm(bp)
    zp = dp + pick(bias_ref[0:1, :], h)
    return sb, live, rate, zp


def fwd_kernel(
    heads, len_ref, q_ref, k_ref, v_ref, g_ref, bd_ref, fq_ref, fk_ref, fv_ref, log_ref, bias_ref,
    gain_ref, gated_ref, inv_ref, u_ref, mixed_ref, state_ref, qpad, kpad, vpad, qs, ks, vs,
):
    h = pl.program_id(0)
    length = q_ref.shape[0]
    chunks = length // CH
    load_padded(qpad, q_ref)
    load_padded(kpad, k_ref)
    load_padded(vpad, v_ref)
    fill_vectors(
        length, qpad, kpad, vpad, taps(fq_ref), taps(fk_ref), taps(fv_ref), qs, ks, vs
    )
    sb, live, rate, zp = beta_decay(h, heads, length, len_ref[0], bd_ref[...], log_ref, bias_ref)
    beta = sb * live
    logs = -rate * softplus(zp)
    rows, cols = iotas(CH)
    kept = []
    mats = []
    for n in range(chunks):
        part = slice(n * CH, (n + 1) * CH)
        col, row = chunk_decay(logs[part], CH)
        gaps = col - row
        decay = jnp.where(rows >= cols, jnp.exp(jnp.where(rows >= cols, gaps, 0.0)), 0.0)
        kf = ks[part, :]
        gram = mm3(kf, kf, 1, 1)
        mats.append(jnp.where(rows > cols, beta[part] * decay * gram, 0.0))
        kept.append((part, col, decay))
    inverses = unit_lower_inverses(mats)
    state = None
    for n in range(chunks):
        part, col, decay = kept[n]
        kf = ks[part, :]
        qf = qs[part, :]
        inv_ref[0, part, :] = inverses[n].astype(inv_ref.dtype)
        grow = jnp.exp(col)
        rhs = vs[part, :]
        if state is not None:
            rhs = rhs - grow * mm(kf, state)
        u = mm3(inverses[n], beta[part] * rhs)
        u_ref[part, :] = u.astype(u_ref.dtype)
        scores = mm(qf, kf, 1, 1) * decay
        out = mm(scores, u)
        if state is not None:
            out = out + grow * mm(qf, state)
        mixed_ref[part, :] = out
        if n + 1 < chunks:
            last = col[CH - 1 :, :]
            add = mm(kf * jnp.exp(last - col), u, 0, 0)
            state = add if state is None else jnp.exp(last) * state + add
            state_ref[0, n] = state
    gain = gain_ref[0:1, :]
    live_len = len_ref[0]

    def finish(t, _):
        start = pl.multiple_of(t * TILE, TILE)
        sl = pl.ds(start, TILE)
        m = mixed_ref[sl, :]
        gp = g_ref[sl, :].astype(f32)
        pos = start + lax.broadcasted_iota(jnp.int32, (TILE, 1), 0)
        alive = (pos < live_len).astype(f32)
        r = lax.rsqrt(jnp.mean(m * m, axis=1, keepdims=True) + 1e-05)
        gated_ref[sl, :] = (m * r * gain * (gp * sigm(gp)) * alive).astype(bf16)
        return 0

    lax.fori_loop(0, length // TILE, finish, 0)


def bwd_kernel(
    heads, len_ref, q_ref, k_ref, v_ref, g_ref, bd_ref, fq_ref, fk_ref, fv_ref, log_ref, bias_ref,
    gain_ref, inv_ref, u_ref, mixed_ref, state_ref, dg_ref,
    dpre_out, dfq_out, dfk_out, dfv_out, dgain_out, dsmall_out,
    qpad, kpad, vpad, qs, ks, vs, dos, dqs, dks, dvs, dbds,
):
    h = pl.program_id(0)
    length = q_ref.shape[0]
    chunks = length // CH
    load_padded(qpad, q_ref)
    load_padded(kpad, k_ref)
    load_padded(vpad, v_ref)
    fq, fk, fv = taps(fq_ref), taps(fk_ref), taps(fv_ref)
    fill_vectors(length, qpad, kpad, vpad, fq, fk, fv, qs, ks, vs)
    live_len = len_ref[0]
    gain = gain_ref[0:1, :]

    @pl.when(h == 0)
    def _():
        dgain_out[...] = jnp.zeros(dgain_out.shape, f32)
        dbds[...] = jnp.zeros(dbds.shape, f32)
        dsmall_out[...] = jnp.zeros(dsmall_out.shape, f32)

    def gate_back(t, acc):
        start = pl.multiple_of(t * TILE, TILE)
        sl = pl.ds(start, TILE)
        m = mixed_ref[sl, :]
        gp = g_ref[sl, :].astype(f32)
        pos = start + lax.broadcasted_iota(jnp.int32, (TILE, 1), 0)
        alive = (pos < live_len).astype(f32)
        r = lax.rsqrt(jnp.mean(m * m, axis=1, keepdims=True) + 1e-05)
        n = m * r
        t_ = dg_ref[sl, :].astype(f32) * alive
        s = sigm(gp)
        act = gp * s
        tn = t_ * n
        dpre_out[sl, lanes_at(2 * heads + h, 512)] = (
            tn * gain * (s + act * (1.0 - s))
        ).astype(bf16)
        dn = t_ * gain * act
        dos[sl, :] = r * (dn - n * jnp.mean(dn * n, axis=1, keepdims=True))
        return acc + jnp.sum((tn * act).reshape(TILE // 8, 8, tn.shape[1]), axis=0)

    dgain = lax.fori_loop(0, length // TILE, gate_back, jnp.zeros((8, gain.shape[1]), f32))
    dgain_out[...] += dgain

    sb, live, rate, zp = beta_decay(h, heads, length, live_len, bd_ref[...], log_ref, bias_ref)
    beta = sb * live
    sp = softplus(zp)
    logs = -rate * sp
    rows, cols = iotas(CH)
    incl = rows >= cols
    ones = jnp.ones((CH, 128), f32)
    dstate = None
    dbetas = [None] * chunks
    dlogs = [None] * chunks
    for n in reversed(range(chunks)):
        part = slice(n * CH, (n + 1) * CH)
        col, row = chunk_decay(logs[part], CH)
        gaps = col - row
        decay = jnp.where(incl, jnp.exp(jnp.where(incl, gaps, 0.0)), 0.0)
        grow = jnp.exp(col)
        last = col[CH - 1 :, :]
        kf = ks[part, :]
        qf = qs[part, :]
        u = u_ref[part, :].astype(f32)
        inv = inv_ref[0, part, :]
        do = dos[part, :]
        b = beta[part]
        gram = mm(kf, kf, 1, 1)
        strict_decay = jnp.where(rows > cols, decay, 0.0)
        scores = mm(qf, kf, 1, 1) * decay
        m_all = mm(do, u, 1, 1)
        du = mm(scores, do, 0, 0)
        tail = jnp.exp(last - col)
        if dstate is not None:
            kend = kf * tail
            du = du + mm(kend, dstate)
        dr = mm(inv, du, 0, 0)
        dvs[part, :] = b * dr
        da = mm(dr, u, 1, 1)
        da_dec = -da * strict_decay
        da_gram = da_dec * gram
        dbeta = jnp.sum(da_gram, axis=1, keepdims=True)
        msc = m_all * scores
        both = msc + b * da_gram
        rs = jnp.sum(both, axis=1, keepdims=True)
        both_h, both_l = split2(both)
        cs = (mm(both_h, ones, 0, 0) + mm(both_l, ones, 0, 0))[:, :1]
        dc = rs - cs
        dqk = m_all * decay
        dgram = b * da_dec
        dq = mm(dqk, kf)
        dk = mm(dqk, qf, 0, 0) + mm(dgram, kf) + mm(dgram, kf, 0, 0)
        rest = vs[part, :]
        dlast = None
        if n > 0:
            state = state_ref[0, n - 1]
            kst = mm(kf, state)
            qst = mm(qf, state)
            rest = rest - grow * kst
            dkst = -(b * grow) * dr
            dqst = grow * do
            dk = dk + mm(dkst, state, 1, 1)
            dq = dq + mm(dqst, state, 1, 1)
            dc = dc + jnp.sum(dkst * kst + dqst * qst, axis=1, keepdims=True)
            dprev = mm(kf, dkst, 0, 0) + mm(qf, dqst, 0, 0)
        dbetas[n] = dbeta + jnp.sum(dr * rest, axis=1, keepdims=True)
        if dstate is not None:
            dkend = mm(u, dstate, 1, 1)
            dk = dk + dkend * tail
            w = jnp.sum(dkend * kend, axis=1, keepdims=True)
            dc = dc - w
            dlast = jnp.sum(w, axis=0, keepdims=True)
            if n > 0:
                scale = jnp.exp(last)
                dprev = dprev + scale * dstate
                dlast = dlast + scale * jnp.sum(
                    jnp.sum(dstate * state, axis=1, keepdims=True), axis=0, keepdims=True
                )
        dlog = suffix_sum(dc, CH)
        if dlast is not None:
            dlog = dlog + dlast
        dlogs[n] = dlog
        dqs[part, :] = dq
        dks[part, :] = dk
        if n > 0:
            dstate = dprev
    dbeta = jnp.concatenate(dbetas, axis=0)
    dlog = jnp.concatenate(dlogs, axis=0)
    dbp = dbeta * live * sb * (1.0 - sb)
    dzp = -rate * dlog * sigm(zp)
    lanes = lax.broadcasted_iota(jnp.int32, (length, 128), 1)
    dbds[...] += jnp.where(lanes == h, dbp, 0.0) + jnp.where(lanes == heads + h, dzp, 0.0)

    @pl.when(h == heads - 1)
    def _():
        dpre_out[:, 12 * heads * 128 : (12 * heads + 1) * 128] = dbds[...].astype(bf16)

    small_lane = lax.broadcasted_iota(jnp.int32, (8, 128), 1)
    small_row = lax.broadcasted_iota(jnp.int32, (8, 128), 0)
    at_head = small_lane == h
    dsmall_out[...] += jnp.where(
        at_head & (small_row == 0), jnp.sum(dlog * logs, axis=0, keepdims=True), 0.0
    ) + jnp.where(at_head & (small_row == 1), jnp.sum(dzp, axis=0, keepdims=True), 0.0)

    def pre_back(t, _):
        start = pl.multiple_of(t * TILE, TILE)
        sl = pl.ds(start, TILE)
        for pad, filt, dref, scale in ((qpad, fq, dqs, 256 ** (-0.5)), (kpad, fk, dks, 1.0)):
            y = conv_rows(pad, start, TILE, filt)
            s = sigm(y)
            a = y * s
            r = lax.rsqrt(jnp.sum(a * a, axis=1, keepdims=True) + 1e-06)
            nn = a * r
            dn = dref[sl, :] * scale
            da_ = r * (dn - nn * jnp.sum(dn * nn, axis=1, keepdims=True))
            dref[sl, :] = da_ * (s + a * (1.0 - s))
        y = conv_rows(vpad, start, TILE, fv)
        s = sigm(y)
        dvs[sl, :] = dvs[sl, :] * (s + y * s * (1.0 - s))
        return 0

    lax.fori_loop(0, length // TILE, pre_back, 0)
    for dref in (dqs, dks, dvs):
        dref[length : length + PADR, :] = jnp.zeros((PADR, dref.shape[1]), f32)

    for pad, filt, dref, first, fout in (
        (qpad, fq, dqs, h, dfq_out),
        (kpad, fk, dks, heads + h, dfk_out),
        (vpad, fv, dvs, heads + h, dfv_out),
    ):
        width = dref.shape[1]

        def conv_back(t, accs, pad=pad, filt=filt, dref=dref, first=first, width=width):
            start = pl.multiple_of(t * TILE, TILE)
            dx = None
            new = []
            dys = dref[pl.ds(start, TILE + PADR), :]
            xs = pad[pl.ds(start, TILE + PADR), :]
            dy = dys[:TILE]
            for i in range(4):
                term = filt[i] * dys[3 - i : 3 - i + TILE]
                dx = term if dx is None else dx + term
                prod = dy * xs[PADR - 3 + i : PADR - 3 + i + TILE]
                new.append(accs[i] + jnp.sum(prod.reshape(TILE // 8, 8, width), axis=0))
            dpre_out[pl.ds(start, TILE), lanes_at(first, width)] = dx.astype(bf16)
            return tuple(new)

        accs = lax.fori_loop(
            0, length // TILE, conv_back, tuple(jnp.zeros((8, width), f32) for _ in range(4))
        )
        for i in range(4):
            fout[i : i + 1, :] = jnp.sum(accs[i], axis=0, keepdims=True)


def col_spec(length, width, first=0):
    return pl.BlockSpec((length, width), lambda h: (0, first + h))


def whole_spec(shape):
    return pl.BlockSpec(shape, lambda h: (0,) * len(shape))


def front_specs(length, heads):
    return [
        pl.BlockSpec(memory_space=pltpu.SMEM),
        col_spec(length, 256),
        col_spec(length, 256, heads),
        col_spec(length, 512, heads),
        col_spec(length, 512, 2 * heads),
        pl.BlockSpec((length, 128), lambda h: (0, 12 * heads)),
        col_spec(4, 256),
        col_spec(4, 256),
        col_spec(4, 512),
        whole_spec((1, 128)),
        whole_spec((1, 128)),
        whole_spec((1, 512)),
    ]


def mixer_forward(heads, lens, pre, fq, fk, fv, logs, bias, gain):
    length = pre.shape[0]
    chunks = length // CH
    kept = max(1, chunks - 1)
    return pl.pallas_call(
        functools.partial(fwd_kernel, heads),
        grid=(heads,),
        in_specs=front_specs(length, heads),
        out_specs=[
            col_spec(length, 512),
            pl.BlockSpec((1, length, CH), lambda h: (h, 0, 0)),
            col_spec(length, 512),
            col_spec(length, 512),
            pl.BlockSpec((1, kept, 256, 512), lambda h: (h, 0, 0, 0)),
        ],
        out_shape=[
            jax.ShapeDtypeStruct((length, heads * 512), bf16),
            jax.ShapeDtypeStruct((heads, length, CH), bf16),
            jax.ShapeDtypeStruct((length, heads * 512), bf16),
            jax.ShapeDtypeStruct((length, heads * 512), f32),
            jax.ShapeDtypeStruct((heads, kept, 256, 512), f32),
        ],
        scratch_shapes=[
            pltpu.VMEM((length + PADR, 256), f32),
            pltpu.VMEM((length + PADR, 256), f32),
            pltpu.VMEM((length + PADR, 512), f32),
            pltpu.VMEM((length, 256), f32),
            pltpu.VMEM((length, 256), f32),
            pltpu.VMEM((length, 512), f32),
        ],
        compiler_params=pltpu.CompilerParams(vmem_limit_bytes=50 * 1024 * 1024),
        name="mixer_forward",
    )(lens, pre, pre, pre, pre, pre, fq, fk, fv, logs, bias, gain)


def mixer_backward(heads, lens, pre, fq, fk, fv, logs, bias, gain, saved, dgated):
    length = pre.shape[0]
    chunks = length // CH
    kept = max(1, chunks - 1)
    inv, u, mixed, states = saved
    return pl.pallas_call(
        functools.partial(bwd_kernel, heads),
        grid=(heads,),
        in_specs=front_specs(length, heads)
        + [
            pl.BlockSpec((1, length, CH), lambda h: (h, 0, 0)),
            col_spec(length, 512),
            col_spec(length, 512),
            pl.BlockSpec((1, kept, 256, 512), lambda h: (h, 0, 0, 0)),
            col_spec(length, 512),
        ],
        out_specs=[
            whole_spec((length, pre.shape[1])),
            col_spec(4, 256), col_spec(4, 256), col_spec(4, 512),
            whole_spec((8, 512)), whole_spec((8, 128)),
        ],
        out_shape=[
            jax.ShapeDtypeStruct(pre.shape, bf16),
            jax.ShapeDtypeStruct((4, heads * 256), f32),
            jax.ShapeDtypeStruct((4, heads * 256), f32),
            jax.ShapeDtypeStruct((4, heads * 512), f32),
            jax.ShapeDtypeStruct((8, 512), f32),
            jax.ShapeDtypeStruct((8, 128), f32),
        ],
        scratch_shapes=[
            pltpu.VMEM((length + PADR, 256), f32),
            pltpu.VMEM((length + PADR, 256), f32),
            pltpu.VMEM((length + PADR, 512), f32),
            pltpu.VMEM((length, 256), f32),
            pltpu.VMEM((length, 256), f32),
            pltpu.VMEM((length, 512), f32),
            pltpu.VMEM((length, 512), f32),
            pltpu.VMEM((length + PADR, 256), f32),
            pltpu.VMEM((length + PADR, 256), f32),
            pltpu.VMEM((length + PADR, 512), f32),
            pltpu.VMEM((length, 128), f32),
        ],
        compiler_params=pltpu.CompilerParams(vmem_limit_bytes=50 * 1024 * 1024),
        name="mixer_backward",
    )(lens, pre, pre, pre, pre, pre, fq, fk, fv, logs, bias, gain, inv, u, mixed, states, dgated)


MESH = pl.DeviceIdType.MESH


def column_chunks(widths, size, layers):
    size = size * max(1, layers // 4)
    out = []
    for a, width in enumerate(widths):
        units = width // 128
        count = max(1, -(-width // size))
        lo = 0
        for i in range(count):
            hi = units * (i + 1) // count
            out.append((a, lo * 128, (hi - lo) * 128))
            lo = hi
    return out


def placement():
    spot = lax.axis_index("dp")
    return spot, lax.rem(spot, 2), lax.rem(lax.div(spot, 2), 2), lax.div(spot, 4)


def greet(partners):
    barrier = pltpu.get_barrier_semaphore()
    for partner in partners:
        pl.semaphore_signal(barrier, inc=1, device_id={"dp": partner}, device_id_type=MESH)
    pl.semaphore_wait(barrier, len(partners))


def remote(src, dst, send, recv, target):
    return pltpu.make_async_remote_copy(
        src_ref=src, dst_ref=dst, send_sem=send, recv_sem=recv,
        device_id={"dp": target}, device_id_type=MESH,
    )


def gather_kernel(layers, chunks, count, pairs, *refs):
    srcs, outs = refs[: count + pairs], refs[count + pairs : 2 * (count + pairs)]
    own_sem, us, ur, ds, dr, ys, yr, cs, cr, ps, pr, pair_sem = refs[2 * (count + pairs) :]
    rows = srcs[0].shape[0]
    spot, core, side, layer = placement()
    turn = lax.axis_index("tensor")
    at = lambda z, y, c: 4 * z + 2 * y + c
    y_to, c_to = at(layer, 1 - side, core), at(layer, side, 1 - core)
    has_up, has_down = layer < layers - 1, layer > 0
    barrier = pltpu.get_barrier_semaphore()
    around = [4 * lax.rem(layer + s, layers) + 2 * side + core for s in (1, layers - 1)]
    for partner in [y_to, c_to] + around:
        pl.semaphore_signal(barrier, inc=1, device_id={"dp": partner}, device_id_type=MESH)
    pl.semaphore_signal(barrier, inc=1, device_id={"tensor": 1 - turn}, device_id_type=MESH)
    pl.semaphore_wait(barrier, 5)

    def place(j, origin):
        a, lo, width, _ = chunks[j]
        start = pl.multiple_of(origin * rows, rows)
        return outs[a].at[pl.ds(start, rows), lo : lo + width]

    def own(j):
        a, lo, width, _ = chunks[j]
        return srcs[a].at[:, lo : lo + width]

    def up_copy(j, k, half, origin, src):
        i = 2 * k + half
        return remote(src, place(j, origin), us.at[j, i], ur.at[j, i], spot + 4)

    def down_copy(j, k, half, origin, src):
        i = 2 * k + half
        return remote(src, place(j, origin), ds.at[j, i], dr.at[j, i], spot - 4)

    def y_copy(j, slot, origin, src):
        return remote(src, place(j, origin), ys.at[j, slot], yr.at[j, slot], y_to)

    def c_copy(j, slot, origin, src):
        return remote(src, place(j, origin), cs.at[j, slot], cr.at[j, slot], c_to)

    number = len(chunks)
    narrow = [j for j in range(number) if not chunks[j][3]]
    early = [j for j in range(number) if chunks[j][3]]
    keep = []
    for p in range(pairs):
        half_rows = srcs[count + p].shape[0]
        spot_rows = pl.ds(pl.multiple_of(turn * half_rows, half_rows), half_rows)
        copy = pltpu.make_async_remote_copy(
            src_ref=srcs[count + p], dst_ref=outs[count + p].at[spot_rows, :],
            send_sem=ps.at[p], recv_sem=pr.at[p],
            device_id={"tensor": 1 - turn}, device_id_type=MESH,
        )
        copy.start()
        local_copy = pltpu.make_async_copy(
            srcs[count + p], outs[count + p].at[spot_rows, :], pair_sem.at[p]
        )
        local_copy.start()
        keep.append((copy, local_copy))

    def send_z(j, half, origin, src):
        @pl.when(has_up)
        def _():
            up_copy(j, 0, half, origin, src).start()

        @pl.when(has_down)
        def _():
            down_copy(j, 0, half, origin, src).start()

    locals_ = []
    for j in early + narrow:
        y_copy(j, 0, spot, own(j)).start()
        send_z(j, 0, spot, own(j))
        c_copy(j, 0, spot, own(j)).start()
        copy = pltpu.make_async_copy(own(j), place(j, spot), own_sem.at[j])
        copy.start()
        locals_.append(copy)
    across = at(layer, 1 - side, core)

    def take_z(j, k, half):
        there = lax.rem(side + half, 2)
        for sign, fits, more, copy in (
            (-1, layer >= k + 1, has_up, up_copy),
            (1, layer + k + 1 < layers, has_down, down_copy),
        ):

            @pl.when(fits)
            def _(sign=sign, more=more, copy=copy):
                origin = at(layer + sign * (k + 1), there, core)
                here = place(j, origin)
                copy(j, k, half, origin, here).wait_recv()

                @pl.when(more)
                def _():
                    copy(j, k + 1, half, origin, here).start()

                slot = 2 * k + (1 if sign < 0 else 2)
                if not chunks[j][3]:
                    y_copy(j, slot, origin, here).start()
                c_copy(j, slot if half == 0 else slot + 2 * layers - 1, origin, here).start()

    def take_y(j, k):
        slots = [(0, None, None)] if k == 0 else [
            (2 * k - 1, layer >= k, -1), (2 * k, layer + k < layers, 1)
        ]
        for slot, fits, sign in slots:
            shift = 0 if sign is None else sign * k

            def body(slot=slot, shift=shift):
                origin = at(layer + shift, 1 - side, core)
                here = place(j, origin)
                y_copy(j, slot, origin, here).wait_recv()
                c_copy(j, 2 * layers - 1 + slot, origin, here).start()

            if fits is None:
                body()
            else:
                pl.when(fits)(body)

    for j in early:
        y_copy(j, 0, across, own(j)).wait_recv()
        send_z(j, 1, across, place(j, across))
        c_copy(j, 2 * layers - 1, across, place(j, across)).start()
    for k in range(layers):
        if k < layers - 1:
            for j in early:
                for half in range(2):
                    take_z(j, k, half)
            for j in narrow:
                take_z(j, k, 0)
        if k > 0:
            for j in narrow:
                take_y(j, k - 1)
    for j in narrow:
        take_y(j, layers - 1)

    for copy, local_copy in keep:
        local_copy.wait()
        copy.wait()
    for copy in locals_:
        copy.wait()
    for j in range(number):
        wide = chunks[j][3]
        me = own(j)
        for half in range(2 if wide else 1):
            for k in range(layers - 1):

                @pl.when(has_up & (layer >= k))
                def _(k=k, half=half):
                    up_copy(j, k, half, spot, me).wait_send()

                @pl.when(has_down & (layer + k < layers))
                def _(k=k, half=half):
                    down_copy(j, k, half, spot, me).wait_send()

        def settle(slot, shift):
            if slot == 0 or not wide:
                y_copy(j, slot, spot, me).wait_send()
            for half in range(2):
                origin = at(layer + shift, lax.rem(side + half, 2), 1 - core)
                c_copy(j, slot + half * (2 * layers - 1), origin, place(j, origin)).wait()

        settle(0, 0)
        for k in range(1, layers):
            pl.when(layer >= k)(functools.partial(settle, 2 * k - 1, -k))
            pl.when(layer + k < layers)(functools.partial(settle, 2 * k, k))


def mark_early(chunks, share):
    total = sum(c[2] for c in chunks)
    marked, done = [], 0
    for c in chunks:
        early = done + c[2] <= share * total + 64
        done += c[2] if early else 0
        marked.append(c + (early,))
    return marked


def gather_all(shards, pairs, devices, ident, size=512, share=1 / 6):
    rows = shards[0].shape[0]
    layers = devices // 4
    chunks = mark_early(column_chunks([s.shape[1] for s in shards], size, layers), share)
    n = len(chunks)
    sem = lambda *shape: pltpu.SemaphoreType.DMA(shape)
    z_slots, slots = 2 * layers, 2 * layers - 1
    arrays = tuple(shards) + tuple(pairs)
    return pl.pallas_call(
        functools.partial(gather_kernel, layers, chunks, len(shards), len(pairs)),
        in_specs=[pl.BlockSpec(memory_space=pl.ANY)] * len(arrays),
        out_specs=[pl.BlockSpec(memory_space=pl.ANY)] * len(arrays),
        out_shape=[jax.ShapeDtypeStruct((devices * rows, s.shape[1]), s.dtype) for s in shards]
        + [jax.ShapeDtypeStruct((2 * p.shape[0], p.shape[1]), p.dtype) for p in pairs],
        scratch_shapes=[
            sem(n), sem(n, z_slots), sem(n, z_slots), sem(n, z_slots), sem(n, z_slots),
            sem(n, slots), sem(n, slots), sem(n, 2 * slots), sem(n, 2 * slots),
            sem(max(1, len(pairs))), sem(max(1, len(pairs))), sem(max(1, len(pairs))),
        ],
        compiler_params=pltpu.CompilerParams(collective_id=ident, has_side_effects=True),
        name="gather_rows",
    )(*arrays)


def scatter_kernel(layers, chunks, count, *refs):
    srcs, out = refs[:count], refs[count]
    stage, buf1, buf2, buf3, own_sem, cs, cr, ys, yr, zs, zr = refs[count + 1 :]
    rows = out.shape[0]
    spot, core, side, layer = placement()
    at = lambda z, y, c: 4 * lax.rem(z + layers, layers) + 2 * y + c
    z_to = [at(layer + k, side, core) for k in range(1, layers)]
    y_to, c_to = at(layer, 1 - side, core), at(layer, side, 1 - core)
    greet(z_to + [y_to, c_to])
    number = len(chunks)
    firsts = []
    total = 0
    for a, lo, width in chunks:
        firsts.append(total)
        total += width

    def cols(j):
        return slice(firsts[j], firsts[j] + chunks[j][2])

    def c_copy(j):
        a, lo, width = chunks[j]
        return remote(
            srcs[a].at[:, 1 - core, :, lo : lo + width], buf1.at[:, :, cols(j)],
            cs.at[j], cr.at[j], c_to,
        )

    def own_copy(j):
        a, lo, width = chunks[j]
        return pltpu.make_async_copy(
            srcs[a].at[:, core, :, lo : lo + width],
            stage.at[j % 2, :, :, 0:width], own_sem.at[j],
        )

    def y_copy(j, m):
        block = 2 * lax.rem(layer + m, layers) + 1 - side
        return remote(
            buf1.at[block, :, cols(j)], buf2.at[m, :, cols(j)], ys.at[j, m], yr.at[j, m], y_to
        )

    def z_copy(j, k):
        return remote(
            buf2.at[k, :, cols(j)], buf3.at[k - 1, :, cols(j)], zs.at[j, k - 1], zr.at[j, k - 1],
            z_to[k - 1],
        )

    for j in range(number):
        c_copy(j).start()
    for j in range(min(2, number)):
        own_copy(j).start()

    def first(j):
        width = chunks[j][2]
        own_copy(j).wait()
        c_copy(j).wait_recv()

        def body(b, _):
            mine = stage[j % 2, b, :, 0:width].astype(f32)
            buf1[b, :, cols(j)] = (buf1[b, :, cols(j)].astype(f32) + mine).astype(bf16)
            return 0

        lax.fori_loop(0, 2 * layers, body, 0)
        for m in list(range(1, layers)) + [0]:
            y_copy(j, m).start()
        if j + 2 < number:
            own_copy(j + 2).start()

    def second(j):
        for m in list(range(1, layers)) + [0]:
            y_copy(j, m).wait_recv()
            block = 2 * lax.rem(layer + m, layers) + side
            mine = buf1[block, :, cols(j)].astype(f32)
            buf2[m, :, cols(j)] = (buf2[m, :, cols(j)].astype(f32) + mine).astype(bf16)
            if m:
                z_copy(j, m).start()

    def third(j):
        total = buf2[0, :, cols(j)].astype(f32)
        for k in range(1, layers):
            z_copy(j, k).wait_recv()
            total = total + buf3[k - 1, :, cols(j)].astype(f32)
        out[:, cols(j)] = total

    for j in range(number + 4):
        if j < number:
            first(j)
        if 0 <= j - 2 < number:
            second(j - 2)
        if 0 <= j - 4 < number:
            third(j - 4)
    for j in range(number):
        c_copy(j).wait_send()
        for m in range(layers):
            y_copy(j, m).wait_send()
        for k in range(1, layers):
            z_copy(j, k).wait_send()


def scatter_sum(parts, widths, devices, ident, size=512):
    widths = [w or p.shape[1] for w, p in zip(widths, parts)]
    rows = parts[0].shape[0] // devices
    layers = devices // 4
    chunks = column_chunks(widths, size, layers)
    n = len(chunks)
    width = sum(widths)
    widest = max(c[2] for c in chunks)
    sem = lambda *shape: pltpu.SemaphoreType.DMA(shape)
    return pl.pallas_call(
        functools.partial(scatter_kernel, layers, chunks, len(parts)),
        in_specs=[pl.BlockSpec(memory_space=pl.ANY)] * len(parts),
        out_specs=pl.BlockSpec(memory_space=pltpu.VMEM),
        out_shape=jax.ShapeDtypeStruct((rows, width), f32),
        scratch_shapes=[
            pltpu.VMEM((2, 2 * layers, rows, widest), bf16),
            pltpu.VMEM((2 * layers, rows, width), bf16),
            pltpu.VMEM((layers, rows, width), bf16),
            pltpu.VMEM((layers - 1, rows, width), bf16),
            sem(n), sem(n), sem(n), sem(n, layers), sem(n, layers),
            sem(n, layers - 1), sem(n, layers - 1),
        ],
        compiler_params=pltpu.CompilerParams(
            collective_id=ident, has_side_effects=True, vmem_limit_bytes=52 * 1024 * 1024
        ),
        name="scatter_sum",
    )(*[p.reshape(devices // 2, 2, rows, p.shape[1]) for p in parts])


EXTRA = 128


def rms_scale(values):
    return lax.rsqrt(jnp.mean(values * values, axis=-1, keepdims=True) + 1e-05)


def norm_back(values, gain, grad_normed):
    scale = rms_scale(values)
    unit_vals = values * scale
    grad_unit = grad_normed * gain
    grad_values = scale * (
        grad_unit - unit_vals * jnp.mean(grad_unit * unit_vals, axis=-1, keepdims=True)
    )
    return (grad_values, jnp.sum(grad_normed * unit_vals, axis=0))


def pair_swap(values):
    return lax.ppermute(values, "tensor", [(0, 1), (1, 0)])


def pair_gather(values):
    other = pair_swap(values)
    first = lax.axis_index("tensor") == 0
    return jnp.concatenate(
        [jnp.where(first, values, other), jnp.where(first, other, values)], axis=0
    )


def pair_halves(parts):
    rows = parts.shape[0] // 2
    mine = lax.axis_index("tensor") * rows
    kept = lax.dynamic_slice_in_dim(parts, mine, rows)
    sent = lax.dynamic_slice_in_dim(parts, rows - mine, rows).astype(bf16)
    return kept, sent


def pair_scatter(parts):
    kept, sent = pair_halves(parts)
    return kept + pair_swap(sent).astype(f32)


def dot(a, b, ca=1, cb=0):
    return lax.dot_general(a, b, (((ca,), (cb,)), ((), ())), preferred_element_type=f32)


def high_low(values):
    high = lax.reduce_precision(values, 8, 7)
    return jnp.stack([high, values - high], axis=1).astype(bf16)


def gather_rows(values):
    return lax.all_gather(values, "dp", axis=0, tiled=True)


def scatter_rows(values):
    return lax.psum_scatter(values, "dp", scatter_dimension=0, tiled=True)


def pack_filters(fq, fk, fv, rows):
    flat = jnp.concatenate([fq, fk, fv], axis=2).reshape(-1)
    return flat.reshape(-1, rows).T


def local(
    tokens,
    lengths,
    cotangent,
    gain_in,
    gain_ffn,
    gain_out,
    w_query,
    w_key,
    w_value,
    w_gate,
    w_beta,
    w_decay,
    conv_query,
    conv_key,
    conv_value,
    decay_log,
    decay_bias,
    w_output,
    w_ffn_gate,
    w_ffn_up,
    w_ffn_down,
):
    heads = w_beta.shape[1]
    rows = w_query.shape[0]
    devices = lax.axis_size("dp")
    low = lambda v: v.astype(bf16)
    filters = pack_filters(conv_query, conv_key, conv_value, rows)
    filter_cols = filters.shape[1]
    gains = pair_gather(jnp.concatenate([gain_in, gain_ffn, gain_out])[None])
    n_in, n_out = gain_in.shape[0], gain_out.shape[0]
    pair_out = jnp.pad(gains[:, 2 * n_in :].reshape(-1), (0, rows - 2 * n_out))
    small = jnp.concatenate(
        [
            low(jnp.concatenate([w_beta, w_decay, filters], axis=1)),
            high_low(gains[:, :n_in].reshape(-1)),
            high_low(gains[:, n_in : 2 * n_in].reshape(-1)),
            high_low(pair_out),
        ],
        axis=1,
    )
    small = jnp.pad(small, ((0, 0), (0, EXTRA - small.shape[1])))
    proj_shard = jnp.concatenate(
        [low(w_query), low(w_key), low(w_value), low(w_gate), small], axis=1
    )
    proj, out_t, seq_x, seq_cot = gather_all(
        (proj_shard, low(w_output).T), (tokens, cotangent), devices, 0
    )
    extra_at = 12 * heads * 128
    gain_at = extra_at + 2 * heads + filter_cols
    sides = proj[:, gain_at : gain_at + 6].astype(f32)
    sides = sides[:, 0::2] + sides[:, 1::2]
    full_in, full_ffn = sides[:, 0], sides[:, 1]
    full_out = sides[:, 2].reshape(devices, rows)[:, : 2 * n_out].reshape(1, -1)
    gate_weight = gather_rows(low(w_ffn_gate))
    up_weight = gather_rows(low(w_ffn_up))
    down_t = gather_rows(low(w_ffn_down).T)

    tap_count = conv_query.shape[0]
    piece_q, piece_v = conv_query.shape[2], conv_value.shape[2]
    flat = proj[:, extra_at + 2 * heads : gain_at]
    flat = flat.reshape(devices, rows, filter_cols).transpose(0, 2, 1)
    flat = flat.reshape(devices, tap_count, heads, 2 * piece_q + piece_v).astype(f32)
    flat = flat.transpose(1, 2, 0, 3)
    filt_q = flat[..., :piece_q].reshape(tap_count, -1)
    filt_k = flat[..., piece_q : 2 * piece_q].reshape(tap_count, -1)
    filt_v = flat[..., 2 * piece_q :].reshape(tap_count, -1)

    head_start = lax.axis_index("tensor") * heads
    lane_pad = lambda v: jnp.pad(
        lax.dynamic_slice_in_dim(v, head_start, heads), (0, 128 - heads)
    ).reshape(1, 128)
    local_log, local_bias = lane_pad(decay_log), lane_pad(decay_bias)

    inputs = tokens.astype(f32)
    seq_inputs = seq_x.astype(f32)
    seq_unit = seq_inputs * rms_scale(seq_inputs)
    seq_in = low(seq_unit * full_in)
    pre = dot(seq_in, proj)
    mixer_args = (heads, lengths, pre, filt_q, filt_k, filt_v, local_log, local_bias, full_out)
    gated, *saved = mixer_forward(*mixer_args)
    hidden = inputs + pair_scatter(dot(gated, out_t, 1, 1))
    normed_ffn = low(hidden * rms_scale(hidden) * full_ffn)
    seq_ffn = pair_gather(normed_ffn)

    gate_act = dot(seq_ffn, gate_weight)
    up_act = dot(seq_ffn, up_weight)
    sigmoid_gate = jax.nn.sigmoid(gate_act)
    silu_gate = gate_act * sigmoid_gate
    inner = low(silu_gate * up_act)
    grad_inner = dot(seq_cot, down_t)
    grad_gate_act = low(
        grad_inner * up_act * sigmoid_gate * (1.0 + gate_act * (1.0 - sigmoid_gate))
    )
    grad_up_act = low(grad_inner * silu_gate)
    grad_down = low(dot(seq_cot, inner, 0, 0))
    grad_gate_act, grad_up_act, grad_down = lax.optimization_barrier(
        (grad_gate_act, grad_up_act, grad_down)
    )
    down_piece = scatter_rows(grad_down)
    grad_seq_ffn = dot(grad_gate_act, gate_weight, 1, 1) + dot(grad_up_act, up_weight, 1, 1)
    kept_ffn, sent_ffn = pair_halves(grad_seq_ffn)
    sent_ffn, grad_gate_act, grad_up_act, inner = lax.optimization_barrier(
        (sent_ffn, grad_gate_act, grad_up_act, inner)
    )
    grad_normed_ffn = kept_ffn + pair_swap(sent_ffn).astype(f32)
    grad_gate_w = low(dot(seq_ffn, grad_gate_act, 0, 0))
    grad_up_w = low(dot(seq_ffn, grad_up_act, 0, 0))
    gate_piece = scatter_rows(grad_gate_w)
    kept_out, sent_out = pair_halves(dot(inner, down_t, 1, 1))
    grad_hidden_norm, grad_gain_ffn = norm_back(hidden, full_ffn, grad_normed_ffn)
    grad_hidden = cotangent.astype(f32) + grad_hidden_norm
    seq_grad_branch = pair_gather(low(grad_hidden))
    seq_grad_branch, sent_out = lax.optimization_barrier((seq_grad_branch, sent_out))
    come_out = pair_swap(sent_out)

    grad_gated = dot(seq_grad_branch, out_t)
    grad_pre, grad_fq, grad_fk, grad_fv, grad_gain_out, grad_small = mixer_backward(
        *mixer_args, saved, low(grad_gated)
    )
    grad_pre, come_out = lax.optimization_barrier((grad_pre, come_out))
    result = low(hidden + kept_out + come_out.astype(f32))
    grad_seq_in = dot(grad_pre, proj, 1, 1)
    kept_in, sent_in = pair_halves(grad_seq_in)
    sent_in, grad_pre, gated = lax.optimization_barrier((sent_in, grad_pre, gated))
    come_in = pair_swap(sent_in)
    grad_proj = low(dot(seq_in, grad_pre, 0, 0))
    grad_out_t = low(dot(seq_grad_branch, gated, 0, 0))
    come_in, grad_proj, grad_out_t = lax.optimization_barrier((come_in, grad_proj, grad_out_t))
    by_device = lambda g, piece: g.reshape(tap_count, heads, devices, piece)
    grad_flat = jnp.concatenate(
        [by_device(grad_fq, piece_q), by_device(grad_fk, piece_q), by_device(grad_fv, piece_v)],
        axis=3,
    ).transpose(2, 0, 1, 3)
    grad_flat = grad_flat.reshape(devices, filter_cols, rows).transpose(0, 2, 1)
    grad_flat = low(grad_flat.reshape(devices * rows, filter_cols))
    spread = lambda v: lax.dynamic_update_slice(jnp.zeros_like(decay_log), v, (head_start,))
    grad_decay = jnp.concatenate([spread(grad_small[0, :heads]), spread(grad_small[1, :heads])])
    by_rows = lambda v: jnp.pad(v, ((0, 0), (0, rows - v.shape[1]))).reshape(-1)
    columns = jnp.stack(
        [
            jnp.sum(grad_seq_in * seq_unit, axis=0),
            grad_gain_ffn,
            by_rows(jnp.sum(grad_gain_out, axis=0).reshape(devices, -1)),
            by_rows(jnp.broadcast_to(grad_decay, (devices,) + grad_decay.shape)),
        ],
        axis=1,
    )
    grad_tiny = jnp.concatenate(
        [grad_proj[:, extra_at : extra_at + 2 * heads], grad_flat, low(columns)], axis=1
    )
    grad_tiny = jnp.pad(grad_tiny, ((0, 0), (0, EXTRA - grad_tiny.shape[1])))
    pieces = scatter_sum(
        (grad_up_w, grad_proj, grad_out_t, grad_tiny), (None, extra_at, None, None), devices, 1
    )
    ffn_width = grad_up_w.shape[1]
    up_piece, pieces = pieces[:, :ffn_width], pieces[:, ffn_width:]
    grad_normed_in = kept_in + come_in.astype(f32)
    out_width = w_output.shape[0]
    out_piece = pieces[:, extra_at : extra_at + out_width]
    tiny_piece = pieces[:, extra_at + out_width :]

    grad_inputs_norm, _ = norm_back(inputs, full_in, grad_normed_in)
    grad_tokens = grad_hidden + grad_inputs_norm

    sums = tiny_piece[:, 2 * heads + filter_cols : 2 * heads + filter_cols + 4].T
    sums = sums + pair_swap(sums)
    turn = lax.axis_index("tensor")
    take = lambda row, piece: lax.dynamic_slice_in_dim(sums[row], turn * piece, piece)
    n_heads = decay_log.shape[0]

    q_end, k_end = heads * 256, 2 * heads * 256
    v_end, g_end = k_end + heads * 512, k_end + 2 * heads * 512
    grad_filters = tiny_piece[:, 2 * heads : 2 * heads + filter_cols]
    grad_filters = grad_filters.T.reshape(tap_count, heads, 2 * piece_q + piece_v)
    return (
        result,
        grad_tokens,
        take(0, n_in),
        take(1, n_in),
        take(2, n_out),
        pieces[:, :q_end],
        pieces[:, q_end:k_end],
        pieces[:, k_end:v_end],
        pieces[:, v_end:g_end],
        tiny_piece[:, :heads],
        tiny_piece[:, heads : 2 * heads],
        grad_filters[..., :piece_q],
        grad_filters[..., piece_q : 2 * piece_q],
        grad_filters[..., 2 * piece_q :],
        sums[3, :n_heads],
        sums[3, n_heads : 2 * n_heads],
        out_piece.T,
        gate_piece.astype(f32),
        up_piece,
        down_piece.astype(f32).T,
    )


def solution(mesh):
    rows = P(("dp", "tensor"), None)
    spread = P(("dp", "tensor"))
    weight = P("dp", "tensor")
    filters = P(None, "tensor", "dp")
    turned = P("tensor", "dp")
    return jax.shard_map(
        local,
        mesh=mesh,
        in_specs=(rows, P("dp"), rows, spread, spread, spread)
        + (weight,) * 6
        + (filters,) * 3
        + (P(), P(), turned, weight, weight, turned),
        out_specs=(rows, rows, spread, spread, spread)
        + (weight,) * 6
        + (filters,) * 3
        + (P(), P(), turned, weight, weight, turned),
        check_vma=False,
    )
```

```python
import functools
import jax
import jax.numpy as jnp
from jax import lax
from jax.sharding import PartitionSpec as P
from jax.experimental import pallas as pl
from jax.experimental.pallas import tpu as pltpu

CH = 256
TILE = 64
PADR = 8
f32 = jnp.float32
bf16 = jnp.bfloat16


def mm(a, b, ca=1, cb=0):
    return lax.dot_general(
        a.astype(bf16), b.astype(bf16), (((ca,), (cb,)), ((), ())), preferred_element_type=f32
    )


def split2(a):
    high = a.astype(bf16)
    return high, (a - high.astype(f32)).astype(bf16)


def mm3(a, b, ca=1, cb=0):
    ah, al = split2(a)
    bh, bl = split2(b)
    return mm(ah, bh, ca, cb) + (mm(ah, bl, ca, cb) + mm(al, bh, ca, cb))


def iotas(n):
    return (
        lax.broadcasted_iota(jnp.int32, (n, n), 0),
        lax.broadcasted_iota(jnp.int32, (n, n), 1),
    )


def unit_lower_inverses(mats):
    n = mats[0].shape[0]
    rows, cols = iotas(n)
    eye = jnp.where(rows == cols, 1.0, 0.0).astype(f32)
    base = 8
    near = (rows // base) == (cols // base)
    powers = [jnp.where(near, a, 0.0) for a in mats]
    outs = [eye - p for p in powers]
    for _ in range(2):
        powers = [mm3(p, p) for p in powers]
        outs = [x + mm3(x, p) for x, p in zip(outs, powers)]
    size = base
    while size < n:
        wide = ((rows // (2 * size)) == (cols // (2 * size))) & ((rows // size) != (cols // size))
        halves = [mm3(jnp.where(wide, a, 0.0), x) for a, x in zip(mats, outs)]
        outs = [x - mm3(x, h) for x, h in zip(outs, halves)]
        size *= 2
    return outs


def sigm(v):
    return 1.0 / (1.0 + jnp.exp(-v))


def softplus(v):
    return jnp.maximum(v, 0.0) + jnp.log1p(jnp.exp(-jnp.abs(v)))


def pick(block, lane):
    lanes = lax.broadcasted_iota(jnp.int32, block.shape, 1)
    return jnp.sum(jnp.where(lanes == lane, block, 0.0), axis=1, keepdims=True)


def taps(ref):
    return [ref[i : i + 1, :] for i in range(4)]


def lanes_at(block, width):
    return pl.ds(pl.multiple_of(block * width, width), width)


def conv_rows(pad_ref, start, size, filt):
    total = None
    block = pad_ref[pl.ds(start, size + PADR), :]
    for i in range(4):
        term = filt[i] * block[PADR - 3 + i : PADR - 3 + i + size]
        total = term if total is None else total + term
    return total


def chunk_decay(logs, n):
    rows, cols = iotas(n)
    lower = jnp.where(rows >= cols, 1.0, 0.0).astype(f32)
    wide = jnp.broadcast_to(logs, (n, 128))
    h0 = wide.astype(bf16)
    r1 = wide - h0.astype(f32)
    h1 = r1.astype(bf16)
    h2 = (r1 - h1.astype(f32)).astype(bf16)
    col = (mm(lower, h0) + (mm(lower, h1) + mm(lower, h2)))[:, :1]
    row = (mm(h0, lower, 0, 1) + (mm(h1, lower, 0, 1) + mm(h2, lower, 0, 1)))[:1, :]
    return col, row


def suffix_sum(vals, n):
    rows, cols = iotas(n)
    upper = jnp.where(cols >= rows, 1.0, 0.0).astype(f32)
    wide = jnp.broadcast_to(vals, (n, 128))
    h0 = wide.astype(bf16)
    r1 = wide - h0.astype(f32)
    h1 = r1.astype(bf16)
    h2 = (r1 - h1.astype(f32)).astype(bf16)
    return (mm(upper, h0) + (mm(upper, h1) + mm(upper, h2)))[:, :1]


def load_padded(pad_ref, src_ref):
    pad_ref[0:PADR, :] = jnp.zeros((PADR, pad_ref.shape[1]), f32)
    pad_ref[PADR : PADR + src_ref.shape[0], :] = src_ref[...].astype(f32)


def fill_vectors(length, qpad, kpad, vpad, fq, fk, fv, qs, ks, vs):
    def body(t, _):
        start = pl.multiple_of(t * TILE, TILE)
        for pad, filt, dst, scale in ((qpad, fq, qs, 256 ** (-0.5)), (kpad, fk, ks, 1.0)):
            y = conv_rows(pad, start, TILE, filt)
            a = y * sigm(y)
            n = a * lax.rsqrt(jnp.sum(a * a, axis=1, keepdims=True) + 1e-06)
            dst[pl.ds(start, TILE), :] = (n * scale).astype(dst.dtype)
        y = conv_rows(vpad, start, TILE, fv)
        vs[pl.ds(start, TILE), :] = y * sigm(y)
        return 0

    lax.fori_loop(0, length // TILE, body, 0)


def beta_decay(h, heads, length, live_len, bd, log_ref, bias_ref):
    bp = pick(bd, h)
    dp = pick(bd, heads + h)
    live = (lax.broadcasted_iota(jnp.int32, (length, 1), 0) < live_len).astype(f32)
    rate = jnp.exp(pick(log_ref[0:1, :], h))
    sb = sigm(bp)
    zp = dp + pick(bias_ref[0:1, :], h)
    return sb, live, rate, zp


def fwd_kernel(
    heads, len_ref, q_ref, k_ref, v_ref, g_ref, bd_ref, fq_ref, fk_ref, fv_ref, log_ref, bias_ref,
    gain_ref, gated_ref, inv_ref, u_ref, mixed_ref, state_ref, qpad, kpad, vpad, qs, ks, vs,
):
    h = pl.program_id(0)
    length = q_ref.shape[0]
    chunks = length // CH
    load_padded(qpad, q_ref)
    load_padded(kpad, k_ref)
    load_padded(vpad, v_ref)
    fill_vectors(
        length, qpad, kpad, vpad, taps(fq_ref), taps(fk_ref), taps(fv_ref), qs, ks, vs
    )
    sb, live, rate, zp = beta_decay(h, heads, length, len_ref[0], bd_ref[...], log_ref, bias_ref)
    beta = sb * live
    logs = -rate * softplus(zp)
    rows, cols = iotas(CH)
    kept = []
    mats = []
    for n in range(chunks):
        part = slice(n * CH, (n + 1) * CH)
        col, row = chunk_decay(logs[part], CH)
        gaps = col - row
        decay = jnp.where(rows >= cols, jnp.exp(jnp.where(rows >= cols, gaps, 0.0)), 0.0)
        kf = ks[part, :]
        gram = mm3(kf, kf, 1, 1)
        mats.append(jnp.where(rows > cols, beta[part] * decay * gram, 0.0))
        kept.append((part, col, decay))
    inverses = unit_lower_inverses(mats)
    state = None
    for n in range(chunks):
        part, col, decay = kept[n]
        kf = ks[part, :]
        qf = qs[part, :]
        inv_ref[0, part, :] = inverses[n].astype(inv_ref.dtype)
        grow = jnp.exp(col)
        rhs = vs[part, :]
        if state is not None:
            rhs = rhs - grow * mm(kf, state)
        u = mm3(inverses[n], beta[part] * rhs)
        u_ref[part, :] = u.astype(u_ref.dtype)
        scores = mm(qf, kf, 1, 1) * decay
        out = mm(scores, u)
        if state is not None:
            out = out + grow * mm(qf, state)
        mixed_ref[part, :] = out
        if n + 1 < chunks:
            last = col[CH - 1 :, :]
            add = mm(kf * jnp.exp(last - col), u, 0, 0)
            state = add if state is None else jnp.exp(last) * state + add
            state_ref[0, n] = state
    gain = gain_ref[0:1, :]
    live_len = len_ref[0]

    def finish(t, _):
        start = pl.multiple_of(t * TILE, TILE)
        sl = pl.ds(start, TILE)
        m = mixed_ref[sl, :]
        gp = g_ref[sl, :].astype(f32)
        pos = start + lax.broadcasted_iota(jnp.int32, (TILE, 1), 0)
        alive = (pos < live_len).astype(f32)
        r = lax.rsqrt(jnp.mean(m * m, axis=1, keepdims=True) + 1e-05)
        gated_ref[sl, :] = (m * r * gain * (gp * sigm(gp)) * alive).astype(bf16)
        return 0

    lax.fori_loop(0, length // TILE, finish, 0)


def bwd_kernel(
    heads, len_ref, q_ref, k_ref, v_ref, g_ref, bd_ref, fq_ref, fk_ref, fv_ref, log_ref, bias_ref,
    gain_ref, inv_ref, u_ref, mixed_ref, state_ref, dg_ref,
    dpre_out, dfq_out, dfk_out, dfv_out, dgain_out, dsmall_out,
    qpad, kpad, vpad, qs, ks, vs, dos, dqs, dks, dvs, dbds,
):
    h = pl.program_id(0)
    length = q_ref.shape[0]
    chunks = length // CH
    load_padded(qpad, q_ref)
    load_padded(kpad, k_ref)
    load_padded(vpad, v_ref)
    fq, fk, fv = taps(fq_ref), taps(fk_ref), taps(fv_ref)
    fill_vectors(length, qpad, kpad, vpad, fq, fk, fv, qs, ks, vs)
    live_len = len_ref[0]
    gain = gain_ref[0:1, :]

    @pl.when(h == 0)
    def _():
        dgain_out[...] = jnp.zeros(dgain_out.shape, f32)
        dbds[...] = jnp.zeros(dbds.shape, f32)
        dsmall_out[...] = jnp.zeros(dsmall_out.shape, f32)

    def gate_back(t, acc):
        start = pl.multiple_of(t * TILE, TILE)
        sl = pl.ds(start, TILE)
        m = mixed_ref[sl, :]
        gp = g_ref[sl, :].astype(f32)
        pos = start + lax.broadcasted_iota(jnp.int32, (TILE, 1), 0)
        alive = (pos < live_len).astype(f32)
        r = lax.rsqrt(jnp.mean(m * m, axis=1, keepdims=True) + 1e-05)
        n = m * r
        t_ = dg_ref[sl, :].astype(f32) * alive
        s = sigm(gp)
        act = gp * s
        tn = t_ * n
        dpre_out[sl, lanes_at(2 * heads + h, 512)] = (
            tn * gain * (s + act * (1.0 - s))
        ).astype(bf16)
        dn = t_ * gain * act
        dos[sl, :] = r * (dn - n * jnp.mean(dn * n, axis=1, keepdims=True))
        return acc + jnp.sum((tn * act).reshape(TILE // 8, 8, tn.shape[1]), axis=0)

    dgain = lax.fori_loop(0, length // TILE, gate_back, jnp.zeros((8, gain.shape[1]), f32))
    dgain_out[...] += dgain

    sb, live, rate, zp = beta_decay(h, heads, length, live_len, bd_ref[...], log_ref, bias_ref)
    beta = sb * live
    sp = softplus(zp)
    logs = -rate * sp
    rows, cols = iotas(CH)
    incl = rows >= cols
    ones = jnp.ones((CH, 128), f32)
    dstate = None
    dbetas = [None] * chunks
    dlogs = [None] * chunks
    for n in reversed(range(chunks)):
        part = slice(n * CH, (n + 1) * CH)
        col, row = chunk_decay(logs[part], CH)
        gaps = col - row
        decay = jnp.where(incl, jnp.exp(jnp.where(incl, gaps, 0.0)), 0.0)
        grow = jnp.exp(col)
        last = col[CH - 1 :, :]
        kf = ks[part, :]
        qf = qs[part, :]
        u = u_ref[part, :].astype(f32)
        inv = inv_ref[0, part, :]
        do = dos[part, :]
        b = beta[part]
        gram = mm(kf, kf, 1, 1)
        strict_decay = jnp.where(rows > cols, decay, 0.0)
        scores = mm(qf, kf, 1, 1) * decay
        m_all = mm(do, u, 1, 1)
        du = mm(scores, do, 0, 0)
        tail = jnp.exp(last - col)
        if dstate is not None:
            kend = kf * tail
            du = du + mm(kend, dstate)
        dr = mm(inv, du, 0, 0)
        dvs[part, :] = b * dr
        da = mm(dr, u, 1, 1)
        da_dec = -da * strict_decay
        da_gram = da_dec * gram
        dbeta = jnp.sum(da_gram, axis=1, keepdims=True)
        msc = m_all * scores
        both = msc + b * da_gram
        rs = jnp.sum(both, axis=1, keepdims=True)
        both_h, both_l = split2(both)
        cs = (mm(both_h, ones, 0, 0) + mm(both_l, ones, 0, 0))[:, :1]
        dc = rs - cs
        dqk = m_all * decay
        dgram = b * da_dec
        dq = mm(dqk, kf)
        dk = mm(dqk, qf, 0, 0) + mm(dgram, kf) + mm(dgram, kf, 0, 0)
        rest = vs[part, :]
        dlast = None
        if n > 0:
            state = state_ref[0, n - 1]
            kst = mm(kf, state)
            qst = mm(qf, state)
            rest = rest - grow * kst
            dkst = -(b * grow) * dr
            dqst = grow * do
            dk = dk + mm(dkst, state, 1, 1)
            dq = dq + mm(dqst, state, 1, 1)
            dc = dc + jnp.sum(dkst * kst + dqst * qst, axis=1, keepdims=True)
            dprev = mm(kf, dkst, 0, 0) + mm(qf, dqst, 0, 0)
        dbetas[n] = dbeta + jnp.sum(dr * rest, axis=1, keepdims=True)
        if dstate is not None:
            dkend = mm(u, dstate, 1, 1)
            dk = dk + dkend * tail
            w = jnp.sum(dkend * kend, axis=1, keepdims=True)
            dc = dc - w
            dlast = jnp.sum(w, axis=0, keepdims=True)
            if n > 0:
                scale = jnp.exp(last)
                dprev = dprev + scale * dstate
                dlast = dlast + scale * jnp.sum(
                    jnp.sum(dstate * state, axis=1, keepdims=True), axis=0, keepdims=True
                )
        dlog = suffix_sum(dc, CH)
        if dlast is not None:
            dlog = dlog + dlast
        dlogs[n] = dlog
        dqs[part, :] = dq
        dks[part, :] = dk
        if n > 0:
            dstate = dprev
    dbeta = jnp.concatenate(dbetas, axis=0)
    dlog = jnp.concatenate(dlogs, axis=0)
    dbp = dbeta * live * sb * (1.0 - sb)
    dzp = -rate * dlog * sigm(zp)
    lanes = lax.broadcasted_iota(jnp.int32, (length, 128), 1)
    dbds[...] += jnp.where(lanes == h, dbp, 0.0) + jnp.where(lanes == heads + h, dzp, 0.0)

    @pl.when(h == heads - 1)
    def _():
        dpre_out[:, 12 * heads * 128 : (12 * heads + 1) * 128] = dbds[...].astype(bf16)

    small_lane = lax.broadcasted_iota(jnp.int32, (8, 128), 1)
    small_row = lax.broadcasted_iota(jnp.int32, (8, 128), 0)
    at_head = small_lane == h
    dsmall_out[...] += jnp.where(
        at_head & (small_row == 0), jnp.sum(dlog * logs, axis=0, keepdims=True), 0.0
    ) + jnp.where(at_head & (small_row == 1), jnp.sum(dzp, axis=0, keepdims=True), 0.0)

    def pre_back(t, _):
        start = pl.multiple_of(t * TILE, TILE)
        sl = pl.ds(start, TILE)
        for pad, filt, dref, scale in ((qpad, fq, dqs, 256 ** (-0.5)), (kpad, fk, dks, 1.0)):
            y = conv_rows(pad, start, TILE, filt)
            s = sigm(y)
            a = y * s
            r = lax.rsqrt(jnp.sum(a * a, axis=1, keepdims=True) + 1e-06)
            nn = a * r
            dn = dref[sl, :] * scale
            da_ = r * (dn - nn * jnp.sum(dn * nn, axis=1, keepdims=True))
            dref[sl, :] = da_ * (s + a * (1.0 - s))
        y = conv_rows(vpad, start, TILE, fv)
        s = sigm(y)
        dvs[sl, :] = dvs[sl, :] * (s + y * s * (1.0 - s))
        return 0

    lax.fori_loop(0, length // TILE, pre_back, 0)
    for dref in (dqs, dks, dvs):
        dref[length : length + PADR, :] = jnp.zeros((PADR, dref.shape[1]), f32)

    for pad, filt, dref, first, fout in (
        (qpad, fq, dqs, h, dfq_out),
        (kpad, fk, dks, heads + h, dfk_out),
        (vpad, fv, dvs, heads + h, dfv_out),
    ):
        width = dref.shape[1]

        def conv_back(t, accs, pad=pad, filt=filt, dref=dref, first=first, width=width):
            start = pl.multiple_of(t * TILE, TILE)
            dx = None
            new = []
            dys = dref[pl.ds(start, TILE + PADR), :]
            xs = pad[pl.ds(start, TILE + PADR), :]
            dy = dys[:TILE]
            for i in range(4):
                term = filt[i] * dys[3 - i : 3 - i + TILE]
                dx = term if dx is None else dx + term
                prod = dy * xs[PADR - 3 + i : PADR - 3 + i + TILE]
                new.append(accs[i] + jnp.sum(prod.reshape(TILE // 8, 8, width), axis=0))
            dpre_out[pl.ds(start, TILE), lanes_at(first, width)] = dx.astype(bf16)
            return tuple(new)

        accs = lax.fori_loop(
            0, length // TILE, conv_back, tuple(jnp.zeros((8, width), f32) for _ in range(4))
        )
        for i in range(4):
            fout[i : i + 1, :] = jnp.sum(accs[i], axis=0, keepdims=True)


def col_spec(length, width, first=0):
    return pl.BlockSpec((length, width), lambda h: (0, first + h))


def whole_spec(shape):
    return pl.BlockSpec(shape, lambda h: (0,) * len(shape))


def front_specs(length, heads):
    return [
        pl.BlockSpec(memory_space=pltpu.SMEM),
        col_spec(length, 256),
        col_spec(length, 256, heads),
        col_spec(length, 512, heads),
        col_spec(length, 512, 2 * heads),
        pl.BlockSpec((length, 128), lambda h: (0, 12 * heads)),
        col_spec(4, 256),
        col_spec(4, 256),
        col_spec(4, 512),
        whole_spec((1, 128)),
        whole_spec((1, 128)),
        whole_spec((1, 512)),
    ]


def mixer_forward(heads, lens, pre, fq, fk, fv, logs, bias, gain):
    length = pre.shape[0]
    chunks = length // CH
    kept = max(1, chunks - 1)
    return pl.pallas_call(
        functools.partial(fwd_kernel, heads),
        grid=(heads,),
        in_specs=front_specs(length, heads),
        out_specs=[
            col_spec(length, 512),
            pl.BlockSpec((1, length, CH), lambda h: (h, 0, 0)),
            col_spec(length, 512),
            col_spec(length, 512),
            pl.BlockSpec((1, kept, 256, 512), lambda h: (h, 0, 0, 0)),
        ],
        out_shape=[
            jax.ShapeDtypeStruct((length, heads * 512), bf16),
            jax.ShapeDtypeStruct((heads, length, CH), bf16),
            jax.ShapeDtypeStruct((length, heads * 512), bf16),
            jax.ShapeDtypeStruct((length, heads * 512), f32),
            jax.ShapeDtypeStruct((heads, kept, 256, 512), f32),
        ],
        scratch_shapes=[
            pltpu.VMEM((length + PADR, 256), f32),
            pltpu.VMEM((length + PADR, 256), f32),
            pltpu.VMEM((length + PADR, 512), f32),
            pltpu.VMEM((length, 256), f32),
            pltpu.VMEM((length, 256), f32),
            pltpu.VMEM((length, 512), f32),
        ],
        compiler_params=pltpu.CompilerParams(vmem_limit_bytes=50 * 1024 * 1024),
        name="mixer_forward",
    )(lens, pre, pre, pre, pre, pre, fq, fk, fv, logs, bias, gain)


def mixer_backward(heads, lens, pre, fq, fk, fv, logs, bias, gain, saved, dgated):
    length = pre.shape[0]
    chunks = length // CH
    kept = max(1, chunks - 1)
    inv, u, mixed, states = saved
    return pl.pallas_call(
        functools.partial(bwd_kernel, heads),
        grid=(heads,),
        in_specs=front_specs(length, heads)
        + [
            pl.BlockSpec((1, length, CH), lambda h: (h, 0, 0)),
            col_spec(length, 512),
            col_spec(length, 512),
            pl.BlockSpec((1, kept, 256, 512), lambda h: (h, 0, 0, 0)),
            col_spec(length, 512),
        ],
        out_specs=[
            whole_spec((length, pre.shape[1])),
            col_spec(4, 256), col_spec(4, 256), col_spec(4, 512),
            whole_spec((8, 512)), whole_spec((8, 128)),
        ],
        out_shape=[
            jax.ShapeDtypeStruct(pre.shape, bf16),
            jax.ShapeDtypeStruct((4, heads * 256), f32),
            jax.ShapeDtypeStruct((4, heads * 256), f32),
            jax.ShapeDtypeStruct((4, heads * 512), f32),
            jax.ShapeDtypeStruct((8, 512), f32),
            jax.ShapeDtypeStruct((8, 128), f32),
        ],
        scratch_shapes=[
            pltpu.VMEM((length + PADR, 256), f32),
            pltpu.VMEM((length + PADR, 256), f32),
            pltpu.VMEM((length + PADR, 512), f32),
            pltpu.VMEM((length, 256), f32),
            pltpu.VMEM((length, 256), f32),
            pltpu.VMEM((length, 512), f32),
            pltpu.VMEM((length, 512), f32),
            pltpu.VMEM((length + PADR, 256), f32),
            pltpu.VMEM((length + PADR, 256), f32),
            pltpu.VMEM((length + PADR, 512), f32),
            pltpu.VMEM((length, 128), f32),
        ],
        compiler_params=pltpu.CompilerParams(vmem_limit_bytes=50 * 1024 * 1024),
        name="mixer_backward",
    )(lens, pre, pre, pre, pre, pre, fq, fk, fv, logs, bias, gain, inv, u, mixed, states, dgated)


MESH = pl.DeviceIdType.MESH


def column_chunks(widths, size, layers):
    size = size * max(1, layers // 4)
    out = []
    for a, width in enumerate(widths):
        units = width // 128
        count = max(1, -(-width // size))
        lo = 0
        for i in range(count):
            hi = units * (i + 1) // count
            out.append((a, lo * 128, (hi - lo) * 128))
            lo = hi
    return out


def placement():
    spot = lax.axis_index("dp")
    return spot, lax.rem(spot, 2), lax.rem(lax.div(spot, 2), 2), lax.div(spot, 4)


def greet(partners):
    barrier = pltpu.get_barrier_semaphore()
    for partner in partners:
        pl.semaphore_signal(barrier, inc=1, device_id={"dp": partner}, device_id_type=MESH)
    pl.semaphore_wait(barrier, len(partners))


def remote(src, dst, send, recv, target):
    return pltpu.make_async_remote_copy(
        src_ref=src, dst_ref=dst, send_sem=send, recv_sem=recv,
        device_id={"dp": target}, device_id_type=MESH,
    )


def gather_kernel(layers, chunks, count, pairs, *refs):
    srcs, outs = refs[: count + pairs], refs[count + pairs : 2 * (count + pairs)]
    own_sem, us, ur, ds, dr, ys, yr, cs, cr, ps, pr, pair_sem = refs[2 * (count + pairs) :]
    rows = srcs[0].shape[0]
    spot, core, side, layer = placement()
    turn = lax.axis_index("tensor")
    at = lambda z, y, c: 4 * z + 2 * y + c
    y_to, c_to = at(layer, 1 - side, core), at(layer, side, 1 - core)
    has_up, has_down = layer < layers - 1, layer > 0
    barrier = pltpu.get_barrier_semaphore()
    around = [4 * lax.rem(layer + s, layers) + 2 * side + core for s in (1, layers - 1)]
    for partner in [y_to, c_to] + around:
        pl.semaphore_signal(barrier, inc=1, device_id={"dp": partner}, device_id_type=MESH)
    pl.semaphore_signal(barrier, inc=1, device_id={"tensor": 1 - turn}, device_id_type=MESH)
    pl.semaphore_wait(barrier, 5)

    def place(j, origin):
        a, lo, width, _ = chunks[j]
        start = pl.multiple_of(origin * rows, rows)
        return outs[a].at[pl.ds(start, rows), lo : lo + width]

    def own(j):
        a, lo, width, _ = chunks[j]
        return srcs[a].at[:, lo : lo + width]

    def up_copy(j, k, half, origin, src):
        i = 2 * k + half
        return remote(src, place(j, origin), us.at[j, i], ur.at[j, i], spot + 4)

    def down_copy(j, k, half, origin, src):
        i = 2 * k + half
        return remote(src, place(j, origin), ds.at[j, i], dr.at[j, i], spot - 4)

    def y_copy(j, slot, origin, src):
        return remote(src, place(j, origin), ys.at[j, slot], yr.at[j, slot], y_to)

    def c_copy(j, slot, origin, src):
        return remote(src, place(j, origin), cs.at[j, slot], cr.at[j, slot], c_to)

    number = len(chunks)
    narrow = [j for j in range(number) if not chunks[j][3]]
    early = [j for j in range(number) if chunks[j][3]]
    keep = []
    for p in range(pairs):
        half_rows = srcs[count + p].shape[0]
        spot_rows = pl.ds(pl.multiple_of(turn * half_rows, half_rows), half_rows)
        copy = pltpu.make_async_remote_copy(
            src_ref=srcs[count + p], dst_ref=outs[count + p].at[spot_rows, :],
            send_sem=ps.at[p], recv_sem=pr.at[p],
            device_id={"tensor": 1 - turn}, device_id_type=MESH,
        )
        copy.start()
        local_copy = pltpu.make_async_copy(
            srcs[count + p], outs[count + p].at[spot_rows, :], pair_sem.at[p]
        )
        local_copy.start()
        keep.append((copy, local_copy))

    def send_z(j, half, origin, src):
        @pl.when(has_up)
        def _():
            up_copy(j, 0, half, origin, src).start()

        @pl.when(has_down)
        def _():
            down_copy(j, 0, half, origin, src).start()

    locals_ = []
    for j in early + narrow:
        y_copy(j, 0, spot, own(j)).start()
        send_z(j, 0, spot, own(j))
        c_copy(j, 0, spot, own(j)).start()
        copy = pltpu.make_async_copy(own(j), place(j, spot), own_sem.at[j])
        copy.start()
        locals_.append(copy)
    across = at(layer, 1 - side, core)

    def take_z(j, k, half):
        there = lax.rem(side + half, 2)
        for sign, fits, more, copy in (
            (-1, layer >= k + 1, has_up, up_copy),
            (1, layer + k + 1 < layers, has_down, down_copy),
        ):

            @pl.when(fits)
            def _(sign=sign, more=more, copy=copy):
                origin = at(layer + sign * (k + 1), there, core)
                here = place(j, origin)
                copy(j, k, half, origin, here).wait_recv()

                @pl.when(more)
                def _():
                    copy(j, k + 1, half, origin, here).start()

                slot = 2 * k + (1 if sign < 0 else 2)
                if not chunks[j][3]:
                    y_copy(j, slot, origin, here).start()
                c_copy(j, slot if half == 0 else slot + 2 * layers - 1, origin, here).start()

    def take_y(j, k):
        slots = [(0, None, None)] if k == 0 else [
            (2 * k - 1, layer >= k, -1), (2 * k, layer + k < layers, 1)
        ]
        for slot, fits, sign in slots:
            shift = 0 if sign is None else sign * k

            def body(slot=slot, shift=shift):
                origin = at(layer + shift, 1 - side, core)
                here = place(j, origin)
                y_copy(j, slot, origin, here).wait_recv()
                c_copy(j, 2 * layers - 1 + slot, origin, here).start()

            if fits is None:
                body()
            else:
                pl.when(fits)(body)

    for j in early:
        y_copy(j, 0, across, own(j)).wait_recv()
        send_z(j, 1, across, place(j, across))
        c_copy(j, 2 * layers - 1, across, place(j, across)).start()
    for k in range(layers):
        if k < layers - 1:
            for j in early:
                for half in range(2):
                    take_z(j, k, half)
            for j in narrow:
                take_z(j, k, 0)
        if k > 0:
            for j in narrow:
                take_y(j, k - 1)
    for j in narrow:
        take_y(j, layers - 1)

    for copy, local_copy in keep:
        local_copy.wait()
        copy.wait()
    for copy in locals_:
        copy.wait()
    for j in range(number):
        wide = chunks[j][3]
        me = own(j)
        for half in range(2 if wide else 1):
            for k in range(layers - 1):

                @pl.when(has_up & (layer >= k))
                def _(k=k, half=half):
                    up_copy(j, k, half, spot, me).wait_send()

                @pl.when(has_down & (layer + k < layers))
                def _(k=k, half=half):
                    down_copy(j, k, half, spot, me).wait_send()

        def settle(slot, shift):
            if slot == 0 or not wide:
                y_copy(j, slot, spot, me).wait_send()
            for half in range(2):
                origin = at(layer + shift, lax.rem(side + half, 2), 1 - core)
                c_copy(j, slot + half * (2 * layers - 1), origin, place(j, origin)).wait()

        settle(0, 0)
        for k in range(1, layers):
            pl.when(layer >= k)(functools.partial(settle, 2 * k - 1, -k))
            pl.when(layer + k < layers)(functools.partial(settle, 2 * k, k))


def mark_early(chunks, share):
    total = sum(c[2] for c in chunks)
    marked, done = [], 0
    for c in chunks:
        early = done + c[2] <= share * total + 64
        done += c[2] if early else 0
        marked.append(c + (early,))
    return marked


def gather_all(shards, pairs, devices, ident, size=512, share=1 / 6):
    rows = shards[0].shape[0]
    layers = devices // 4
    chunks = mark_early(column_chunks([s.shape[1] for s in shards], size, layers), share)
    n = len(chunks)
    sem = lambda *shape: pltpu.SemaphoreType.DMA(shape)
    z_slots, slots = 2 * layers, 2 * layers - 1
    arrays = tuple(shards) + tuple(pairs)
    return pl.pallas_call(
        functools.partial(gather_kernel, layers, chunks, len(shards), len(pairs)),
        in_specs=[pl.BlockSpec(memory_space=pl.ANY)] * len(arrays),
        out_specs=[pl.BlockSpec(memory_space=pl.ANY)] * len(arrays),
        out_shape=[jax.ShapeDtypeStruct((devices * rows, s.shape[1]), s.dtype) for s in shards]
        + [jax.ShapeDtypeStruct((2 * p.shape[0], p.shape[1]), p.dtype) for p in pairs],
        scratch_shapes=[
            sem(n), sem(n, z_slots), sem(n, z_slots), sem(n, z_slots), sem(n, z_slots),
            sem(n, slots), sem(n, slots), sem(n, 2 * slots), sem(n, 2 * slots),
            sem(max(1, len(pairs))), sem(max(1, len(pairs))), sem(max(1, len(pairs))),
        ],
        compiler_params=pltpu.CompilerParams(collective_id=ident, has_side_effects=True),
        name="gather_rows",
    )(*arrays)


def scatter_kernel(layers, chunks, dots, *refs):
    n_held = max([c[0] for c in chunks if c[3] is None]) + 1
    srcs, lefts = refs[:n_held], refs[n_held : n_held + dots]
    rights = refs[n_held + dots : n_held + 2 * dots]
    sent_ref, out, come_ref = refs[n_held + 2 * dots : n_held + 2 * dots + 3]
    (stage, sends, buf1, buf2, buf3, own_sem, cs, cr, ys, yr, zs, zr, pair_send,
     pair_recv) = refs[n_held + 2 * dots + 3 :]
    rows = out.shape[0]
    spot, core, side, layer = placement()
    turn = lax.axis_index("tensor")
    at = lambda z, y, c: 4 * lax.rem(z + layers, layers) + 2 * y + c
    z_to = [at(layer + k, side, core) for k in range(1, layers)]
    y_to, c_to = at(layer, 1 - side, core), at(layer, side, 1 - core)
    barrier = pltpu.get_barrier_semaphore()
    for partner in z_to + [y_to, c_to]:
        pl.semaphore_signal(barrier, inc=1, device_id={"dp": partner}, device_id_type=MESH)
    pl.semaphore_signal(barrier, inc=1, device_id={"tensor": 1 - turn}, device_id_type=MESH)
    pl.semaphore_wait(barrier, layers + 2)
    number = len(chunks)
    firsts = []
    total = 0
    for chunk in chunks:
        firsts.append(total)
        total += chunk[2]
    pair = pltpu.make_async_remote_copy(
        src_ref=sent_ref, dst_ref=come_ref, send_sem=pair_send, recv_sem=pair_recv,
        device_id={"tensor": 1 - turn}, device_id_type=MESH,
    )
    pair.start()

    def cols(j):
        return slice(firsts[j], firsts[j] + chunks[j][2])

    def c_copy(j):
        a, lo, width, which = chunks[j]
        if which is None:
            src = srcs[a].at[:, 1 - core, :, lo : lo + width]
        else:
            src = sends.at[j % 3, :, :, 0:width]
        return remote(src, buf1.at[:, :, cols(j)], cs.at[j], cr.at[j], c_to)

    def own_copy(j):
        a, lo, width, _ = chunks[j]
        return pltpu.make_async_copy(
            srcs[a].at[:, core, :, lo : lo + width],
            stage.at[j % 3, :, :, 0:width], own_sem.at[j],
        )

    def y_copy(j, m):
        block = 2 * lax.rem(layer + m, layers) + 1 - side
        return remote(
            buf1.at[block, :, cols(j)], buf2.at[m, :, cols(j)], ys.at[j, m], yr.at[j, m], y_to
        )

    def z_copy(j, k):
        return remote(
            buf2.at[k, :, cols(j)], buf3.at[k - 1, :, cols(j)], zs.at[j, k - 1], zr.at[j, k - 1],
            z_to[k - 1],
        )

    def produce(j):
        a, lo, width, which = chunks[j]
        if which is None:
            own_copy(j).start()
        else:
            if j >= 3:
                c_copy(j - 3).wait_send()
            right = rights[which][:, lo : lo + width]

            wide = 256
            per = wide // (2 * rows)

            def body(g, _):
                left = lefts[which][:, pl.ds(pl.multiple_of(g * wide, wide), wide)]
                both = mm(left, right, 0, 0)
                for i in range(per):
                    low_half = both[2 * i * rows : (2 * i + 1) * rows]
                    high_half = both[(2 * i + 1) * rows : (2 * i + 2) * rows]
                    mine = jnp.where(core == 0, low_half, high_half)
                    other = jnp.where(core == 0, high_half, low_half)
                    stage[j % 3, g * per + i, :, 0:width] = mine.astype(bf16)
                    sends[j % 3, g * per + i, :, 0:width] = other.astype(bf16)
                return 0

            lax.fori_loop(0, 2 * layers // per, body, 0)
        c_copy(j).start()

    for j in range(min(2, number)):
        produce(j)

    def first(j):
        width = chunks[j][2]
        if chunks[j][3] is None:
            own_copy(j).wait()
        c_copy(j).wait_recv()

        def body(b, _):
            mine = stage[j % 3, b, :, 0:width].astype(f32)
            buf1[b, :, cols(j)] = (buf1[b, :, cols(j)].astype(f32) + mine).astype(bf16)
            return 0

        lax.fori_loop(0, 2 * layers, body, 0)
        for m in list(range(1, layers)) + [0]:
            y_copy(j, m).start()
        if j + 2 < number:
            produce(j + 2)

    def second(j):
        for m in list(range(1, layers)) + [0]:
            y_copy(j, m).wait_recv()
            block = 2 * lax.rem(layer + m, layers) + side
            mine = buf1[block, :, cols(j)].astype(f32)
            buf2[m, :, cols(j)] = (buf2[m, :, cols(j)].astype(f32) + mine).astype(bf16)
            if m:
                z_copy(j, m).start()

    def third(j):
        total = buf2[0, :, cols(j)].astype(f32)
        for k in range(1, layers):
            z_copy(j, k).wait_recv()
            total = total + buf3[k - 1, :, cols(j)].astype(f32)
        out[:, cols(j)] = total

    for j in range(number + 4):
        if j < number:
            first(j)
        if 0 <= j - 2 < number:
            second(j - 2)
        if 0 <= j - 4 < number:
            third(j - 4)
    for j in range(number):
        later = j + 3 < number and chunks[j + 3][3] is not None
        if not later:
            c_copy(j).wait_send()
        for m in range(layers):
            y_copy(j, m).wait_send()
        for k in range(1, layers):
            z_copy(j, k).wait_send()
    pair.wait()


def scatter_sum(held, products, tail, sent, devices, ident, size=512):
    parts = [held, tail]
    rows = held.shape[0] // devices
    layers = devices // 4
    widths = [held.shape[1]] + [w for _, _, w in products] + [tail.shape[1]]
    chunks = []
    for a, lo, width in column_chunks(widths, size, 4):
        if a == 0:
            chunks.append((0, lo, width, None))
        elif a <= len(products):
            chunks.append((a, lo, width, a - 1))
        else:
            chunks.append((1, lo, width, None))
    n = len(chunks)
    width = sum(widths)
    widest = max(c[2] for c in chunks)
    sem = lambda *shape: pltpu.SemaphoreType.DMA(shape)
    hbm, vmem = pl.BlockSpec(memory_space=pl.ANY), pl.BlockSpec(memory_space=pltpu.VMEM)
    return pl.pallas_call(
        functools.partial(scatter_kernel, layers, chunks, len(products)),
        in_specs=[hbm] * 2 + [vmem] * (2 * len(products)) + [hbm],
        out_specs=[vmem, hbm],
        out_shape=[
            jax.ShapeDtypeStruct((rows, width), f32),
            jax.ShapeDtypeStruct(sent.shape, sent.dtype),
        ],
        scratch_shapes=[
            pltpu.VMEM((3, 2 * layers, rows, widest), bf16),
            pltpu.VMEM((3, 2 * layers, rows, widest), bf16),
            pltpu.VMEM((2 * layers, rows, width), bf16),
            pltpu.VMEM((layers, rows, width), bf16),
            pltpu.VMEM((layers - 1, rows, width), bf16),
            sem(n), sem(n), sem(n), sem(n, layers), sem(n, layers),
            sem(n, layers - 1), sem(n, layers - 1),
            pltpu.SemaphoreType.DMA, pltpu.SemaphoreType.DMA,
        ],
        compiler_params=pltpu.CompilerParams(
            collective_id=ident, has_side_effects=True, vmem_limit_bytes=61 * 1024 * 1024
        ),
        name="scatter_sum",
    )(
        *[p.reshape(devices // 2, 2, rows, p.shape[1]) for p in parts],
        *[p[0] for p in products],
        *[p[1] for p in products],
        sent,
    )


EXTRA = 128


def rms_scale(values):
    return lax.rsqrt(jnp.mean(values * values, axis=-1, keepdims=True) + 1e-05)


def norm_back(values, gain, grad_normed):
    scale = rms_scale(values)
    unit_vals = values * scale
    grad_unit = grad_normed * gain
    grad_values = scale * (
        grad_unit - unit_vals * jnp.mean(grad_unit * unit_vals, axis=-1, keepdims=True)
    )
    return (grad_values, jnp.sum(grad_normed * unit_vals, axis=0))


def pair_swap(values):
    return lax.ppermute(values, "tensor", [(0, 1), (1, 0)])


def pair_gather(values):
    other = pair_swap(values)
    first = lax.axis_index("tensor") == 0
    return jnp.concatenate(
        [jnp.where(first, values, other), jnp.where(first, other, values)], axis=0
    )


def pair_halves(parts):
    rows = parts.shape[0] // 2
    mine = lax.axis_index("tensor") * rows
    kept = lax.dynamic_slice_in_dim(parts, mine, rows)
    sent = lax.dynamic_slice_in_dim(parts, rows - mine, rows).astype(bf16)
    return kept, sent


def pair_scatter(parts):
    kept, sent = pair_halves(parts)
    return kept + pair_swap(sent).astype(f32)


def dot(a, b, ca=1, cb=0):
    return lax.dot_general(a, b, (((ca,), (cb,)), ((), ())), preferred_element_type=f32)


def high_low(values):
    high = lax.reduce_precision(values, 8, 7)
    return jnp.stack([high, values - high], axis=1).astype(bf16)


def gather_rows(values):
    return lax.all_gather(values, "dp", axis=0, tiled=True)


def scatter_rows(values):
    return lax.psum_scatter(values, "dp", scatter_dimension=0, tiled=True)


def pack_filters(fq, fk, fv, rows):
    flat = jnp.concatenate([fq, fk, fv], axis=2).reshape(-1)
    return flat.reshape(-1, rows).T


def local(
    tokens,
    lengths,
    cotangent,
    gain_in,
    gain_ffn,
    gain_out,
    w_query,
    w_key,
    w_value,
    w_gate,
    w_beta,
    w_decay,
    conv_query,
    conv_key,
    conv_value,
    decay_log,
    decay_bias,
    w_output,
    w_ffn_gate,
    w_ffn_up,
    w_ffn_down,
):
    heads = w_beta.shape[1]
    rows = w_query.shape[0]
    devices = lax.axis_size("dp")
    low = lambda v: v.astype(bf16)
    filters = pack_filters(conv_query, conv_key, conv_value, rows)
    filter_cols = filters.shape[1]
    gains = pair_gather(jnp.concatenate([gain_in, gain_ffn, gain_out])[None])
    n_in, n_out = gain_in.shape[0], gain_out.shape[0]
    pair_out = jnp.pad(gains[:, 2 * n_in :].reshape(-1), (0, rows - 2 * n_out))
    small = jnp.concatenate(
        [
            low(jnp.concatenate([w_beta, w_decay, filters], axis=1)),
            high_low(gains[:, :n_in].reshape(-1)),
            high_low(gains[:, n_in : 2 * n_in].reshape(-1)),
            high_low(pair_out),
        ],
        axis=1,
    )
    small = jnp.pad(small, ((0, 0), (0, EXTRA - small.shape[1])))
    proj_shard = jnp.concatenate(
        [low(w_query), low(w_key), low(w_value), low(w_gate), small], axis=1
    )
    proj, out_t, seq_x, seq_cot = gather_all(
        (proj_shard, low(w_output).T), (tokens, cotangent), devices, 0
    )
    extra_at = 12 * heads * 128
    gain_at = extra_at + 2 * heads + filter_cols
    sides = proj[:, gain_at : gain_at + 6].astype(f32)
    sides = sides[:, 0::2] + sides[:, 1::2]
    full_in, full_ffn = sides[:, 0], sides[:, 1]
    full_out = sides[:, 2].reshape(devices, rows)[:, : 2 * n_out].reshape(1, -1)
    gate_weight = gather_rows(low(w_ffn_gate))
    up_weight = gather_rows(low(w_ffn_up))
    down_t = gather_rows(low(w_ffn_down).T)

    tap_count = conv_query.shape[0]
    piece_q, piece_v = conv_query.shape[2], conv_value.shape[2]
    flat = proj[:, extra_at + 2 * heads : gain_at]
    flat = flat.reshape(devices, rows, filter_cols).transpose(0, 2, 1)
    flat = flat.reshape(devices, tap_count, heads, 2 * piece_q + piece_v).astype(f32)
    flat = flat.transpose(1, 2, 0, 3)
    filt_q = flat[..., :piece_q].reshape(tap_count, -1)
    filt_k = flat[..., piece_q : 2 * piece_q].reshape(tap_count, -1)
    filt_v = flat[..., 2 * piece_q :].reshape(tap_count, -1)

    head_start = lax.axis_index("tensor") * heads
    lane_pad = lambda v: jnp.pad(
        lax.dynamic_slice_in_dim(v, head_start, heads), (0, 128 - heads)
    ).reshape(1, 128)
    local_log, local_bias = lane_pad(decay_log), lane_pad(decay_bias)

    inputs = tokens.astype(f32)
    seq_inputs = seq_x.astype(f32)
    seq_unit = seq_inputs * rms_scale(seq_inputs)
    seq_in = low(seq_unit * full_in)
    pre = dot(seq_in, proj)
    mixer_args = (heads, lengths, pre, filt_q, filt_k, filt_v, local_log, local_bias, full_out)
    gated, *saved = mixer_forward(*mixer_args)
    hidden = inputs + pair_scatter(dot(gated, out_t, 1, 1))
    normed_ffn = low(hidden * rms_scale(hidden) * full_ffn)
    normed_ffn, down_t = lax.optimization_barrier((normed_ffn, down_t))
    seq_ffn = pair_gather(normed_ffn)
    grad_inner = dot(seq_cot, down_t)
    seq_ffn, grad_inner = lax.optimization_barrier((seq_ffn, grad_inner))

    gate_act = dot(seq_ffn, gate_weight)
    up_act = dot(seq_ffn, up_weight)
    sigmoid_gate = jax.nn.sigmoid(gate_act)
    silu_gate = gate_act * sigmoid_gate
    inner = low(silu_gate * up_act)
    grad_gate_act = low(
        grad_inner * up_act * sigmoid_gate * (1.0 + gate_act * (1.0 - sigmoid_gate))
    )
    grad_up_act = low(grad_inner * silu_gate)
    grad_down = low(dot(seq_cot, inner, 0, 0))
    grad_gate_act, grad_up_act, grad_down = lax.optimization_barrier(
        (grad_gate_act, grad_up_act, grad_down)
    )
    down_piece = scatter_rows(grad_down)
    grad_seq_ffn = dot(grad_gate_act, gate_weight, 1, 1) + dot(grad_up_act, up_weight, 1, 1)
    kept_ffn, sent_ffn = pair_halves(grad_seq_ffn)
    sent_ffn, inner = lax.optimization_barrier((sent_ffn, inner))
    kept_out, sent_out = pair_halves(dot(inner, down_t, 1, 1))
    come_ffn, sent_out = lax.optimization_barrier((pair_swap(sent_ffn), sent_out))
    grad_normed_ffn = kept_ffn + come_ffn.astype(f32)
    grad_hidden_norm, grad_gain_ffn = norm_back(hidden, full_ffn, grad_normed_ffn)
    grad_hidden = cotangent.astype(f32) + grad_hidden_norm
    sent_branch, grad_gate_act, grad_up_act = lax.optimization_barrier(
        (low(grad_hidden), grad_gate_act, grad_up_act)
    )
    seq_grad_branch = pair_gather(sent_branch)
    grad_gate_w = low(dot(seq_ffn, grad_gate_act, 0, 0))
    grad_up_w = low(dot(seq_ffn, grad_up_act, 0, 0))
    seq_grad_branch, grad_gate_w, grad_up_w, sent_out = lax.optimization_barrier(
        (seq_grad_branch, grad_gate_w, grad_up_w, sent_out)
    )
    gate_piece = scatter_rows(grad_gate_w)
    come_out = pair_swap(sent_out)

    grad_gated = dot(seq_grad_branch, out_t)
    grad_pre, grad_fq, grad_fk, grad_fv, grad_gain_out, grad_small = mixer_backward(
        *mixer_args, saved, low(grad_gated)
    )
    grad_pre, come_out = lax.optimization_barrier((grad_pre, come_out))
    result = low(hidden + kept_out + come_out.astype(f32))
    grad_seq_in = dot(grad_pre, proj, 1, 1)
    kept_in, sent_in = pair_halves(grad_seq_in)
    extra = dot(seq_in, grad_pre[:, extra_at:], 0, 0)
    by_device = lambda g, piece: g.reshape(tap_count, heads, devices, piece)
    grad_flat = jnp.concatenate(
        [by_device(grad_fq, piece_q), by_device(grad_fk, piece_q), by_device(grad_fv, piece_v)],
        axis=3,
    ).transpose(2, 0, 1, 3)
    grad_flat = grad_flat.reshape(devices, filter_cols, rows).transpose(0, 2, 1)
    grad_flat = low(grad_flat.reshape(devices * rows, filter_cols))
    spread = lambda v: lax.dynamic_update_slice(jnp.zeros_like(decay_log), v, (head_start,))
    grad_decay = jnp.concatenate([spread(grad_small[0, :heads]), spread(grad_small[1, :heads])])
    by_rows = lambda v: jnp.pad(v, ((0, 0), (0, rows - v.shape[1]))).reshape(-1)
    columns = jnp.stack(
        [
            jnp.sum(grad_seq_in * seq_unit, axis=0),
            grad_gain_ffn,
            by_rows(jnp.sum(grad_gain_out, axis=0).reshape(devices, -1)),
            by_rows(jnp.broadcast_to(grad_decay, (devices,) + grad_decay.shape)),
        ],
        axis=1,
    )
    grad_tiny = jnp.concatenate(
        [low(extra[:, : 2 * heads]), grad_flat, low(columns)], axis=1
    )
    grad_tiny = jnp.pad(grad_tiny, ((0, 0), (0, EXTRA - grad_tiny.shape[1])))
    products = (
        (seq_in, grad_pre, extra_at),
        (seq_grad_branch, gated, gated.shape[1]),
    )
    pieces, come_in = scatter_sum(grad_up_w, products, grad_tiny, sent_in, devices, 1)
    ffn_width = grad_up_w.shape[1]
    up_piece, pieces = pieces[:, :ffn_width], pieces[:, ffn_width:]
    grad_normed_in = kept_in + come_in.astype(f32)
    out_width = w_output.shape[0]
    out_piece = pieces[:, extra_at : extra_at + out_width]
    tiny_piece = pieces[:, extra_at + out_width :]

    grad_inputs_norm, _ = norm_back(inputs, full_in, grad_normed_in)
    grad_tokens = grad_hidden + grad_inputs_norm

    sums = tiny_piece[:, 2 * heads + filter_cols : 2 * heads + filter_cols + 4].T
    sums = sums + pair_swap(sums)
    turn = lax.axis_index("tensor")
    take = lambda row, piece: lax.dynamic_slice_in_dim(sums[row], turn * piece, piece)
    n_heads = decay_log.shape[0]

    q_end, k_end = heads * 256, 2 * heads * 256
    v_end, g_end = k_end + heads * 512, k_end + 2 * heads * 512
    grad_filters = tiny_piece[:, 2 * heads : 2 * heads + filter_cols]
    grad_filters = grad_filters.T.reshape(tap_count, heads, 2 * piece_q + piece_v)
    return (
        result,
        grad_tokens,
        take(0, n_in),
        take(1, n_in),
        take(2, n_out),
        pieces[:, :q_end],
        pieces[:, q_end:k_end],
        pieces[:, k_end:v_end],
        pieces[:, v_end:g_end],
        tiny_piece[:, :heads],
        tiny_piece[:, heads : 2 * heads],
        grad_filters[..., :piece_q],
        grad_filters[..., piece_q : 2 * piece_q],
        grad_filters[..., 2 * piece_q :],
        sums[3, :n_heads],
        sums[3, n_heads : 2 * n_heads],
        out_piece.T,
        gate_piece.astype(f32),
        up_piece,
        down_piece.astype(f32).T,
    )


def solution(mesh):
    rows = P(("dp", "tensor"), None)
    spread = P(("dp", "tensor"))
    weight = P("dp", "tensor")
    filters = P(None, "tensor", "dp")
    turned = P("tensor", "dp")
    return jax.shard_map(
        local,
        mesh=mesh,
        in_specs=(rows, P("dp"), rows, spread, spread, spread)
        + (weight,) * 6
        + (filters,) * 3
        + (P(), P(), turned, weight, weight, turned),
        out_specs=(rows, rows, spread, spread, spread)
        + (weight,) * 6
        + (filters,) * 3
        + (P(), P(), turned, weight, weight, turned),
        check_vma=False,
    )
```

```python
import functools
import jax
import jax.numpy as jnp
from jax import lax
from jax.sharding import PartitionSpec as P
from jax.experimental import pallas as pl
from jax.experimental.pallas import tpu as pltpu

CH = 256
TILE = 64
PADR = 8
f32 = jnp.float32
bf16 = jnp.bfloat16


def mm(a, b, ca=1, cb=0):
    return lax.dot_general(
        a.astype(bf16), b.astype(bf16), (((ca,), (cb,)), ((), ())), preferred_element_type=f32
    )


def split2(a):
    high = a.astype(bf16)
    return high, (a - high.astype(f32)).astype(bf16)


def mm3(a, b, ca=1, cb=0):
    ah, al = split2(a)
    bh, bl = split2(b)
    return mm(ah, bh, ca, cb) + (mm(ah, bl, ca, cb) + mm(al, bh, ca, cb))


def iotas(n):
    return (
        lax.broadcasted_iota(jnp.int32, (n, n), 0),
        lax.broadcasted_iota(jnp.int32, (n, n), 1),
    )


def unit_lower_inverses(mats):
    n = mats[0].shape[0]
    rows, cols = iotas(n)
    eye = jnp.where(rows == cols, 1.0, 0.0).astype(f32)
    base = 8
    near = (rows // base) == (cols // base)
    powers = [jnp.where(near, a, 0.0) for a in mats]
    outs = [eye - p for p in powers]
    for _ in range(2):
        powers = [mm3(p, p) for p in powers]
        outs = [x + mm3(x, p) for x, p in zip(outs, powers)]
    size = base
    while size < n:
        wide = ((rows // (2 * size)) == (cols // (2 * size))) & ((rows // size) != (cols // size))
        halves = [mm3(jnp.where(wide, a, 0.0), x) for a, x in zip(mats, outs)]
        outs = [x - mm3(x, h) for x, h in zip(outs, halves)]
        size *= 2
    return outs


def sigm(v):
    return 1.0 / (1.0 + jnp.exp(-v))


def softplus(v):
    return jnp.maximum(v, 0.0) + jnp.log1p(jnp.exp(-jnp.abs(v)))


def pick(block, lane):
    lanes = lax.broadcasted_iota(jnp.int32, block.shape, 1)
    return jnp.sum(jnp.where(lanes == lane, block, 0.0), axis=1, keepdims=True)


def taps(ref):
    return [ref[i : i + 1, :] for i in range(4)]


def lanes_at(block, width):
    return pl.ds(pl.multiple_of(block * width, width), width)


def conv_rows(pad_ref, start, size, filt):
    total = None
    block = pad_ref[pl.ds(start, size + PADR), :]
    for i in range(4):
        term = filt[i] * block[PADR - 3 + i : PADR - 3 + i + size]
        total = term if total is None else total + term
    return total


def chunk_decay(logs, n):
    rows, cols = iotas(n)
    lower = jnp.where(rows >= cols, 1.0, 0.0).astype(f32)
    wide = jnp.broadcast_to(logs, (n, 128))
    h0 = wide.astype(bf16)
    r1 = wide - h0.astype(f32)
    h1 = r1.astype(bf16)
    h2 = (r1 - h1.astype(f32)).astype(bf16)
    col = (mm(lower, h0) + (mm(lower, h1) + mm(lower, h2)))[:, :1]
    row = (mm(h0, lower, 0, 1) + (mm(h1, lower, 0, 1) + mm(h2, lower, 0, 1)))[:1, :]
    return col, row


def suffix_sum(vals, n):
    rows, cols = iotas(n)
    upper = jnp.where(cols >= rows, 1.0, 0.0).astype(f32)
    wide = jnp.broadcast_to(vals, (n, 128))
    h0 = wide.astype(bf16)
    r1 = wide - h0.astype(f32)
    h1 = r1.astype(bf16)
    h2 = (r1 - h1.astype(f32)).astype(bf16)
    return (mm(upper, h0) + (mm(upper, h1) + mm(upper, h2)))[:, :1]


def load_padded(pad_ref, src_ref):
    pad_ref[0:PADR, :] = jnp.zeros((PADR, pad_ref.shape[1]), f32)
    pad_ref[PADR : PADR + src_ref.shape[0], :] = src_ref[...].astype(f32)


def fill_vectors(length, qpad, kpad, vpad, fq, fk, fv, qs, ks, vs):
    def body(t, _):
        start = pl.multiple_of(t * TILE, TILE)
        for pad, filt, dst, scale in ((qpad, fq, qs, 256 ** (-0.5)), (kpad, fk, ks, 1.0)):
            y = conv_rows(pad, start, TILE, filt)
            a = y * sigm(y)
            n = a * lax.rsqrt(jnp.sum(a * a, axis=1, keepdims=True) + 1e-06)
            dst[pl.ds(start, TILE), :] = (n * scale).astype(dst.dtype)
        y = conv_rows(vpad, start, TILE, fv)
        vs[pl.ds(start, TILE), :] = y * sigm(y)
        return 0

    lax.fori_loop(0, length // TILE, body, 0)


def beta_decay(h, heads, length, live_len, bd, log_ref, bias_ref):
    bp = pick(bd, h)
    dp = pick(bd, heads + h)
    live = (lax.broadcasted_iota(jnp.int32, (length, 1), 0) < live_len).astype(f32)
    rate = jnp.exp(pick(log_ref[0:1, :], h))
    sb = sigm(bp)
    zp = dp + pick(bias_ref[0:1, :], h)
    return sb, live, rate, zp


def fwd_kernel(
    heads, len_ref, q_ref, k_ref, v_ref, g_ref, bd_ref, fq_ref, fk_ref, fv_ref, log_ref, bias_ref,
    gain_ref, gated_ref, inv_ref, u_ref, mixed_ref, state_ref, qpad, kpad, vpad, qs, ks, vs,
):
    h = pl.program_id(0)
    length = q_ref.shape[0]
    chunks = length // CH
    load_padded(qpad, q_ref)
    load_padded(kpad, k_ref)
    load_padded(vpad, v_ref)
    fill_vectors(
        length, qpad, kpad, vpad, taps(fq_ref), taps(fk_ref), taps(fv_ref), qs, ks, vs
    )
    sb, live, rate, zp = beta_decay(h, heads, length, len_ref[0], bd_ref[...], log_ref, bias_ref)
    beta = sb * live
    logs = -rate * softplus(zp)
    rows, cols = iotas(CH)
    kept = []
    mats = []
    for n in range(chunks):
        part = slice(n * CH, (n + 1) * CH)
        col, row = chunk_decay(logs[part], CH)
        gaps = col - row
        decay = jnp.where(rows >= cols, jnp.exp(jnp.where(rows >= cols, gaps, 0.0)), 0.0)
        kf = ks[part, :]
        gram = mm3(kf, kf, 1, 1)
        mats.append(jnp.where(rows > cols, beta[part] * decay * gram, 0.0))
        kept.append((part, col, decay))
    inverses = unit_lower_inverses(mats)
    state = None
    for n in range(chunks):
        part, col, decay = kept[n]
        kf = ks[part, :]
        qf = qs[part, :]
        inv_ref[0, part, :] = inverses[n].astype(inv_ref.dtype)
        grow = jnp.exp(col)
        rhs = vs[part, :]
        if state is not None:
            rhs = rhs - grow * mm(kf, state)
        u = mm3(inverses[n], beta[part] * rhs)
        u_ref[part, :] = u.astype(u_ref.dtype)
        scores = mm(qf, kf, 1, 1) * decay
        out = mm(scores, u)
        if state is not None:
            out = out + grow * mm(qf, state)
        mixed_ref[part, :] = out
        if n + 1 < chunks:
            last = col[CH - 1 :, :]
            add = mm(kf * jnp.exp(last - col), u, 0, 0)
            state = add if state is None else jnp.exp(last) * state + add
            state_ref[0, n] = state
    gain = gain_ref[0:1, :]
    live_len = len_ref[0]

    def finish(t, _):
        start = pl.multiple_of(t * TILE, TILE)
        sl = pl.ds(start, TILE)
        m = mixed_ref[sl, :]
        gp = g_ref[sl, :].astype(f32)
        pos = start + lax.broadcasted_iota(jnp.int32, (TILE, 1), 0)
        alive = (pos < live_len).astype(f32)
        r = lax.rsqrt(jnp.mean(m * m, axis=1, keepdims=True) + 1e-05)
        gated_ref[sl, :] = (m * r * gain * (gp * sigm(gp)) * alive).astype(bf16)
        return 0

    lax.fori_loop(0, length // TILE, finish, 0)


def bwd_kernel(
    heads, len_ref, q_ref, k_ref, v_ref, g_ref, bd_ref, fq_ref, fk_ref, fv_ref, log_ref, bias_ref,
    gain_ref, inv_ref, u_ref, mixed_ref, state_ref, dg_ref,
    dpre_out, dfq_out, dfk_out, dfv_out, dgain_out, dsmall_out,
    qpad, kpad, vpad, qs, ks, vs, dos, dqs, dks, dvs, dbds,
):
    h = pl.program_id(0)
    length = q_ref.shape[0]
    chunks = length // CH
    load_padded(qpad, q_ref)
    load_padded(kpad, k_ref)
    load_padded(vpad, v_ref)
    fq, fk, fv = taps(fq_ref), taps(fk_ref), taps(fv_ref)
    fill_vectors(length, qpad, kpad, vpad, fq, fk, fv, qs, ks, vs)
    live_len = len_ref[0]
    gain = gain_ref[0:1, :]

    @pl.when(h == 0)
    def _():
        dgain_out[...] = jnp.zeros(dgain_out.shape, f32)
        dbds[...] = jnp.zeros(dbds.shape, f32)
        dsmall_out[...] = jnp.zeros(dsmall_out.shape, f32)

    def gate_back(t, acc):
        start = pl.multiple_of(t * TILE, TILE)
        sl = pl.ds(start, TILE)
        m = mixed_ref[sl, :]
        gp = g_ref[sl, :].astype(f32)
        pos = start + lax.broadcasted_iota(jnp.int32, (TILE, 1), 0)
        alive = (pos < live_len).astype(f32)
        r = lax.rsqrt(jnp.mean(m * m, axis=1, keepdims=True) + 1e-05)
        n = m * r
        t_ = dg_ref[sl, :].astype(f32) * alive
        s = sigm(gp)
        act = gp * s
        tn = t_ * n
        dpre_out[sl, lanes_at(2 * heads + h, 512)] = (
            tn * gain * (s + act * (1.0 - s))
        ).astype(bf16)
        dn = t_ * gain * act
        dos[sl, :] = r * (dn - n * jnp.mean(dn * n, axis=1, keepdims=True))
        return acc + jnp.sum((tn * act).reshape(TILE // 8, 8, tn.shape[1]), axis=0)

    dgain = lax.fori_loop(0, length // TILE, gate_back, jnp.zeros((8, gain.shape[1]), f32))
    dgain_out[...] += dgain

    sb, live, rate, zp = beta_decay(h, heads, length, live_len, bd_ref[...], log_ref, bias_ref)
    beta = sb * live
    sp = softplus(zp)
    logs = -rate * sp
    rows, cols = iotas(CH)
    incl = rows >= cols
    ones = jnp.ones((CH, 128), f32)
    dstate = None
    dbetas = [None] * chunks
    dlogs = [None] * chunks
    for n in reversed(range(chunks)):
        part = slice(n * CH, (n + 1) * CH)
        col, row = chunk_decay(logs[part], CH)
        gaps = col - row
        decay = jnp.where(incl, jnp.exp(jnp.where(incl, gaps, 0.0)), 0.0)
        grow = jnp.exp(col)
        last = col[CH - 1 :, :]
        kf = ks[part, :]
        qf = qs[part, :]
        u = u_ref[part, :].astype(f32)
        inv = inv_ref[0, part, :]
        do = dos[part, :]
        b = beta[part]
        gram = mm(kf, kf, 1, 1)
        strict_decay = jnp.where(rows > cols, decay, 0.0)
        scores = mm(qf, kf, 1, 1) * decay
        m_all = mm(do, u, 1, 1)
        du = mm(scores, do, 0, 0)
        tail = jnp.exp(last - col)
        if dstate is not None:
            kend = kf * tail
            du = du + mm(kend, dstate)
        dr = mm(inv, du, 0, 0)
        dvs[part, :] = b * dr
        da = mm(dr, u, 1, 1)
        da_dec = -da * strict_decay
        da_gram = da_dec * gram
        dbeta = jnp.sum(da_gram, axis=1, keepdims=True)
        msc = m_all * scores
        both = msc + b * da_gram
        rs = jnp.sum(both, axis=1, keepdims=True)
        both_h, both_l = split2(both)
        cs = (mm(both_h, ones, 0, 0) + mm(both_l, ones, 0, 0))[:, :1]
        dc = rs - cs
        dqk = m_all * decay
        dgram = b * da_dec
        dq = mm(dqk, kf)
        dk = mm(dqk, qf, 0, 0) + mm(dgram, kf) + mm(dgram, kf, 0, 0)
        rest = vs[part, :]
        dlast = None
        if n > 0:
            state = state_ref[0, n - 1]
            kst = mm(kf, state)
            qst = mm(qf, state)
            rest = rest - grow * kst
            dkst = -(b * grow) * dr
            dqst = grow * do
            dk = dk + mm(dkst, state, 1, 1)
            dq = dq + mm(dqst, state, 1, 1)
            dc = dc + jnp.sum(dkst * kst + dqst * qst, axis=1, keepdims=True)
            dprev = mm(kf, dkst, 0, 0) + mm(qf, dqst, 0, 0)
        dbetas[n] = dbeta + jnp.sum(dr * rest, axis=1, keepdims=True)
        if dstate is not None:
            dkend = mm(u, dstate, 1, 1)
            dk = dk + dkend * tail
            w = jnp.sum(dkend * kend, axis=1, keepdims=True)
            dc = dc - w
            dlast = jnp.sum(w, axis=0, keepdims=True)
            if n > 0:
                scale = jnp.exp(last)
                dprev = dprev + scale * dstate
                dlast = dlast + scale * jnp.sum(
                    jnp.sum(dstate * state, axis=1, keepdims=True), axis=0, keepdims=True
                )
        dlog = suffix_sum(dc, CH)
        if dlast is not None:
            dlog = dlog + dlast
        dlogs[n] = dlog
        dqs[part, :] = dq
        dks[part, :] = dk
        if n > 0:
            dstate = dprev
    dbeta = jnp.concatenate(dbetas, axis=0)
    dlog = jnp.concatenate(dlogs, axis=0)
    dbp = dbeta * live * sb * (1.0 - sb)
    dzp = -rate * dlog * sigm(zp)
    lanes = lax.broadcasted_iota(jnp.int32, (length, 128), 1)
    dbds[...] += jnp.where(lanes == h, dbp, 0.0) + jnp.where(lanes == heads + h, dzp, 0.0)

    @pl.when(h == heads - 1)
    def _():
        dpre_out[:, 12 * heads * 128 : (12 * heads + 1) * 128] = dbds[...].astype(bf16)

    small_lane = lax.broadcasted_iota(jnp.int32, (8, 128), 1)
    small_row = lax.broadcasted_iota(jnp.int32, (8, 128), 0)
    at_head = small_lane == h
    dsmall_out[...] += jnp.where(
        at_head & (small_row == 0), jnp.sum(dlog * logs, axis=0, keepdims=True), 0.0
    ) + jnp.where(at_head & (small_row == 1), jnp.sum(dzp, axis=0, keepdims=True), 0.0)

    def pre_back(t, _):
        start = pl.multiple_of(t * TILE, TILE)
        sl = pl.ds(start, TILE)
        for pad, filt, dref, scale in ((qpad, fq, dqs, 256 ** (-0.5)), (kpad, fk, dks, 1.0)):
            y = conv_rows(pad, start, TILE, filt)
            s = sigm(y)
            a = y * s
            r = lax.rsqrt(jnp.sum(a * a, axis=1, keepdims=True) + 1e-06)
            nn = a * r
            dn = dref[sl, :] * scale
            da_ = r * (dn - nn * jnp.sum(dn * nn, axis=1, keepdims=True))
            dref[sl, :] = da_ * (s + a * (1.0 - s))
        y = conv_rows(vpad, start, TILE, fv)
        s = sigm(y)
        dvs[sl, :] = dvs[sl, :] * (s + y * s * (1.0 - s))
        return 0

    lax.fori_loop(0, length // TILE, pre_back, 0)
    for dref in (dqs, dks, dvs):
        dref[length : length + PADR, :] = jnp.zeros((PADR, dref.shape[1]), f32)

    for pad, filt, dref, first, fout in (
        (qpad, fq, dqs, h, dfq_out),
        (kpad, fk, dks, heads + h, dfk_out),
        (vpad, fv, dvs, heads + h, dfv_out),
    ):
        width = dref.shape[1]

        def conv_back(t, accs, pad=pad, filt=filt, dref=dref, first=first, width=width):
            start = pl.multiple_of(t * TILE, TILE)
            dx = None
            new = []
            dys = dref[pl.ds(start, TILE + PADR), :]
            xs = pad[pl.ds(start, TILE + PADR), :]
            dy = dys[:TILE]
            for i in range(4):
                term = filt[i] * dys[3 - i : 3 - i + TILE]
                dx = term if dx is None else dx + term
                prod = dy * xs[PADR - 3 + i : PADR - 3 + i + TILE]
                new.append(accs[i] + jnp.sum(prod.reshape(TILE // 8, 8, width), axis=0))
            dpre_out[pl.ds(start, TILE), lanes_at(first, width)] = dx.astype(bf16)
            return tuple(new)

        accs = lax.fori_loop(
            0, length // TILE, conv_back, tuple(jnp.zeros((8, width), f32) for _ in range(4))
        )
        for i in range(4):
            fout[i : i + 1, :] = jnp.sum(accs[i], axis=0, keepdims=True)


def col_spec(length, width, first=0):
    return pl.BlockSpec((length, width), lambda h: (0, first + h))


def whole_spec(shape):
    return pl.BlockSpec(shape, lambda h: (0,) * len(shape))


def front_specs(length, heads):
    return [
        pl.BlockSpec(memory_space=pltpu.SMEM),
        col_spec(length, 256),
        col_spec(length, 256, heads),
        col_spec(length, 512, heads),
        col_spec(length, 512, 2 * heads),
        pl.BlockSpec((length, 128), lambda h: (0, 12 * heads)),
        col_spec(4, 256),
        col_spec(4, 256),
        col_spec(4, 512),
        whole_spec((1, 128)),
        whole_spec((1, 128)),
        whole_spec((1, 512)),
    ]


def mixer_forward(heads, lens, pre, fq, fk, fv, logs, bias, gain):
    length = pre.shape[0]
    chunks = length // CH
    kept = max(1, chunks - 1)
    return pl.pallas_call(
        functools.partial(fwd_kernel, heads),
        grid=(heads,),
        in_specs=front_specs(length, heads),
        out_specs=[
            col_spec(length, 512),
            pl.BlockSpec((1, length, CH), lambda h: (h, 0, 0)),
            col_spec(length, 512),
            col_spec(length, 512),
            pl.BlockSpec((1, kept, 256, 512), lambda h: (h, 0, 0, 0)),
        ],
        out_shape=[
            jax.ShapeDtypeStruct((length, heads * 512), bf16),
            jax.ShapeDtypeStruct((heads, length, CH), bf16),
            jax.ShapeDtypeStruct((length, heads * 512), bf16),
            jax.ShapeDtypeStruct((length, heads * 512), f32),
            jax.ShapeDtypeStruct((heads, kept, 256, 512), f32),
        ],
        scratch_shapes=[
            pltpu.VMEM((length + PADR, 256), f32),
            pltpu.VMEM((length + PADR, 256), f32),
            pltpu.VMEM((length + PADR, 512), f32),
            pltpu.VMEM((length, 256), f32),
            pltpu.VMEM((length, 256), f32),
            pltpu.VMEM((length, 512), f32),
        ],
        compiler_params=pltpu.CompilerParams(vmem_limit_bytes=50 * 1024 * 1024),
        name="mixer_forward",
    )(lens, pre, pre, pre, pre, pre, fq, fk, fv, logs, bias, gain)


def mixer_backward(heads, lens, pre, fq, fk, fv, logs, bias, gain, saved, dgated):
    length = pre.shape[0]
    chunks = length // CH
    kept = max(1, chunks - 1)
    inv, u, mixed, states = saved
    return pl.pallas_call(
        functools.partial(bwd_kernel, heads),
        grid=(heads,),
        in_specs=front_specs(length, heads)
        + [
            pl.BlockSpec((1, length, CH), lambda h: (h, 0, 0)),
            col_spec(length, 512),
            col_spec(length, 512),
            pl.BlockSpec((1, kept, 256, 512), lambda h: (h, 0, 0, 0)),
            col_spec(length, 512),
        ],
        out_specs=[
            whole_spec((length, pre.shape[1])),
            col_spec(4, 256), col_spec(4, 256), col_spec(4, 512),
            whole_spec((8, 512)), whole_spec((8, 128)),
        ],
        out_shape=[
            jax.ShapeDtypeStruct(pre.shape, bf16),
            jax.ShapeDtypeStruct((4, heads * 256), f32),
            jax.ShapeDtypeStruct((4, heads * 256), f32),
            jax.ShapeDtypeStruct((4, heads * 512), f32),
            jax.ShapeDtypeStruct((8, 512), f32),
            jax.ShapeDtypeStruct((8, 128), f32),
        ],
        scratch_shapes=[
            pltpu.VMEM((length + PADR, 256), f32),
            pltpu.VMEM((length + PADR, 256), f32),
            pltpu.VMEM((length + PADR, 512), f32),
            pltpu.VMEM((length, 256), f32),
            pltpu.VMEM((length, 256), f32),
            pltpu.VMEM((length, 512), f32),
            pltpu.VMEM((length, 512), f32),
            pltpu.VMEM((length + PADR, 256), f32),
            pltpu.VMEM((length + PADR, 256), f32),
            pltpu.VMEM((length + PADR, 512), f32),
            pltpu.VMEM((length, 128), f32),
        ],
        compiler_params=pltpu.CompilerParams(vmem_limit_bytes=50 * 1024 * 1024),
        name="mixer_backward",
    )(lens, pre, pre, pre, pre, pre, fq, fk, fv, logs, bias, gain, inv, u, mixed, states, dgated)


MESH = pl.DeviceIdType.MESH


def column_chunks(widths, size, layers):
    size = size * max(1, layers // 4)
    out = []
    for a, width in enumerate(widths):
        units = width // 128
        count = max(1, -(-width // size))
        lo = 0
        for i in range(count):
            hi = units * (i + 1) // count
            out.append((a, lo * 128, (hi - lo) * 128))
            lo = hi
    return out


def placement():
    spot = lax.axis_index("dp")
    return spot, lax.rem(spot, 2), lax.rem(lax.div(spot, 2), 2), lax.div(spot, 4)


def greet(partners):
    barrier = pltpu.get_barrier_semaphore()
    for partner in partners:
        pl.semaphore_signal(barrier, inc=1, device_id={"dp": partner}, device_id_type=MESH)
    pl.semaphore_wait(barrier, len(partners))


def remote(src, dst, send, recv, target):
    return pltpu.make_async_remote_copy(
        src_ref=src, dst_ref=dst, send_sem=send, recv_sem=recv,
        device_id={"dp": target}, device_id_type=MESH,
    )


def gather_kernel(layers, chunks, count, pairs, *refs):
    srcs, outs = refs[: count + pairs], refs[count + pairs : 2 * (count + pairs)]
    own_sem, us, ur, ds, dr, ys, yr, cs, cr, ps, pr, pair_sem = refs[2 * (count + pairs) :]
    rows = srcs[0].shape[0]
    spot, core, side, layer = placement()
    turn = lax.axis_index("tensor")
    at = lambda z, y, c: 4 * z + 2 * y + c
    y_to, c_to = at(layer, 1 - side, core), at(layer, side, 1 - core)
    has_up, has_down = layer < layers - 1, layer > 0
    barrier = pltpu.get_barrier_semaphore()
    around = [4 * lax.rem(layer + s, layers) + 2 * side + core for s in (1, layers - 1)]
    for partner in [y_to, c_to] + around:
        pl.semaphore_signal(barrier, inc=1, device_id={"dp": partner}, device_id_type=MESH)
    pl.semaphore_signal(barrier, inc=1, device_id={"tensor": 1 - turn}, device_id_type=MESH)
    pl.semaphore_wait(barrier, 5)

    def place(j, origin):
        a, lo, width, _ = chunks[j]
        start = pl.multiple_of(origin * rows, rows)
        return outs[a].at[pl.ds(start, rows), lo : lo + width]

    def own(j):
        a, lo, width, _ = chunks[j]
        return srcs[a].at[:, lo : lo + width]

    def up_copy(j, k, half, origin, src):
        i = 2 * k + half
        return remote(src, place(j, origin), us.at[j, i], ur.at[j, i], spot + 4)

    def down_copy(j, k, half, origin, src):
        i = 2 * k + half
        return remote(src, place(j, origin), ds.at[j, i], dr.at[j, i], spot - 4)

    def y_copy(j, slot, origin, src):
        return remote(src, place(j, origin), ys.at[j, slot], yr.at[j, slot], y_to)

    def c_copy(j, slot, origin, src):
        return remote(src, place(j, origin), cs.at[j, slot], cr.at[j, slot], c_to)

    number = len(chunks)
    narrow = [j for j in range(number) if not chunks[j][3]]
    early = [j for j in range(number) if chunks[j][3]]
    keep = []
    for p in range(pairs):
        half_rows = srcs[count + p].shape[0]
        spot_rows = pl.ds(pl.multiple_of(turn * half_rows, half_rows), half_rows)
        copy = pltpu.make_async_remote_copy(
            src_ref=srcs[count + p], dst_ref=outs[count + p].at[spot_rows, :],
            send_sem=ps.at[p], recv_sem=pr.at[p],
            device_id={"tensor": 1 - turn}, device_id_type=MESH,
        )
        copy.start()
        local_copy = pltpu.make_async_copy(
            srcs[count + p], outs[count + p].at[spot_rows, :], pair_sem.at[p]
        )
        local_copy.start()
        keep.append((copy, local_copy))

    def send_z(j, half, origin, src):
        @pl.when(has_up)
        def _():
            up_copy(j, 0, half, origin, src).start()

        @pl.when(has_down)
        def _():
            down_copy(j, 0, half, origin, src).start()

    locals_ = []
    for j in early + narrow:
        y_copy(j, 0, spot, own(j)).start()
        send_z(j, 0, spot, own(j))
        c_copy(j, 0, spot, own(j)).start()
        copy = pltpu.make_async_copy(own(j), place(j, spot), own_sem.at[j])
        copy.start()
        locals_.append(copy)
    across = at(layer, 1 - side, core)

    def take_z(j, k, half):
        there = lax.rem(side + half, 2)
        for sign, fits, more, copy in (
            (-1, layer >= k + 1, has_up, up_copy),
            (1, layer + k + 1 < layers, has_down, down_copy),
        ):

            @pl.when(fits)
            def _(sign=sign, more=more, copy=copy):
                origin = at(layer + sign * (k + 1), there, core)
                here = place(j, origin)
                copy(j, k, half, origin, here).wait_recv()

                @pl.when(more)
                def _():
                    copy(j, k + 1, half, origin, here).start()

                slot = 2 * k + (1 if sign < 0 else 2)
                if not chunks[j][3]:
                    y_copy(j, slot, origin, here).start()
                c_copy(j, slot if half == 0 else slot + 2 * layers - 1, origin, here).start()

    def take_y(j, k):
        slots = [(0, None, None)] if k == 0 else [
            (2 * k - 1, layer >= k, -1), (2 * k, layer + k < layers, 1)
        ]
        for slot, fits, sign in slots:
            shift = 0 if sign is None else sign * k

            def body(slot=slot, shift=shift):
                origin = at(layer + shift, 1 - side, core)
                here = place(j, origin)
                y_copy(j, slot, origin, here).wait_recv()
                c_copy(j, 2 * layers - 1 + slot, origin, here).start()

            if fits is None:
                body()
            else:
                pl.when(fits)(body)

    for j in early:
        y_copy(j, 0, across, own(j)).wait_recv()
        send_z(j, 1, across, place(j, across))
        c_copy(j, 2 * layers - 1, across, place(j, across)).start()
    for k in range(layers):
        if k < layers - 1:
            for j in early:
                for half in range(2):
                    take_z(j, k, half)
            for j in narrow:
                take_z(j, k, 0)
        if k > 0:
            for j in narrow:
                take_y(j, k - 1)
    for j in narrow:
        take_y(j, layers - 1)

    for copy, local_copy in keep:
        local_copy.wait()
        copy.wait()
    for copy in locals_:
        copy.wait()
    for j in range(number):
        wide = chunks[j][3]
        me = own(j)
        for half in range(2 if wide else 1):
            for k in range(layers - 1):

                @pl.when(has_up & (layer >= k))
                def _(k=k, half=half):
                    up_copy(j, k, half, spot, me).wait_send()

                @pl.when(has_down & (layer + k < layers))
                def _(k=k, half=half):
                    down_copy(j, k, half, spot, me).wait_send()

        def settle(slot, shift):
            if slot == 0 or not wide:
                y_copy(j, slot, spot, me).wait_send()
            for half in range(2):
                origin = at(layer + shift, lax.rem(side + half, 2), 1 - core)
                c_copy(j, slot + half * (2 * layers - 1), origin, place(j, origin)).wait()

        settle(0, 0)
        for k in range(1, layers):
            pl.when(layer >= k)(functools.partial(settle, 2 * k - 1, -k))
            pl.when(layer + k < layers)(functools.partial(settle, 2 * k, k))


def mark_early(chunks, share):
    total = sum(c[2] for c in chunks)
    marked, done = [], 0
    for c in chunks:
        early = done + c[2] <= share * total + 64
        done += c[2] if early else 0
        marked.append(c + (early,))
    return marked


def gather_all(shards, pairs, devices, ident, size=1600, share=0):
    rows = shards[0].shape[0]
    layers = devices // 4
    chunks = mark_early(column_chunks([s.shape[1] for s in shards], size, layers), share)
    n = len(chunks)
    sem = lambda *shape: pltpu.SemaphoreType.DMA(shape)
    z_slots, slots = 2 * layers, 2 * layers - 1
    arrays = tuple(shards) + tuple(pairs)
    return pl.pallas_call(
        functools.partial(gather_kernel, layers, chunks, len(shards), len(pairs)),
        in_specs=[pl.BlockSpec(memory_space=pl.ANY)] * len(arrays),
        out_specs=[pl.BlockSpec(memory_space=pl.ANY)] * len(arrays),
        out_shape=[jax.ShapeDtypeStruct((devices * rows, s.shape[1]), s.dtype) for s in shards]
        + [jax.ShapeDtypeStruct((2 * p.shape[0], p.shape[1]), p.dtype) for p in pairs],
        scratch_shapes=[
            sem(n), sem(n, z_slots), sem(n, z_slots), sem(n, z_slots), sem(n, z_slots),
            sem(n, slots), sem(n, slots), sem(n, 2 * slots), sem(n, 2 * slots),
            sem(max(1, len(pairs))), sem(max(1, len(pairs))), sem(max(1, len(pairs))),
        ],
        compiler_params=pltpu.CompilerParams(collective_id=ident, has_side_effects=True),
        name="gather_rows",
    )(*arrays)


def scatter_kernel(layers, chunks, dots, *refs):
    n_held = max([c[0] for c in chunks if c[3] is None]) + 1
    srcs, lefts = refs[:n_held], refs[n_held : n_held + dots]
    rights = refs[n_held + dots : n_held + 2 * dots]
    sent_ref, out, come_ref = refs[n_held + 2 * dots : n_held + 2 * dots + 3]
    (stage, sends, buf1, buf2, buf3, own_sem, cs, cr, ys, yr, zs, zr, pair_send,
     pair_recv) = refs[n_held + 2 * dots + 3 :]
    rows = out.shape[0]
    spot, core, side, layer = placement()
    turn = lax.axis_index("tensor")
    at = lambda z, y, c: 4 * lax.rem(z + layers, layers) + 2 * y + c
    z_to = [at(layer + k, side, core) for k in range(1, layers)]
    y_to, c_to = at(layer, 1 - side, core), at(layer, side, 1 - core)
    barrier = pltpu.get_barrier_semaphore()
    for partner in z_to + [y_to, c_to]:
        pl.semaphore_signal(barrier, inc=1, device_id={"dp": partner}, device_id_type=MESH)
    pl.semaphore_signal(barrier, inc=1, device_id={"tensor": 1 - turn}, device_id_type=MESH)
    pl.semaphore_wait(barrier, layers + 2)
    number = len(chunks)
    firsts = []
    total = 0
    for chunk in chunks:
        firsts.append(total)
        total += chunk[2]
    pair = pltpu.make_async_remote_copy(
        src_ref=sent_ref, dst_ref=come_ref, send_sem=pair_send, recv_sem=pair_recv,
        device_id={"tensor": 1 - turn}, device_id_type=MESH,
    )
    pair.start()

    def cols(j):
        return slice(firsts[j], firsts[j] + chunks[j][2])

    def c_copy(j):
        a, lo, width, which = chunks[j]
        if which is None:
            src = srcs[a].at[:, 1 - core, :, lo : lo + width]
        else:
            src = sends.at[j % 3, :, :, 0:width]
        return remote(src, buf1.at[:, :, cols(j)], cs.at[j], cr.at[j], c_to)

    def own_copy(j):
        a, lo, width, _ = chunks[j]
        return pltpu.make_async_copy(
            srcs[a].at[:, core, :, lo : lo + width],
            stage.at[j % 3, :, :, 0:width], own_sem.at[j],
        )

    def y_copy(j, m):
        block = 2 * lax.rem(layer + m, layers) + 1 - side
        return remote(
            buf1.at[block, :, cols(j)], buf2.at[m, :, cols(j)], ys.at[j, m], yr.at[j, m], y_to
        )

    def z_copy(j, k):
        return remote(
            buf2.at[k, :, cols(j)], buf3.at[k - 1, :, cols(j)], zs.at[j, k - 1], zr.at[j, k - 1],
            z_to[k - 1],
        )

    def produce(j):
        a, lo, width, which = chunks[j]
        if which is None:
            own_copy(j).start()
        else:
            if j >= 3:
                c_copy(j - 3).wait_send()
            right = rights[which][:, lo : lo + width]

            wide = 256
            per = wide // (2 * rows)

            def body(g, _):
                left = lefts[which][:, pl.ds(pl.multiple_of(g * wide, wide), wide)]
                both = mm(left, right, 0, 0)
                for i in range(per):
                    low_half = both[2 * i * rows : (2 * i + 1) * rows]
                    high_half = both[(2 * i + 1) * rows : (2 * i + 2) * rows]
                    mine = jnp.where(core == 0, low_half, high_half)
                    other = jnp.where(core == 0, high_half, low_half)
                    stage[j % 3, g * per + i, :, 0:width] = mine.astype(bf16)
                    sends[j % 3, g * per + i, :, 0:width] = other.astype(bf16)
                return 0

            lax.fori_loop(0, 2 * layers // per, body, 0)
        c_copy(j).start()

    for j in range(min(2, number)):
        produce(j)

    def first(j):
        width = chunks[j][2]
        if chunks[j][3] is None:
            own_copy(j).wait()
        c_copy(j).wait_recv()

        def body(b, _):
            mine = stage[j % 3, b, :, 0:width].astype(f32)
            buf1[b, :, cols(j)] = (buf1[b, :, cols(j)].astype(f32) + mine).astype(bf16)
            return 0

        lax.fori_loop(0, 2 * layers, body, 0)
        for m in list(range(1, layers)) + [0]:
            y_copy(j, m).start()
        if j + 2 < number:
            produce(j + 2)

    def second(j):
        for m in list(range(1, layers)) + [0]:
            y_copy(j, m).wait_recv()
            block = 2 * lax.rem(layer + m, layers) + side
            mine = buf1[block, :, cols(j)].astype(f32)
            buf2[m, :, cols(j)] = (buf2[m, :, cols(j)].astype(f32) + mine).astype(bf16)
            if m:
                z_copy(j, m).start()

    def third(j):
        total = buf2[0, :, cols(j)].astype(f32)
        for k in range(1, layers):
            z_copy(j, k).wait_recv()
            total = total + buf3[k - 1, :, cols(j)].astype(f32)
        out[:, cols(j)] = total

    for j in range(number + 4):
        if j < number:
            first(j)
        if 0 <= j - 2 < number:
            second(j - 2)
        if 0 <= j - 4 < number:
            third(j - 4)
    for j in range(number):
        later = j + 3 < number and chunks[j + 3][3] is not None
        if not later:
            c_copy(j).wait_send()
        for m in range(layers):
            y_copy(j, m).wait_send()
        for k in range(1, layers):
            z_copy(j, k).wait_send()
    pair.wait()


def scatter_sum(held, products, tail, sent, devices, ident, size=512):
    parts = [held, tail]
    rows = held.shape[0] // devices
    layers = devices // 4
    widths = [held.shape[1]] + [w for _, _, w in products] + [tail.shape[1]]
    chunks = []
    for a, lo, width in column_chunks(widths, size, 4):
        if a == 0:
            chunks.append((0, lo, width, None))
        elif a <= len(products):
            chunks.append((a, lo, width, a - 1))
        else:
            chunks.append((1, lo, width, None))
    n = len(chunks)
    width = sum(widths)
    widest = max(c[2] for c in chunks)
    sem = lambda *shape: pltpu.SemaphoreType.DMA(shape)
    hbm, vmem = pl.BlockSpec(memory_space=pl.ANY), pl.BlockSpec(memory_space=pltpu.VMEM)
    return pl.pallas_call(
        functools.partial(scatter_kernel, layers, chunks, len(products)),
        in_specs=[hbm] * 2 + [vmem] * (2 * len(products)) + [hbm],
        out_specs=[vmem, hbm],
        out_shape=[
            jax.ShapeDtypeStruct((rows, width), f32),
            jax.ShapeDtypeStruct(sent.shape, sent.dtype),
        ],
        scratch_shapes=[
            pltpu.VMEM((3, 2 * layers, rows, widest), bf16),
            pltpu.VMEM((3, 2 * layers, rows, widest), bf16),
            pltpu.VMEM((2 * layers, rows, width), bf16),
            pltpu.VMEM((layers, rows, width), bf16),
            pltpu.VMEM((layers - 1, rows, width), bf16),
            sem(n), sem(n), sem(n), sem(n, layers), sem(n, layers),
            sem(n, layers - 1), sem(n, layers - 1),
            pltpu.SemaphoreType.DMA, pltpu.SemaphoreType.DMA,
        ],
        compiler_params=pltpu.CompilerParams(
            collective_id=ident, has_side_effects=True, vmem_limit_bytes=61 * 1024 * 1024
        ),
        name="scatter_sum",
    )(
        *[p.reshape(devices // 2, 2, rows, p.shape[1]) for p in parts],
        *[p[0] for p in products],
        *[p[1] for p in products],
        sent,
    )


EXTRA = 128


def rms_scale(values):
    return lax.rsqrt(jnp.mean(values * values, axis=-1, keepdims=True) + 1e-05)


def norm_back(values, gain, grad_normed):
    scale = rms_scale(values)
    unit_vals = values * scale
    grad_unit = grad_normed * gain
    grad_values = scale * (
        grad_unit - unit_vals * jnp.mean(grad_unit * unit_vals, axis=-1, keepdims=True)
    )
    return (grad_values, jnp.sum(grad_normed * unit_vals, axis=0))


def pair_swap(values):
    return lax.ppermute(values, "tensor", [(0, 1), (1, 0)])


def pair_gather(values):
    other = pair_swap(values)
    first = lax.axis_index("tensor") == 0
    return jnp.concatenate(
        [jnp.where(first, values, other), jnp.where(first, other, values)], axis=0
    )


def pair_halves(parts):
    rows = parts.shape[0] // 2
    mine = lax.axis_index("tensor") * rows
    kept = lax.dynamic_slice_in_dim(parts, mine, rows)
    sent = lax.dynamic_slice_in_dim(parts, rows - mine, rows).astype(bf16)
    return kept, sent


def pair_scatter(parts):
    kept, sent = pair_halves(parts)
    return kept + pair_swap(sent).astype(f32)


def dot(a, b, ca=1, cb=0):
    return lax.dot_general(a, b, (((ca,), (cb,)), ((), ())), preferred_element_type=f32)


def high_low(values):
    high = lax.reduce_precision(values, 8, 7)
    return jnp.stack([high, values - high], axis=1).astype(bf16)


def gather_rows(values):
    return lax.all_gather(values, "dp", axis=0, tiled=True)


def scatter_rows(values):
    return lax.psum_scatter(values, "dp", scatter_dimension=0, tiled=True)


def pack_filters(fq, fk, fv, rows):
    flat = jnp.concatenate([fq, fk, fv], axis=2).reshape(-1)
    return flat.reshape(-1, rows).T


def local(
    tokens,
    lengths,
    cotangent,
    gain_in,
    gain_ffn,
    gain_out,
    w_query,
    w_key,
    w_value,
    w_gate,
    w_beta,
    w_decay,
    conv_query,
    conv_key,
    conv_value,
    decay_log,
    decay_bias,
    w_output,
    w_ffn_gate,
    w_ffn_up,
    w_ffn_down,
):
    heads = w_beta.shape[1]
    rows = w_query.shape[0]
    devices = lax.axis_size("dp")
    low = lambda v: v.astype(bf16)
    filters = pack_filters(conv_query, conv_key, conv_value, rows)
    filter_cols = filters.shape[1]
    gains = pair_gather(jnp.concatenate([gain_in, gain_ffn, gain_out])[None])
    n_in, n_out = gain_in.shape[0], gain_out.shape[0]
    pair_out = jnp.pad(gains[:, 2 * n_in :].reshape(-1), (0, rows - 2 * n_out))
    small = jnp.concatenate(
        [
            low(jnp.concatenate([w_beta, w_decay, filters], axis=1)),
            high_low(gains[:, :n_in].reshape(-1)),
            high_low(gains[:, n_in : 2 * n_in].reshape(-1)),
            high_low(pair_out),
        ],
        axis=1,
    )
    small = jnp.pad(small, ((0, 0), (0, EXTRA - small.shape[1])))
    proj_shard = jnp.concatenate(
        [low(w_query), low(w_key), low(w_value), low(w_gate), small], axis=1
    )
    proj, out_t, seq_x, seq_cot = gather_all(
        (proj_shard, low(w_output).T), (tokens, cotangent), devices, 0
    )
    extra_at = 12 * heads * 128
    gain_at = extra_at + 2 * heads + filter_cols
    sides = proj[:, gain_at : gain_at + 6].astype(f32)
    sides = sides[:, 0::2] + sides[:, 1::2]
    full_in, full_ffn = sides[:, 0], sides[:, 1]
    full_out = sides[:, 2].reshape(devices, rows)[:, : 2 * n_out].reshape(1, -1)
    gate_weight = gather_rows(low(w_ffn_gate))
    up_weight = gather_rows(low(w_ffn_up))
    down_t = gather_rows(low(w_ffn_down).T)

    tap_count = conv_query.shape[0]
    piece_q, piece_v = conv_query.shape[2], conv_value.shape[2]
    flat = proj[:, extra_at + 2 * heads : gain_at]
    flat = flat.reshape(devices, rows, filter_cols).transpose(0, 2, 1)
    flat = flat.reshape(devices, tap_count, heads, 2 * piece_q + piece_v).astype(f32)
    flat = flat.transpose(1, 2, 0, 3)
    filt_q = flat[..., :piece_q].reshape(tap_count, -1)
    filt_k = flat[..., piece_q : 2 * piece_q].reshape(tap_count, -1)
    filt_v = flat[..., 2 * piece_q :].reshape(tap_count, -1)

    head_start = lax.axis_index("tensor") * heads
    lane_pad = lambda v: jnp.pad(
        lax.dynamic_slice_in_dim(v, head_start, heads), (0, 128 - heads)
    ).reshape(1, 128)
    local_log, local_bias = lane_pad(decay_log), lane_pad(decay_bias)

    inputs = tokens.astype(f32)
    seq_inputs = seq_x.astype(f32)
    seq_unit = seq_inputs * rms_scale(seq_inputs)
    seq_in = low(seq_unit * full_in)
    pre = dot(seq_in, proj)
    mixer_args = (heads, lengths, pre, filt_q, filt_k, filt_v, local_log, local_bias, full_out)
    gated, *saved = mixer_forward(*mixer_args)
    hidden = inputs + pair_scatter(dot(gated, out_t, 1, 1))
    normed_ffn = low(hidden * rms_scale(hidden) * full_ffn)
    normed_ffn, down_t = lax.optimization_barrier((normed_ffn, down_t))
    seq_ffn = pair_gather(normed_ffn)
    grad_inner = dot(seq_cot, down_t)
    seq_ffn, grad_inner = lax.optimization_barrier((seq_ffn, grad_inner))

    gate_act = dot(seq_ffn, gate_weight)
    up_act = dot(seq_ffn, up_weight)
    sigmoid_gate = jax.nn.sigmoid(gate_act)
    silu_gate = gate_act * sigmoid_gate
    inner = low(silu_gate * up_act)
    grad_gate_act = low(
        grad_inner * up_act * sigmoid_gate * (1.0 + gate_act * (1.0 - sigmoid_gate))
    )
    grad_up_act = low(grad_inner * silu_gate)
    grad_down = low(dot(seq_cot, inner, 0, 0))
    grad_gate_act, grad_up_act, grad_down = lax.optimization_barrier(
        (grad_gate_act, grad_up_act, grad_down)
    )
    down_piece = scatter_rows(grad_down)
    grad_seq_ffn = dot(grad_gate_act, gate_weight, 1, 1) + dot(grad_up_act, up_weight, 1, 1)
    kept_ffn, sent_ffn = pair_halves(grad_seq_ffn)
    sent_ffn, inner = lax.optimization_barrier((sent_ffn, inner))
    kept_out, sent_out = pair_halves(dot(inner, down_t, 1, 1))
    come_ffn, sent_out = lax.optimization_barrier((pair_swap(sent_ffn), sent_out))
    grad_normed_ffn = kept_ffn + come_ffn.astype(f32)
    grad_hidden_norm, grad_gain_ffn = norm_back(hidden, full_ffn, grad_normed_ffn)
    grad_hidden = cotangent.astype(f32) + grad_hidden_norm
    sent_branch, grad_gate_act, grad_up_act = lax.optimization_barrier(
        (low(grad_hidden), grad_gate_act, grad_up_act)
    )
    seq_grad_branch = pair_gather(sent_branch)
    grad_gate_w = low(dot(seq_ffn, grad_gate_act, 0, 0))
    grad_up_w = low(dot(seq_ffn, grad_up_act, 0, 0))
    seq_grad_branch, grad_gate_w, grad_up_w, sent_out = lax.optimization_barrier(
        (seq_grad_branch, grad_gate_w, grad_up_w, sent_out)
    )
    gate_piece = scatter_rows(grad_gate_w)
    come_out = pair_swap(sent_out)

    grad_gated = dot(seq_grad_branch, out_t)
    grad_pre, grad_fq, grad_fk, grad_fv, grad_gain_out, grad_small = mixer_backward(
        *mixer_args, saved, low(grad_gated)
    )
    grad_pre, come_out = lax.optimization_barrier((grad_pre, come_out))
    result = low(hidden + kept_out + come_out.astype(f32))
    grad_seq_in = dot(grad_pre, proj, 1, 1)
    kept_in, sent_in = pair_halves(grad_seq_in)
    extra = dot(seq_in, grad_pre[:, extra_at:], 0, 0)
    by_device = lambda g, piece: g.reshape(tap_count, heads, devices, piece)
    grad_flat = jnp.concatenate(
        [by_device(grad_fq, piece_q), by_device(grad_fk, piece_q), by_device(grad_fv, piece_v)],
        axis=3,
    ).transpose(2, 0, 1, 3)
    grad_flat = grad_flat.reshape(devices, filter_cols, rows).transpose(0, 2, 1)
    grad_flat = low(grad_flat.reshape(devices * rows, filter_cols))
    spread = lambda v: lax.dynamic_update_slice(jnp.zeros_like(decay_log), v, (head_start,))
    grad_decay = jnp.concatenate([spread(grad_small[0, :heads]), spread(grad_small[1, :heads])])
    by_rows = lambda v: jnp.pad(v, ((0, 0), (0, rows - v.shape[1]))).reshape(-1)
    columns = jnp.stack(
        [
            jnp.sum(grad_seq_in * seq_unit, axis=0),
            grad_gain_ffn,
            by_rows(jnp.sum(grad_gain_out, axis=0).reshape(devices, -1)),
            by_rows(jnp.broadcast_to(grad_decay, (devices,) + grad_decay.shape)),
        ],
        axis=1,
    )
    grad_tiny = jnp.concatenate(
        [low(extra[:, : 2 * heads]), grad_flat, low(columns)], axis=1
    )
    grad_tiny = jnp.pad(grad_tiny, ((0, 0), (0, EXTRA - grad_tiny.shape[1])))
    products = (
        (seq_in, grad_pre, extra_at),
        (seq_grad_branch, gated, gated.shape[1]),
    )
    pieces, come_in = scatter_sum(grad_up_w, products, grad_tiny, sent_in, devices, 1)
    ffn_width = grad_up_w.shape[1]
    up_piece, pieces = pieces[:, :ffn_width], pieces[:, ffn_width:]
    grad_normed_in = kept_in + come_in.astype(f32)
    out_width = w_output.shape[0]
    out_piece = pieces[:, extra_at : extra_at + out_width]
    tiny_piece = pieces[:, extra_at + out_width :]

    grad_inputs_norm, _ = norm_back(inputs, full_in, grad_normed_in)
    grad_tokens = grad_hidden + grad_inputs_norm

    sums = tiny_piece[:, 2 * heads + filter_cols : 2 * heads + filter_cols + 4].T
    sums = sums + pair_swap(sums)
    turn = lax.axis_index("tensor")
    take = lambda row, piece: lax.dynamic_slice_in_dim(sums[row], turn * piece, piece)
    n_heads = decay_log.shape[0]

    q_end, k_end = heads * 256, 2 * heads * 256
    v_end, g_end = k_end + heads * 512, k_end + 2 * heads * 512
    grad_filters = tiny_piece[:, 2 * heads : 2 * heads + filter_cols]
    grad_filters = grad_filters.T.reshape(tap_count, heads, 2 * piece_q + piece_v)
    return (
        result,
        grad_tokens,
        take(0, n_in),
        take(1, n_in),
        take(2, n_out),
        pieces[:, :q_end],
        pieces[:, q_end:k_end],
        pieces[:, k_end:v_end],
        pieces[:, v_end:g_end],
        tiny_piece[:, :heads],
        tiny_piece[:, heads : 2 * heads],
        grad_filters[..., :piece_q],
        grad_filters[..., piece_q : 2 * piece_q],
        grad_filters[..., 2 * piece_q :],
        sums[3, :n_heads],
        sums[3, n_heads : 2 * n_heads],
        out_piece.T,
        gate_piece.astype(f32),
        up_piece,
        down_piece.astype(f32).T,
    )


def solution(mesh):
    rows = P(("dp", "tensor"), None)
    spread = P(("dp", "tensor"))
    weight = P("dp", "tensor")
    filters = P(None, "tensor", "dp")
    turned = P("tensor", "dp")
    return jax.shard_map(
        local,
        mesh=mesh,
        in_specs=(rows, P("dp"), rows, spread, spread, spread)
        + (weight,) * 6
        + (filters,) * 3
        + (P(), P(), turned, weight, weight, turned),
        out_specs=(rows, rows, spread, spread, spread)
        + (weight,) * 6
        + (filters,) * 3
        + (P(), P(), turned, weight, weight, turned),
        check_vma=False,
    )
```

```python
import functools
import jax
import jax.numpy as jnp
from jax import lax
from jax.sharding import PartitionSpec as P
from jax.experimental import pallas as pl
from jax.experimental.pallas import tpu as pltpu

CH = 256
TILE = 128
PADR = 8
f32 = jnp.float32
bf16 = jnp.bfloat16


def mm(a, b, ca=1, cb=0):
    return lax.dot_general(
        a.astype(bf16), b.astype(bf16), (((ca,), (cb,)), ((), ())), preferred_element_type=f32
    )


def split2(a):
    high = a.astype(bf16)
    return high, (a - high.astype(f32)).astype(bf16)


def mm3(a, b, ca=1, cb=0):
    ah, al = split2(a)
    bh, bl = split2(b)
    return mm(ah, bh, ca, cb) + (mm(ah, bl, ca, cb) + mm(al, bh, ca, cb))


def iotas(n):
    return (
        lax.broadcasted_iota(jnp.int32, (n, n), 0),
        lax.broadcasted_iota(jnp.int32, (n, n), 1),
    )


def unit_lower_inverses(mats):
    n = mats[0].shape[0]
    rows, cols = iotas(n)
    eye = jnp.where(rows == cols, 1.0, 0.0).astype(f32)
    base = 8
    near = (rows // base) == (cols // base)
    powers = [jnp.where(near, a, 0.0) for a in mats]
    outs = [eye - p for p in powers]
    for _ in range(2):
        powers = [mm3(p, p) for p in powers]
        outs = [x + mm3(x, p) for x, p in zip(outs, powers)]
    size = base
    while size < n:
        wide = ((rows // (2 * size)) == (cols // (2 * size))) & ((rows // size) != (cols // size))
        halves = [mm3(jnp.where(wide, a, 0.0), x) for a, x in zip(mats, outs)]
        outs = [x - mm3(x, h) for x, h in zip(outs, halves)]
        size *= 2
    return outs


def sigm(v):
    return 1.0 / (1.0 + jnp.exp(-v))


def softplus(v):
    return jnp.maximum(v, 0.0) + jnp.log1p(jnp.exp(-jnp.abs(v)))


def pick(block, lane):
    lanes = lax.broadcasted_iota(jnp.int32, block.shape, 1)
    return jnp.sum(jnp.where(lanes == lane, block, 0.0), axis=1, keepdims=True)


def taps(ref):
    return [ref[i : i + 1, :] for i in range(4)]


def lanes_at(block, width):
    return pl.ds(pl.multiple_of(block * width, width), width)


def conv_rows(pad_ref, start, size, filt):
    total = None
    block = pad_ref[pl.ds(start, size + PADR), :]
    for i in range(4):
        term = filt[i] * block[PADR - 3 + i : PADR - 3 + i + size]
        total = term if total is None else total + term
    return total


def chunk_decay(logs, n):
    rows, cols = iotas(n)
    lower = jnp.where(rows >= cols, 1.0, 0.0).astype(f32)
    wide = jnp.broadcast_to(logs, (n, 128))
    h0 = wide.astype(bf16)
    r1 = wide - h0.astype(f32)
    h1 = r1.astype(bf16)
    h2 = (r1 - h1.astype(f32)).astype(bf16)
    col = (mm(lower, h0) + (mm(lower, h1) + mm(lower, h2)))[:, :1]
    row = (mm(h0, lower, 0, 1) + (mm(h1, lower, 0, 1) + mm(h2, lower, 0, 1)))[:1, :]
    return col, row


def suffix_sum(vals, n):
    rows, cols = iotas(n)
    upper = jnp.where(cols >= rows, 1.0, 0.0).astype(f32)
    wide = jnp.broadcast_to(vals, (n, 128))
    h0 = wide.astype(bf16)
    r1 = wide - h0.astype(f32)
    h1 = r1.astype(bf16)
    h2 = (r1 - h1.astype(f32)).astype(bf16)
    return (mm(upper, h0) + (mm(upper, h1) + mm(upper, h2)))[:, :1]


def load_padded(pad_ref, src_ref):
    pad_ref[0:PADR, :] = jnp.zeros((PADR, pad_ref.shape[1]), f32)
    pad_ref[PADR : PADR + src_ref.shape[0], :] = src_ref[...].astype(f32)


def fill_vectors(length, qpad, kpad, vpad, fq, fk, fv, qs, ks, vs):
    def body(t, _):
        start = pl.multiple_of(t * TILE, TILE)
        for pad, filt, dst, scale in ((qpad, fq, qs, 256 ** (-0.5)), (kpad, fk, ks, 1.0)):
            y = conv_rows(pad, start, TILE, filt)
            a = y * sigm(y)
            n = a * lax.rsqrt(jnp.sum(a * a, axis=1, keepdims=True) + 1e-06)
            dst[pl.ds(start, TILE), :] = (n * scale).astype(dst.dtype)
        y = conv_rows(vpad, start, TILE, fv)
        vs[pl.ds(start, TILE), :] = y * sigm(y)
        return 0

    lax.fori_loop(0, length // TILE, body, 0)


def beta_decay(h, heads, length, live_len, bd, log_ref, bias_ref):
    bp = pick(bd, h)
    dp = pick(bd, heads + h)
    live = (lax.broadcasted_iota(jnp.int32, (length, 1), 0) < live_len).astype(f32)
    rate = jnp.exp(pick(log_ref[0:1, :], h))
    sb = sigm(bp)
    zp = dp + pick(bias_ref[0:1, :], h)
    return sb, live, rate, zp


def fwd_kernel(
    heads, len_ref, q_ref, k_ref, v_ref, g_ref, bd_ref, fq_ref, fk_ref, fv_ref, log_ref, bias_ref,
    gain_ref, gated_ref, inv_ref, u_ref, mixed_ref, state_ref, qpad, kpad, vpad, qs, ks, vs,
):
    h = pl.program_id(0)
    length = q_ref.shape[0]
    chunks = length // CH
    load_padded(qpad, q_ref)
    load_padded(kpad, k_ref)
    load_padded(vpad, v_ref)
    fill_vectors(
        length, qpad, kpad, vpad, taps(fq_ref), taps(fk_ref), taps(fv_ref), qs, ks, vs
    )
    sb, live, rate, zp = beta_decay(h, heads, length, len_ref[0], bd_ref[...], log_ref, bias_ref)
    beta = sb * live
    logs = -rate * softplus(zp)
    rows, cols = iotas(CH)
    kept = []
    mats = []
    for n in range(chunks):
        part = slice(n * CH, (n + 1) * CH)
        col, row = chunk_decay(logs[part], CH)
        gaps = col - row
        decay = jnp.where(rows >= cols, jnp.exp(jnp.where(rows >= cols, gaps, 0.0)), 0.0)
        kf = ks[part, :]
        gram = mm3(kf, kf, 1, 1)
        mats.append(jnp.where(rows > cols, beta[part] * decay * gram, 0.0))
        kept.append((part, col, decay))
    inverses = unit_lower_inverses(mats)
    state = None
    for n in range(chunks):
        part, col, decay = kept[n]
        kf = ks[part, :]
        qf = qs[part, :]
        inv_ref[0, part, :] = inverses[n].astype(inv_ref.dtype)
        grow = jnp.exp(col)
        rhs = vs[part, :]
        if state is not None:
            rhs = rhs - grow * mm(kf, state)
        u = mm3(inverses[n], beta[part] * rhs)
        u_ref[part, :] = u.astype(u_ref.dtype)
        scores = mm(qf, kf, 1, 1) * decay
        out = mm(scores, u)
        if state is not None:
            out = out + grow * mm(qf, state)
        mixed_ref[part, :] = out
        if n + 1 < chunks:
            last = col[CH - 1 :, :]
            add = mm(kf * jnp.exp(last - col), u, 0, 0)
            state = add if state is None else jnp.exp(last) * state + add
            state_ref[0, n] = state
    gain = gain_ref[0:1, :]
    live_len = len_ref[0]

    def finish(t, _):
        start = pl.multiple_of(t * TILE, TILE)
        sl = pl.ds(start, TILE)
        m = mixed_ref[sl, :]
        gp = g_ref[sl, :].astype(f32)
        pos = start + lax.broadcasted_iota(jnp.int32, (TILE, 1), 0)
        alive = (pos < live_len).astype(f32)
        r = lax.rsqrt(jnp.mean(m * m, axis=1, keepdims=True) + 1e-05)
        gated_ref[sl, :] = (m * r * gain * (gp * sigm(gp)) * alive).astype(bf16)
        return 0

    lax.fori_loop(0, length // TILE, finish, 0)


def bwd_kernel(
    heads, len_ref, q_ref, k_ref, v_ref, g_ref, bd_ref, fq_ref, fk_ref, fv_ref, log_ref, bias_ref,
    gain_ref, inv_ref, u_ref, mixed_ref, state_ref, dg_ref,
    dpre_out, dfq_out, dfk_out, dfv_out, dgain_out, dsmall_out,
    qpad, kpad, vpad, qs, ks, vs, dos, dqs, dks, dvs, dbds,
):
    h = pl.program_id(0)
    length = q_ref.shape[0]
    chunks = length // CH
    load_padded(qpad, q_ref)
    load_padded(kpad, k_ref)
    load_padded(vpad, v_ref)
    fq, fk, fv = taps(fq_ref), taps(fk_ref), taps(fv_ref)
    fill_vectors(length, qpad, kpad, vpad, fq, fk, fv, qs, ks, vs)
    live_len = len_ref[0]
    gain = gain_ref[0:1, :]

    @pl.when(h == 0)
    def _():
        dgain_out[...] = jnp.zeros(dgain_out.shape, f32)
        dbds[...] = jnp.zeros(dbds.shape, f32)
        dsmall_out[...] = jnp.zeros(dsmall_out.shape, f32)

    def gate_back(t, acc):
        start = pl.multiple_of(t * TILE, TILE)
        sl = pl.ds(start, TILE)
        m = mixed_ref[sl, :]
        gp = g_ref[sl, :].astype(f32)
        pos = start + lax.broadcasted_iota(jnp.int32, (TILE, 1), 0)
        alive = (pos < live_len).astype(f32)
        r = lax.rsqrt(jnp.mean(m * m, axis=1, keepdims=True) + 1e-05)
        n = m * r
        t_ = dg_ref[sl, :].astype(f32) * alive
        s = sigm(gp)
        act = gp * s
        tn = t_ * n
        dpre_out[sl, lanes_at(2 * heads + h, 512)] = (
            tn * gain * (s + act * (1.0 - s))
        ).astype(bf16)
        dn = t_ * gain * act
        dos[sl, :] = r * (dn - n * jnp.mean(dn * n, axis=1, keepdims=True))
        return acc + jnp.sum((tn * act).reshape(TILE // 8, 8, tn.shape[1]), axis=0)

    dgain = lax.fori_loop(0, length // TILE, gate_back, jnp.zeros((8, gain.shape[1]), f32))
    dgain_out[...] += dgain

    sb, live, rate, zp = beta_decay(h, heads, length, live_len, bd_ref[...], log_ref, bias_ref)
    beta = sb * live
    sp = softplus(zp)
    logs = -rate * sp
    rows, cols = iotas(CH)
    incl = rows >= cols
    ones = jnp.ones((CH, 128), f32)
    dstate = None
    dbetas = [None] * chunks
    dlogs = [None] * chunks
    for n in reversed(range(chunks)):
        part = slice(n * CH, (n + 1) * CH)
        col, row = chunk_decay(logs[part], CH)
        gaps = col - row
        decay = jnp.where(incl, jnp.exp(jnp.where(incl, gaps, 0.0)), 0.0)
        grow = jnp.exp(col)
        last = col[CH - 1 :, :]
        kf = ks[part, :]
        qf = qs[part, :]
        u = u_ref[part, :].astype(f32)
        inv = inv_ref[0, part, :]
        do = dos[part, :]
        b = beta[part]
        gram = mm(kf, kf, 1, 1)
        strict_decay = jnp.where(rows > cols, decay, 0.0)
        scores = mm(qf, kf, 1, 1) * decay
        m_all = mm(do, u, 1, 1)
        du = mm(scores, do, 0, 0)
        tail = jnp.exp(last - col)
        if dstate is not None:
            kend = kf * tail
            du = du + mm(kend, dstate)
        dr = mm(inv, du, 0, 0)
        dvs[part, :] = b * dr
        da = mm(dr, u, 1, 1)
        da_dec = -da * strict_decay
        da_gram = da_dec * gram
        dbeta = jnp.sum(da_gram, axis=1, keepdims=True)
        msc = m_all * scores
        both = msc + b * da_gram
        rs = jnp.sum(both, axis=1, keepdims=True)
        both_h, both_l = split2(both)
        cs = (mm(both_h, ones, 0, 0) + mm(both_l, ones, 0, 0))[:, :1]
        dc = rs - cs
        dqk = m_all * decay
        dgram = b * da_dec
        dq = mm(dqk, kf)
        dk = mm(dqk, qf, 0, 0) + mm(dgram, kf) + mm(dgram, kf, 0, 0)
        rest = vs[part, :]
        dlast = None
        if n > 0:
            state = state_ref[0, n - 1]
            kst = mm(kf, state)
            qst = mm(qf, state)
            rest = rest - grow * kst
            dkst = -(b * grow) * dr
            dqst = grow * do
            dk = dk + mm(dkst, state, 1, 1)
            dq = dq + mm(dqst, state, 1, 1)
            dc = dc + jnp.sum(dkst * kst + dqst * qst, axis=1, keepdims=True)
            dprev = mm(kf, dkst, 0, 0) + mm(qf, dqst, 0, 0)
        dbetas[n] = dbeta + jnp.sum(dr * rest, axis=1, keepdims=True)
        if dstate is not None:
            dkend = mm(u, dstate, 1, 1)
            dk = dk + dkend * tail
            w = jnp.sum(dkend * kend, axis=1, keepdims=True)
            dc = dc - w
            dlast = jnp.sum(w, axis=0, keepdims=True)
            if n > 0:
                scale = jnp.exp(last)
                dprev = dprev + scale * dstate
                dlast = dlast + scale * jnp.sum(
                    jnp.sum(dstate * state, axis=1, keepdims=True), axis=0, keepdims=True
                )
        dlog = suffix_sum(dc, CH)
        if dlast is not None:
            dlog = dlog + dlast
        dlogs[n] = dlog
        dqs[part, :] = dq
        dks[part, :] = dk
        if n > 0:
            dstate = dprev
    dbeta = jnp.concatenate(dbetas, axis=0)
    dlog = jnp.concatenate(dlogs, axis=0)
    dbp = dbeta * live * sb * (1.0 - sb)
    dzp = -rate * dlog * sigm(zp)
    lanes = lax.broadcasted_iota(jnp.int32, (length, 128), 1)
    dbds[...] += jnp.where(lanes == h, dbp, 0.0) + jnp.where(lanes == heads + h, dzp, 0.0)

    @pl.when(h == heads - 1)
    def _():
        dpre_out[:, 12 * heads * 128 : (12 * heads + 1) * 128] = dbds[...].astype(bf16)

    small_lane = lax.broadcasted_iota(jnp.int32, (8, 128), 1)
    small_row = lax.broadcasted_iota(jnp.int32, (8, 128), 0)
    at_head = small_lane == h
    dsmall_out[...] += jnp.where(
        at_head & (small_row == 0), jnp.sum(dlog * logs, axis=0, keepdims=True), 0.0
    ) + jnp.where(at_head & (small_row == 1), jnp.sum(dzp, axis=0, keepdims=True), 0.0)

    def pre_back(t, _):
        start = pl.multiple_of(t * TILE, TILE)
        sl = pl.ds(start, TILE)
        for pad, filt, dref, scale in ((qpad, fq, dqs, 256 ** (-0.5)), (kpad, fk, dks, 1.0)):
            y = conv_rows(pad, start, TILE, filt)
            s = sigm(y)
            a = y * s
            r = lax.rsqrt(jnp.sum(a * a, axis=1, keepdims=True) + 1e-06)
            nn = a * r
            dn = dref[sl, :] * scale
            da_ = r * (dn - nn * jnp.sum(dn * nn, axis=1, keepdims=True))
            dref[sl, :] = da_ * (s + a * (1.0 - s))
        y = conv_rows(vpad, start, TILE, fv)
        s = sigm(y)
        dvs[sl, :] = dvs[sl, :] * (s + y * s * (1.0 - s))
        return 0

    lax.fori_loop(0, length // TILE, pre_back, 0)
    for dref in (dqs, dks, dvs):
        dref[length : length + PADR, :] = jnp.zeros((PADR, dref.shape[1]), f32)

    for pad, filt, dref, first, fout in (
        (qpad, fq, dqs, h, dfq_out),
        (kpad, fk, dks, heads + h, dfk_out),
        (vpad, fv, dvs, heads + h, dfv_out),
    ):
        width = dref.shape[1]

        def conv_back(t, accs, pad=pad, filt=filt, dref=dref, first=first, width=width):
            start = pl.multiple_of(t * TILE, TILE)
            dx = None
            new = []
            dys = dref[pl.ds(start, TILE + PADR), :]
            xs = pad[pl.ds(start, TILE + PADR), :]
            dy = dys[:TILE]
            for i in range(4):
                term = filt[i] * dys[3 - i : 3 - i + TILE]
                dx = term if dx is None else dx + term
                prod = dy * xs[PADR - 3 + i : PADR - 3 + i + TILE]
                new.append(accs[i] + jnp.sum(prod.reshape(TILE // 8, 8, width), axis=0))
            dpre_out[pl.ds(start, TILE), lanes_at(first, width)] = dx.astype(bf16)
            return tuple(new)

        accs = lax.fori_loop(
            0, length // TILE, conv_back, tuple(jnp.zeros((8, width), f32) for _ in range(4))
        )
        for i in range(4):
            fout[i : i + 1, :] = jnp.sum(accs[i], axis=0, keepdims=True)


def col_spec(length, width, first=0):
    return pl.BlockSpec((length, width), lambda h: (0, first + h))


def whole_spec(shape):
    return pl.BlockSpec(shape, lambda h: (0,) * len(shape))


def front_specs(length, heads):
    return [
        pl.BlockSpec(memory_space=pltpu.SMEM),
        col_spec(length, 256),
        col_spec(length, 256, heads),
        col_spec(length, 512, heads),
        col_spec(length, 512, 2 * heads),
        pl.BlockSpec((length, 128), lambda h: (0, 12 * heads)),
        col_spec(4, 256),
        col_spec(4, 256),
        col_spec(4, 512),
        whole_spec((1, 128)),
        whole_spec((1, 128)),
        whole_spec((1, 512)),
    ]


def mixer_forward(heads, lens, pre, fq, fk, fv, logs, bias, gain):
    length = pre.shape[0]
    chunks = length // CH
    kept = max(1, chunks - 1)
    return pl.pallas_call(
        functools.partial(fwd_kernel, heads),
        grid=(heads,),
        in_specs=front_specs(length, heads),
        out_specs=[
            col_spec(length, 512),
            pl.BlockSpec((1, length, CH), lambda h: (h, 0, 0)),
            col_spec(length, 512),
            col_spec(length, 512),
            pl.BlockSpec((1, kept, 256, 512), lambda h: (h, 0, 0, 0)),
        ],
        out_shape=[
            jax.ShapeDtypeStruct((length, heads * 512), bf16),
            jax.ShapeDtypeStruct((heads, length, CH), bf16),
            jax.ShapeDtypeStruct((length, heads * 512), bf16),
            jax.ShapeDtypeStruct((length, heads * 512), f32),
            jax.ShapeDtypeStruct((heads, kept, 256, 512), f32),
        ],
        scratch_shapes=[
            pltpu.VMEM((length + PADR, 256), f32),
            pltpu.VMEM((length + PADR, 256), f32),
            pltpu.VMEM((length + PADR, 512), f32),
            pltpu.VMEM((length, 256), f32),
            pltpu.VMEM((length, 256), f32),
            pltpu.VMEM((length, 512), f32),
        ],
        compiler_params=pltpu.CompilerParams(vmem_limit_bytes=50 * 1024 * 1024),
        name="mixer_forward",
    )(lens, pre, pre, pre, pre, pre, fq, fk, fv, logs, bias, gain)


def mixer_backward(heads, lens, pre, fq, fk, fv, logs, bias, gain, saved, dgated):
    length = pre.shape[0]
    chunks = length // CH
    kept = max(1, chunks - 1)
    inv, u, mixed, states = saved
    return pl.pallas_call(
        functools.partial(bwd_kernel, heads),
        grid=(heads,),
        in_specs=front_specs(length, heads)
        + [
            pl.BlockSpec((1, length, CH), lambda h: (h, 0, 0)),
            col_spec(length, 512),
            col_spec(length, 512),
            pl.BlockSpec((1, kept, 256, 512), lambda h: (h, 0, 0, 0)),
            col_spec(length, 512),
        ],
        out_specs=[
            whole_spec((length, pre.shape[1])),
            col_spec(4, 256), col_spec(4, 256), col_spec(4, 512),
            whole_spec((8, 512)), whole_spec((8, 128)),
        ],
        out_shape=[
            jax.ShapeDtypeStruct(pre.shape, bf16),
            jax.ShapeDtypeStruct((4, heads * 256), f32),
            jax.ShapeDtypeStruct((4, heads * 256), f32),
            jax.ShapeDtypeStruct((4, heads * 512), f32),
            jax.ShapeDtypeStruct((8, 512), f32),
            jax.ShapeDtypeStruct((8, 128), f32),
        ],
        scratch_shapes=[
            pltpu.VMEM((length + PADR, 256), f32),
            pltpu.VMEM((length + PADR, 256), f32),
            pltpu.VMEM((length + PADR, 512), f32),
            pltpu.VMEM((length, 256), f32),
            pltpu.VMEM((length, 256), f32),
            pltpu.VMEM((length, 512), f32),
            pltpu.VMEM((length, 512), f32),
            pltpu.VMEM((length + PADR, 256), f32),
            pltpu.VMEM((length + PADR, 256), f32),
            pltpu.VMEM((length + PADR, 512), f32),
            pltpu.VMEM((length, 128), f32),
        ],
        compiler_params=pltpu.CompilerParams(vmem_limit_bytes=50 * 1024 * 1024),
        name="mixer_backward",
    )(lens, pre, pre, pre, pre, pre, fq, fk, fv, logs, bias, gain, inv, u, mixed, states, dgated)


MESH = pl.DeviceIdType.MESH


def column_chunks(widths, size, layers):
    size = size * max(1, layers // 4)
    out = []
    for a, width in enumerate(widths):
        units = width // 128
        count = max(1, -(-width // size))
        lo = 0
        for i in range(count):
            hi = units * (i + 1) // count
            out.append((a, lo * 128, (hi - lo) * 128))
            lo = hi
    return out


def placement():
    spot = lax.axis_index("dp")
    return spot, lax.rem(spot, 2), lax.rem(lax.div(spot, 2), 2), lax.div(spot, 4)


def greet(partners):
    barrier = pltpu.get_barrier_semaphore()
    for partner in partners:
        pl.semaphore_signal(barrier, inc=1, device_id={"dp": partner}, device_id_type=MESH)
    pl.semaphore_wait(barrier, len(partners))


def remote(src, dst, send, recv, target):
    return pltpu.make_async_remote_copy(
        src_ref=src, dst_ref=dst, send_sem=send, recv_sem=recv,
        device_id={"dp": target}, device_id_type=MESH,
    )


def gather_kernel(layers, chunks, count, pairs, *refs):
    srcs, outs = refs[: count + pairs], refs[count + pairs : 2 * (count + pairs)]
    own_sem, us, ur, ds, dr, ys, yr, cs, cr, ps, pr, pair_sem = refs[2 * (count + pairs) :]
    rows = srcs[0].shape[0]
    spot, core, side, layer = placement()
    turn = lax.axis_index("tensor")
    at = lambda z, y, c: 4 * z + 2 * y + c
    y_to, c_to = at(layer, 1 - side, core), at(layer, side, 1 - core)
    has_up, has_down = layer < layers - 1, layer > 0
    barrier = pltpu.get_barrier_semaphore()
    around = [4 * lax.rem(layer + s, layers) + 2 * side + core for s in (1, layers - 1)]
    for partner in [y_to, c_to] + around:
        pl.semaphore_signal(barrier, inc=1, device_id={"dp": partner}, device_id_type=MESH)
    pl.semaphore_signal(barrier, inc=1, device_id={"tensor": 1 - turn}, device_id_type=MESH)
    pl.semaphore_wait(barrier, 5)

    def place(j, origin):
        a, lo, width, _ = chunks[j]
        start = pl.multiple_of(origin * rows, rows)
        return outs[a].at[pl.ds(start, rows), lo : lo + width]

    def own(j):
        a, lo, width, _ = chunks[j]
        return srcs[a].at[:, lo : lo + width]

    def up_copy(j, k, half, origin, src):
        i = 2 * k + half
        return remote(src, place(j, origin), us.at[j, i], ur.at[j, i], spot + 4)

    def down_copy(j, k, half, origin, src):
        i = 2 * k + half
        return remote(src, place(j, origin), ds.at[j, i], dr.at[j, i], spot - 4)

    def y_copy(j, slot, origin, src):
        return remote(src, place(j, origin), ys.at[j, slot], yr.at[j, slot], y_to)

    def c_copy(j, slot, origin, src):
        return remote(src, place(j, origin), cs.at[j, slot], cr.at[j, slot], c_to)

    number = len(chunks)
    narrow = [j for j in range(number) if not chunks[j][3]]
    early = [j for j in range(number) if chunks[j][3]]
    keep = []
    for p in range(pairs):
        half_rows = srcs[count + p].shape[0]
        spot_rows = pl.ds(pl.multiple_of(turn * half_rows, half_rows), half_rows)
        copy = pltpu.make_async_remote_copy(
            src_ref=srcs[count + p], dst_ref=outs[count + p].at[spot_rows, :],
            send_sem=ps.at[p], recv_sem=pr.at[p],
            device_id={"tensor": 1 - turn}, device_id_type=MESH,
        )
        copy.start()
        local_copy = pltpu.make_async_copy(
            srcs[count + p], outs[count + p].at[spot_rows, :], pair_sem.at[p]
        )
        local_copy.start()
        keep.append((copy, local_copy))

    def send_z(j, half, origin, src):
        @pl.when(has_up)
        def _():
            up_copy(j, 0, half, origin, src).start()

        @pl.when(has_down)
        def _():
            down_copy(j, 0, half, origin, src).start()

    locals_ = []
    for j in early + narrow:
        y_copy(j, 0, spot, own(j)).start()
        send_z(j, 0, spot, own(j))
        c_copy(j, 0, spot, own(j)).start()
        copy = pltpu.make_async_copy(own(j), place(j, spot), own_sem.at[j])
        copy.start()
        locals_.append(copy)
    across = at(layer, 1 - side, core)

    def take_z(j, k, half):
        there = lax.rem(side + half, 2)
        for sign, fits, more, copy in (
            (-1, layer >= k + 1, has_up, up_copy),
            (1, layer + k + 1 < layers, has_down, down_copy),
        ):

            @pl.when(fits)
            def _(sign=sign, more=more, copy=copy):
                origin = at(layer + sign * (k + 1), there, core)
                here = place(j, origin)
                copy(j, k, half, origin, here).wait_recv()

                @pl.when(more)
                def _():
                    copy(j, k + 1, half, origin, here).start()

                slot = 2 * k + (1 if sign < 0 else 2)
                if not chunks[j][3]:
                    y_copy(j, slot, origin, here).start()
                c_copy(j, slot if half == 0 else slot + 2 * layers - 1, origin, here).start()

    def take_y(j, k):
        slots = [(0, None, None)] if k == 0 else [
            (2 * k - 1, layer >= k, -1), (2 * k, layer + k < layers, 1)
        ]
        for slot, fits, sign in slots:
            shift = 0 if sign is None else sign * k

            def body(slot=slot, shift=shift):
                origin = at(layer + shift, 1 - side, core)
                here = place(j, origin)
                y_copy(j, slot, origin, here).wait_recv()
                c_copy(j, 2 * layers - 1 + slot, origin, here).start()

            if fits is None:
                body()
            else:
                pl.when(fits)(body)

    for j in early:
        y_copy(j, 0, across, own(j)).wait_recv()
        send_z(j, 1, across, place(j, across))
        c_copy(j, 2 * layers - 1, across, place(j, across)).start()
    for k in range(layers):
        if k < layers - 1:
            for j in early:
                for half in range(2):
                    take_z(j, k, half)
            for j in narrow:
                take_z(j, k, 0)
        if k > 0:
            for j in narrow:
                take_y(j, k - 1)
    for j in narrow:
        take_y(j, layers - 1)

    for copy, local_copy in keep:
        local_copy.wait()
        copy.wait()
    for copy in locals_:
        copy.wait()
    for j in range(number):
        wide = chunks[j][3]
        me = own(j)
        for half in range(2 if wide else 1):
            for k in range(layers - 1):

                @pl.when(has_up & (layer >= k))
                def _(k=k, half=half):
                    up_copy(j, k, half, spot, me).wait_send()

                @pl.when(has_down & (layer + k < layers))
                def _(k=k, half=half):
                    down_copy(j, k, half, spot, me).wait_send()

        def settle(slot, shift):
            if slot == 0 or not wide:
                y_copy(j, slot, spot, me).wait_send()
            for half in range(2):
                origin = at(layer + shift, lax.rem(side + half, 2), 1 - core)
                c_copy(j, slot + half * (2 * layers - 1), origin, place(j, origin)).wait()

        settle(0, 0)
        for k in range(1, layers):
            pl.when(layer >= k)(functools.partial(settle, 2 * k - 1, -k))
            pl.when(layer + k < layers)(functools.partial(settle, 2 * k, k))


def mark_early(chunks, share):
    total = sum(c[2] for c in chunks)
    marked, done = [], 0
    for c in chunks:
        early = done + c[2] <= share * total + 64
        done += c[2] if early else 0
        marked.append(c + (early,))
    return marked


def gather_all(shards, pairs, devices, ident, size=1600, share=0):
    rows = shards[0].shape[0]
    layers = devices // 4
    chunks = mark_early(column_chunks([s.shape[1] for s in shards], size, layers), share)
    n = len(chunks)
    sem = lambda *shape: pltpu.SemaphoreType.DMA(shape)
    z_slots, slots = 2 * layers, 2 * layers - 1
    arrays = tuple(shards) + tuple(pairs)
    return pl.pallas_call(
        functools.partial(gather_kernel, layers, chunks, len(shards), len(pairs)),
        in_specs=[pl.BlockSpec(memory_space=pl.ANY)] * len(arrays),
        out_specs=[pl.BlockSpec(memory_space=pl.ANY)] * len(arrays),
        out_shape=[jax.ShapeDtypeStruct((devices * rows, s.shape[1]), s.dtype) for s in shards]
        + [jax.ShapeDtypeStruct((2 * p.shape[0], p.shape[1]), p.dtype) for p in pairs],
        scratch_shapes=[
            sem(n), sem(n, z_slots), sem(n, z_slots), sem(n, z_slots), sem(n, z_slots),
            sem(n, slots), sem(n, slots), sem(n, 2 * slots), sem(n, 2 * slots),
            sem(max(1, len(pairs))), sem(max(1, len(pairs))), sem(max(1, len(pairs))),
        ],
        compiler_params=pltpu.CompilerParams(collective_id=ident, has_side_effects=True),
        name="gather_rows",
    )(*arrays)


def scatter_kernel(layers, chunks, dots, *refs):
    n_held = max([c[0] for c in chunks if c[3] is None]) + 1
    srcs, lefts = refs[:n_held], refs[n_held : n_held + dots]
    rights = refs[n_held + dots : n_held + 2 * dots]
    sent_ref, out, come_ref = refs[n_held + 2 * dots : n_held + 2 * dots + 3]
    (stage, sends, buf1, buf2, buf3, own_sem, cs, cr, ys, yr, zs, zr, pair_send,
     pair_recv) = refs[n_held + 2 * dots + 3 :]
    rows = out.shape[0]
    spot, core, side, layer = placement()
    turn = lax.axis_index("tensor")
    at = lambda z, y, c: 4 * lax.rem(z + layers, layers) + 2 * y + c
    z_to = [at(layer + k, side, core) for k in range(1, layers)]
    y_to, c_to = at(layer, 1 - side, core), at(layer, side, 1 - core)
    barrier = pltpu.get_barrier_semaphore()
    for partner in z_to + [y_to, c_to]:
        pl.semaphore_signal(barrier, inc=1, device_id={"dp": partner}, device_id_type=MESH)
    pl.semaphore_signal(barrier, inc=1, device_id={"tensor": 1 - turn}, device_id_type=MESH)
    pl.semaphore_wait(barrier, layers + 2)
    number = len(chunks)
    firsts = []
    total = 0
    for chunk in chunks:
        firsts.append(total)
        total += chunk[2]
    pair = pltpu.make_async_remote_copy(
        src_ref=sent_ref, dst_ref=come_ref, send_sem=pair_send, recv_sem=pair_recv,
        device_id={"tensor": 1 - turn}, device_id_type=MESH,
    )
    pair.start()

    def cols(j):
        return slice(firsts[j], firsts[j] + chunks[j][2])

    def c_copy(j):
        a, lo, width, which = chunks[j]
        if which is None:
            src = srcs[a].at[:, 1 - core, :, lo : lo + width]
        else:
            src = sends.at[j % 3, :, :, 0:width]
        return remote(src, buf1.at[:, :, cols(j)], cs.at[j], cr.at[j], c_to)

    def own_copy(j):
        a, lo, width, _ = chunks[j]
        return pltpu.make_async_copy(
            srcs[a].at[:, core, :, lo : lo + width],
            stage.at[j % 3, :, :, 0:width], own_sem.at[j],
        )

    def y_copy(j, m):
        block = 2 * lax.rem(layer + m, layers) + 1 - side
        return remote(
            buf1.at[block, :, cols(j)], buf2.at[m, :, cols(j)], ys.at[j, m], yr.at[j, m], y_to
        )

    def z_copy(j, k):
        return remote(
            buf2.at[k, :, cols(j)], buf3.at[k - 1, :, cols(j)], zs.at[j, k - 1], zr.at[j, k - 1],
            z_to[k - 1],
        )

    def produce(j):
        a, lo, width, which = chunks[j]
        if which is None:
            own_copy(j).start()
        else:
            if j >= 3:
                c_copy(j - 3).wait_send()
            right = rights[which][:, lo : lo + width]

            wide = 256
            per = wide // (2 * rows)

            def body(g, _):
                left = lefts[which][:, pl.ds(pl.multiple_of(g * wide, wide), wide)]
                both = mm(left, right, 0, 0)
                for i in range(per):
                    low_half = both[2 * i * rows : (2 * i + 1) * rows]
                    high_half = both[(2 * i + 1) * rows : (2 * i + 2) * rows]
                    mine = jnp.where(core == 0, low_half, high_half)
                    other = jnp.where(core == 0, high_half, low_half)
                    stage[j % 3, g * per + i, :, 0:width] = mine.astype(bf16)
                    sends[j % 3, g * per + i, :, 0:width] = other.astype(bf16)
                return 0

            lax.fori_loop(0, 2 * layers // per, body, 0)
        c_copy(j).start()

    for j in range(min(2, number)):
        produce(j)

    def first(j):
        width = chunks[j][2]
        if chunks[j][3] is None:
            own_copy(j).wait()
        c_copy(j).wait_recv()

        def body(b, _):
            mine = stage[j % 3, b, :, 0:width].astype(f32)
            buf1[b, :, cols(j)] = (buf1[b, :, cols(j)].astype(f32) + mine).astype(bf16)
            return 0

        lax.fori_loop(0, 2 * layers, body, 0)
        for m in list(range(1, layers)) + [0]:
            y_copy(j, m).start()
        if j + 2 < number:
            produce(j + 2)

    def second(j):
        for m in list(range(1, layers)) + [0]:
            y_copy(j, m).wait_recv()
            block = 2 * lax.rem(layer + m, layers) + side
            mine = buf1[block, :, cols(j)].astype(f32)
            buf2[m, :, cols(j)] = (buf2[m, :, cols(j)].astype(f32) + mine).astype(bf16)
            if m:
                z_copy(j, m).start()

    def third(j):
        total = buf2[0, :, cols(j)].astype(f32)
        for k in range(1, layers):
            z_copy(j, k).wait_recv()
            total = total + buf3[k - 1, :, cols(j)].astype(f32)
        out[:, cols(j)] = total

    for j in range(number + 4):
        if j < number:
            first(j)
        if 0 <= j - 2 < number:
            second(j - 2)
        if 0 <= j - 4 < number:
            third(j - 4)
    for j in range(number):
        later = j + 3 < number and chunks[j + 3][3] is not None
        if not later:
            c_copy(j).wait_send()
        for m in range(layers):
            y_copy(j, m).wait_send()
        for k in range(1, layers):
            z_copy(j, k).wait_send()
    pair.wait()


def scatter_sum(held, products, tail, sent, devices, ident, size=512):
    parts = [held, tail]
    rows = held.shape[0] // devices
    layers = devices // 4
    widths = [held.shape[1]] + [w for _, _, w in products] + [tail.shape[1]]
    chunks = []
    for a, lo, width in column_chunks(widths, size, 4):
        if a == 0:
            chunks.append((0, lo, width, None))
        elif a <= len(products):
            chunks.append((a, lo, width, a - 1))
        else:
            chunks.append((1, lo, width, None))
    n = len(chunks)
    width = sum(widths)
    widest = max(c[2] for c in chunks)
    sem = lambda *shape: pltpu.SemaphoreType.DMA(shape)
    hbm, vmem = pl.BlockSpec(memory_space=pl.ANY), pl.BlockSpec(memory_space=pltpu.VMEM)
    return pl.pallas_call(
        functools.partial(scatter_kernel, layers, chunks, len(products)),
        in_specs=[hbm] * 2 + [vmem] * (2 * len(products)) + [hbm],
        out_specs=[vmem, hbm],
        out_shape=[
            jax.ShapeDtypeStruct((rows, width), f32),
            jax.ShapeDtypeStruct(sent.shape, sent.dtype),
        ],
        scratch_shapes=[
            pltpu.VMEM((3, 2 * layers, rows, widest), bf16),
            pltpu.VMEM((3, 2 * layers, rows, widest), bf16),
            pltpu.VMEM((2 * layers, rows, width), bf16),
            pltpu.VMEM((layers, rows, width), bf16),
            pltpu.VMEM((layers - 1, rows, width), bf16),
            sem(n), sem(n), sem(n), sem(n, layers), sem(n, layers),
            sem(n, layers - 1), sem(n, layers - 1),
            pltpu.SemaphoreType.DMA, pltpu.SemaphoreType.DMA,
        ],
        compiler_params=pltpu.CompilerParams(
            collective_id=ident, has_side_effects=True, vmem_limit_bytes=61 * 1024 * 1024
        ),
        name="scatter_sum",
    )(
        *[p.reshape(devices // 2, 2, rows, p.shape[1]) for p in parts],
        *[p[0] for p in products],
        *[p[1] for p in products],
        sent,
    )


EXTRA = 128


def rms_scale(values):
    return lax.rsqrt(jnp.mean(values * values, axis=-1, keepdims=True) + 1e-05)


def norm_back(values, gain, grad_normed):
    scale = rms_scale(values)
    unit_vals = values * scale
    grad_unit = grad_normed * gain
    grad_values = scale * (
        grad_unit - unit_vals * jnp.mean(grad_unit * unit_vals, axis=-1, keepdims=True)
    )
    return (grad_values, jnp.sum(grad_normed * unit_vals, axis=0))


def pair_swap(values):
    return lax.ppermute(values, "tensor", [(0, 1), (1, 0)])


def pair_gather(values):
    other = pair_swap(values)
    first = lax.axis_index("tensor") == 0
    return jnp.concatenate(
        [jnp.where(first, values, other), jnp.where(first, other, values)], axis=0
    )


def pair_halves(parts):
    rows = parts.shape[0] // 2
    mine = lax.axis_index("tensor") * rows
    kept = lax.dynamic_slice_in_dim(parts, mine, rows)
    sent = lax.dynamic_slice_in_dim(parts, rows - mine, rows).astype(bf16)
    return kept, sent


def pair_scatter(parts):
    kept, sent = pair_halves(parts)
    return kept + pair_swap(sent).astype(f32)


def dot(a, b, ca=1, cb=0):
    return lax.dot_general(a, b, (((ca,), (cb,)), ((), ())), preferred_element_type=f32)


def high_low(values):
    high = lax.reduce_precision(values, 8, 7)
    return jnp.stack([high, values - high], axis=1).astype(bf16)


def gather_rows(values):
    return lax.all_gather(values, "dp", axis=0, tiled=True)


def scatter_rows(values):
    return lax.psum_scatter(values, "dp", scatter_dimension=0, tiled=True)


def pack_filters(fq, fk, fv, rows):
    flat = jnp.concatenate([fq, fk, fv], axis=2).reshape(-1)
    return flat.reshape(-1, rows).T


def local(
    tokens,
    lengths,
    cotangent,
    gain_in,
    gain_ffn,
    gain_out,
    w_query,
    w_key,
    w_value,
    w_gate,
    w_beta,
    w_decay,
    conv_query,
    conv_key,
    conv_value,
    decay_log,
    decay_bias,
    w_output,
    w_ffn_gate,
    w_ffn_up,
    w_ffn_down,
):
    heads = w_beta.shape[1]
    rows = w_query.shape[0]
    devices = lax.axis_size("dp")
    low = lambda v: v.astype(bf16)
    filters = pack_filters(conv_query, conv_key, conv_value, rows)
    filter_cols = filters.shape[1]
    gains = pair_gather(jnp.concatenate([gain_in, gain_ffn, gain_out])[None])
    n_in, n_out = gain_in.shape[0], gain_out.shape[0]
    pair_out = jnp.pad(gains[:, 2 * n_in :].reshape(-1), (0, rows - 2 * n_out))
    small = jnp.concatenate(
        [
            low(jnp.concatenate([w_beta, w_decay, filters], axis=1)),
            high_low(gains[:, :n_in].reshape(-1)),
            high_low(gains[:, n_in : 2 * n_in].reshape(-1)),
            high_low(pair_out),
        ],
        axis=1,
    )
    small = jnp.pad(small, ((0, 0), (0, EXTRA - small.shape[1])))
    proj_shard = jnp.concatenate(
        [low(w_query), low(w_key), low(w_value), low(w_gate), small], axis=1
    )
    proj, out_t, seq_x, seq_cot = gather_all(
        (proj_shard, low(w_output).T), (tokens, cotangent), devices, 0
    )
    extra_at = 12 * heads * 128
    gain_at = extra_at + 2 * heads + filter_cols
    sides = proj[:, gain_at : gain_at + 6].astype(f32)
    sides = sides[:, 0::2] + sides[:, 1::2]
    full_in, full_ffn = sides[:, 0], sides[:, 1]
    full_out = sides[:, 2].reshape(devices, rows)[:, : 2 * n_out].reshape(1, -1)
    gate_weight = gather_rows(low(w_ffn_gate))
    up_weight = gather_rows(low(w_ffn_up))
    down_t = gather_rows(low(w_ffn_down).T)

    tap_count = conv_query.shape[0]
    piece_q, piece_v = conv_query.shape[2], conv_value.shape[2]
    flat = proj[:, extra_at + 2 * heads : gain_at]
    flat = flat.reshape(devices, rows, filter_cols).transpose(0, 2, 1)
    flat = flat.reshape(devices, tap_count, heads, 2 * piece_q + piece_v).astype(f32)
    flat = flat.transpose(1, 2, 0, 3)
    filt_q = flat[..., :piece_q].reshape(tap_count, -1)
    filt_k = flat[..., piece_q : 2 * piece_q].reshape(tap_count, -1)
    filt_v = flat[..., 2 * piece_q :].reshape(tap_count, -1)

    head_start = lax.axis_index("tensor") * heads
    lane_pad = lambda v: jnp.pad(
        lax.dynamic_slice_in_dim(v, head_start, heads), (0, 128 - heads)
    ).reshape(1, 128)
    local_log, local_bias = lane_pad(decay_log), lane_pad(decay_bias)

    inputs = tokens.astype(f32)
    seq_inputs = seq_x.astype(f32)
    seq_unit = seq_inputs * rms_scale(seq_inputs)
    seq_in = low(seq_unit * full_in)
    pre = dot(seq_in, proj)
    mixer_args = (heads, lengths, pre, filt_q, filt_k, filt_v, local_log, local_bias, full_out)
    gated, *saved = mixer_forward(*mixer_args)
    hidden = inputs + pair_scatter(dot(gated, out_t, 1, 1))
    normed_ffn = low(hidden * rms_scale(hidden) * full_ffn)
    normed_ffn, down_t = lax.optimization_barrier((normed_ffn, down_t))
    seq_ffn = pair_gather(normed_ffn)
    grad_inner = dot(seq_cot, down_t)
    seq_ffn, grad_inner = lax.optimization_barrier((seq_ffn, grad_inner))

    gate_act = dot(seq_ffn, gate_weight)
    up_act = dot(seq_ffn, up_weight)
    sigmoid_gate = jax.nn.sigmoid(gate_act)
    silu_gate = gate_act * sigmoid_gate
    inner = low(silu_gate * up_act)
    grad_gate_act = low(
        grad_inner * up_act * sigmoid_gate * (1.0 + gate_act * (1.0 - sigmoid_gate))
    )
    grad_up_act = low(grad_inner * silu_gate)
    grad_down = low(dot(seq_cot, inner, 0, 0))
    grad_gate_act, grad_up_act, grad_down = lax.optimization_barrier(
        (grad_gate_act, grad_up_act, grad_down)
    )
    down_piece = scatter_rows(grad_down)
    grad_seq_ffn = dot(grad_gate_act, gate_weight, 1, 1) + dot(grad_up_act, up_weight, 1, 1)
    kept_ffn, sent_ffn = pair_halves(grad_seq_ffn)
    sent_ffn, inner = lax.optimization_barrier((sent_ffn, inner))
    kept_out, sent_out = pair_halves(dot(inner, down_t, 1, 1))
    come_ffn, sent_out = lax.optimization_barrier((pair_swap(sent_ffn), sent_out))
    grad_normed_ffn = kept_ffn + come_ffn.astype(f32)
    grad_hidden_norm, grad_gain_ffn = norm_back(hidden, full_ffn, grad_normed_ffn)
    grad_hidden = cotangent.astype(f32) + grad_hidden_norm
    sent_branch, grad_gate_act, grad_up_act = lax.optimization_barrier(
        (low(grad_hidden), grad_gate_act, grad_up_act)
    )
    seq_grad_branch = pair_gather(sent_branch)
    grad_gate_w = low(dot(seq_ffn, grad_gate_act, 0, 0))
    grad_up_w = low(dot(seq_ffn, grad_up_act, 0, 0))
    seq_grad_branch, grad_gate_w, grad_up_w, sent_out = lax.optimization_barrier(
        (seq_grad_branch, grad_gate_w, grad_up_w, sent_out)
    )
    gate_piece = scatter_rows(grad_gate_w)
    come_out = pair_swap(sent_out)

    grad_gated = dot(seq_grad_branch, out_t)
    grad_pre, grad_fq, grad_fk, grad_fv, grad_gain_out, grad_small = mixer_backward(
        *mixer_args, saved, low(grad_gated)
    )
    grad_pre, come_out = lax.optimization_barrier((grad_pre, come_out))
    result = low(hidden + kept_out + come_out.astype(f32))
    grad_seq_in = dot(grad_pre, proj, 1, 1)
    kept_in, sent_in = pair_halves(grad_seq_in)
    extra = dot(seq_in, grad_pre[:, extra_at:], 0, 0)
    by_device = lambda g, piece: g.reshape(tap_count, heads, devices, piece)
    grad_flat = jnp.concatenate(
        [by_device(grad_fq, piece_q), by_device(grad_fk, piece_q), by_device(grad_fv, piece_v)],
        axis=3,
    ).transpose(2, 0, 1, 3)
    grad_flat = grad_flat.reshape(devices, filter_cols, rows).transpose(0, 2, 1)
    grad_flat = low(grad_flat.reshape(devices * rows, filter_cols))
    spread = lambda v: lax.dynamic_update_slice(jnp.zeros_like(decay_log), v, (head_start,))
    grad_decay = jnp.concatenate([spread(grad_small[0, :heads]), spread(grad_small[1, :heads])])
    by_rows = lambda v: jnp.pad(v, ((0, 0), (0, rows - v.shape[1]))).reshape(-1)
    columns = jnp.stack(
        [
            jnp.sum(grad_seq_in * seq_unit, axis=0),
            grad_gain_ffn,
            by_rows(jnp.sum(grad_gain_out, axis=0).reshape(devices, -1)),
            by_rows(jnp.broadcast_to(grad_decay, (devices,) + grad_decay.shape)),
        ],
        axis=1,
    )
    grad_tiny = jnp.concatenate(
        [low(extra[:, : 2 * heads]), grad_flat, low(columns)], axis=1
    )
    grad_tiny = jnp.pad(grad_tiny, ((0, 0), (0, EXTRA - grad_tiny.shape[1])))
    products = (
        (seq_in, grad_pre, extra_at),
        (seq_grad_branch, gated, gated.shape[1]),
    )
    pieces, come_in = scatter_sum(grad_up_w, products, grad_tiny, sent_in, devices, 1)
    ffn_width = grad_up_w.shape[1]
    up_piece, pieces = pieces[:, :ffn_width], pieces[:, ffn_width:]
    grad_normed_in = kept_in + come_in.astype(f32)
    out_width = w_output.shape[0]
    out_piece = pieces[:, extra_at : extra_at + out_width]
    tiny_piece = pieces[:, extra_at + out_width :]

    grad_inputs_norm, _ = norm_back(inputs, full_in, grad_normed_in)
    grad_tokens = grad_hidden + grad_inputs_norm

    sums = tiny_piece[:, 2 * heads + filter_cols : 2 * heads + filter_cols + 4].T
    sums = sums + pair_swap(sums)
    turn = lax.axis_index("tensor")
    take = lambda row, piece: lax.dynamic_slice_in_dim(sums[row], turn * piece, piece)
    n_heads = decay_log.shape[0]

    q_end, k_end = heads * 256, 2 * heads * 256
    v_end, g_end = k_end + heads * 512, k_end + 2 * heads * 512
    grad_filters = tiny_piece[:, 2 * heads : 2 * heads + filter_cols]
    grad_filters = grad_filters.T.reshape(tap_count, heads, 2 * piece_q + piece_v)
    return (
        result,
        grad_tokens,
        take(0, n_in),
        take(1, n_in),
        take(2, n_out),
        pieces[:, :q_end],
        pieces[:, q_end:k_end],
        pieces[:, k_end:v_end],
        pieces[:, v_end:g_end],
        tiny_piece[:, :heads],
        tiny_piece[:, heads : 2 * heads],
        grad_filters[..., :piece_q],
        grad_filters[..., piece_q : 2 * piece_q],
        grad_filters[..., 2 * piece_q :],
        sums[3, :n_heads],
        sums[3, n_heads : 2 * n_heads],
        out_piece.T,
        gate_piece.astype(f32),
        up_piece,
        down_piece.astype(f32).T,
    )


def solution(mesh):
    rows = P(("dp", "tensor"), None)
    spread = P(("dp", "tensor"))
    weight = P("dp", "tensor")
    filters = P(None, "tensor", "dp")
    turned = P("tensor", "dp")
    return jax.shard_map(
        local,
        mesh=mesh,
        in_specs=(rows, P("dp"), rows, spread, spread, spread)
        + (weight,) * 6
        + (filters,) * 3
        + (P(), P(), turned, weight, weight, turned),
        out_specs=(rows, rows, spread, spread, spread)
        + (weight,) * 6
        + (filters,) * 3
        + (P(), P(), turned, weight, weight, turned),
        check_vma=False,
    )
```
